128 devices in a mesh: shot: 8 (over z, core), rline: 16 (over y, x).
Axes of the slice: x: 4, y: 4, z: 4, core: 2. Of those that a mesh axis runs over, the one named last changes fastest.
Arguments:
- traces: bfloat16 [32, 1536, 1024], P('shot', 'rline'), may hold values from -6 to 6
- kernels_shot: bfloat16 [4, 15, 31], replicated, may hold values from -0.25 to 0.25
- kernels_rcv: bfloat16 [4, 15, 31], replicated, may hold values from -0.25 to 0.25
- dest: int32 [32, 1536], P('shot', 'rline'), may hold values from -1 to 127, as said below
- gather: int32 [32, 1536], P('shot', 'rline'), may hold values from -1 to 11, as said below
- fold: int32 [32, 1536], P('shot', 'rline'), may hold values from -1 to 31, as said below
- counts: int32 [1536], P(('shot', 'rline')), may hold values from 1 to 32, as said below
Outputs:
- filtered: float32 [32, 1536, 1024], P('shot', 'rline')
The draws below stay inside these ranges and needn't reach their ends.
Inputs may be any that keep to these rules, and one draw needn't show every extreme that they name: `dest`: A live trace names the index, on the shot and rline axes taken together (shot index times the rline size plus rline index), of the device that owns its receiver's gather. All live traces of one receiver name the same owner; every device owns exactly 12 receivers, at most 1 of them among the receivers of one rline index; every receiver has a live trace. `gather`: the 12 receivers of one owner carry distinct numbers; -1 exactly where dest is -1. `fold`: the number of live traces of the same receiver with a lower shot index; -1 exactly where dest is -1. Every owner has one receiver all of whose traces are live. `counts`: entry o * 12 + k is the number of live traces of the receiver with owner o and gather number k.
All inputs are finite; a program needn't handle non-finite values.
Results may differ from the reference program's by a relative error of at most 0.0032.
Values may be sent and summed in bfloat16 or wider, within the bound.
A program may use at most 64 MiB of HBM per device.

```python
import jax
import jax.numpy as jnp
from jax import lax

NT = 1024
FANS = 4
TRACE_TAPS = 15
SAMPLE_TAPS = 31
RCV_DEV = 96
SHOTS = 32
RCV = 1536
FOLD = 32
RG_DEV = 12
DEVICES = 128


def survey_geometry(key):
    keys = jax.random.split(jax.random.fold_in(key, 4099), 7)
    line_count = RCV // RCV_DEV
    owner_perm = jax.random.permutation(keys[0], DEVICES).astype(jnp.int32)
    scores = jax.random.randint(keys[1], (line_count, RCV_DEV), 0, 1 << 20) * RCV_DEV + jnp.arange(RCV_DEV, dtype=jnp.int32)[None, :]
    within = jnp.argsort(jnp.argsort(scores, axis=1), axis=1).astype(jnp.int32)
    cyclic = (jnp.arange(line_count, dtype=jnp.int32)[:, None] * RCV_DEV + within).reshape(-1)
    owner = owner_perm[cyclic % DEVICES]
    number_shift = jax.random.randint(keys[6], (DEVICES,), 0, RG_DEV)
    number = ((cyclic // DEVICES + number_shift[owner]) % RG_DEV).astype(jnp.int32)
    chance = jax.random.randint(keys[2], (RCV,), 35, 101)
    roll = jax.random.randint(keys[3], (SHOTS, RCV), 0, 100)
    alive = roll < chance[None, :]
    anchor = jax.random.randint(keys[4], (RCV,), 0, SHOTS)
    alive = alive | (jnp.arange(SHOTS, dtype=jnp.int32)[:, None] == anchor[None, :])
    full_pick = jax.random.randint(keys[5], (DEVICES,), 0, RG_DEV)
    alive = alive | (number == full_pick[owner])[None, :]
    position = jnp.cumsum(alive.astype(jnp.int32), axis=0) - 1
    return (alive, owner, number, position)


def draw_dest(key, part):
    alive, owner, number, position = survey_geometry(key)
    return jnp.where(alive, owner[None, :], -1).astype(jnp.int32)


def draw_gather(key, part):
    alive, owner, number, position = survey_geometry(key)
    return jnp.where(alive, number[None, :], -1).astype(jnp.int32)


def draw_fold(key, part):
    alive, owner, number, position = survey_geometry(key)
    return jnp.where(alive, position, -1).astype(jnp.int32)


def draw_counts(key, part):
    alive, owner, number, position = survey_geometry(key)
    totals = jnp.sum(alive.astype(jnp.int32), axis=0)
    return jnp.zeros((RG_DEV * DEVICES,), jnp.int32).at[owner * RG_DEV + number].set(totals)


def block_levels(stream_key, extent, cuts, least, high):
    gain = 1.0
    for dim, shards_of in cuts:
        heights = jax.random.uniform(jax.random.fold_in(jax.random.fold_in(stream_key, 6), dim), (shards_of,), jnp.float32, least / len(cuts), high / len(cuts))
        gain = gain * jnp.repeat(jnp.exp(heights), extent[dim] // shards_of).reshape((-1,) + (1,) * (len(extent) - 1 - dim))
    return gain


def bell_draw(own_key, dims, width, reach, cuts=(), held_as=jnp.bfloat16):
    loudness = block_levels(own_key, dims, cuts, -0.22, 0.18) if cuts else 1.0
    values = jax.random.normal(own_key, dims, jnp.float32) * width * loudness
    return jnp.minimum(jnp.maximum(values, -reach), reach).astype(held_as)


def setup_inputs(seed: int = 0) -> dict:
    key_list = jax.random.split(jax.random.key(seed), 8)
    return {
        "traces": bell_draw(key_list[0], (SHOTS, RCV, NT), 1.0, 6.0, ((0, 8), (1, 16))),
        "kernels_shot": bell_draw(key_list[1], (FANS, TRACE_TAPS, SAMPLE_TAPS), (TRACE_TAPS * SAMPLE_TAPS) ** -0.5, 0.25),
        "kernels_rcv": bell_draw(key_list[2], (FANS, TRACE_TAPS, SAMPLE_TAPS), (TRACE_TAPS * SAMPLE_TAPS) ** -0.5, 0.25),
        "dest": draw_dest(jax.random.fold_in(key_list[7], 71), 0),
        "gather": draw_gather(jax.random.fold_in(key_list[7], 71), 0),
        "fold": draw_fold(jax.random.fold_in(key_list[7], 71), 0),
        "counts": draw_counts(jax.random.fold_in(key_list[7], 71), 0),
    }


def dip_subtract(gathers, kernels):
    kernel_stack = kernels.astype(jnp.float32)[:, None]
    coherent = lax.conv_general_dilated(gathers[:, None], kernel_stack, (1, 1), ((7, 7), (15, 15)), dimension_numbers=('NCHW', 'OIHW', 'NCHW'), precision=lax.Precision.HIGHEST)
    energy = lax.optimization_barrier(jnp.sum(coherent * coherent, axis=1))
    return gathers - lax.optimization_barrier(jnp.sum(coherent * coherent * coherent, axis=1)) / (energy + 1.0)

def reference(traces, kernels_shot, kernels_rcv, dest, gather, fold, counts):
    alive_mask = dest >= 0
    first_input = jnp.where(alive_mask[..., None], traces, jnp.zeros_like(traces)).astype(jnp.float32)

    def shot_filter(one_shot):
        return dip_subtract(one_shot[None], kernels_shot)[0]
    first_pass = lax.map(shot_filter, first_input).astype(jnp.bfloat16)
    receiver_col = jnp.broadcast_to(jnp.arange(RCV, dtype=jnp.int32)[None, :], (SHOTS, RCV))
    position = jnp.where(alive_mask, fold, FOLD).astype(jnp.int32)
    stacks = jnp.zeros((RCV, FOLD, NT), jnp.bfloat16).at[receiver_col, position].set(first_pass, mode='drop')
    grouped = stacks.astype(jnp.float32).reshape(RCV // RCV_DEV, RCV_DEV, FOLD, NT)

    def receiver_filter(block_gathers):
        return dip_subtract(block_gathers, kernels_rcv)
    second_pass = lax.map(receiver_filter, grouped).reshape(RCV, FOLD, NT)
    owner = lax.optimization_barrier(jnp.max(dest, axis=0)).astype(jnp.int32)
    number = lax.optimization_barrier(jnp.max(gather, axis=0)).astype(jnp.int32)
    live_count = counts[owner * RG_DEV + number].astype(jnp.float32)
    second_pass = second_pass * jnp.sqrt(FOLD / live_count)[:, None, None]
    picked = second_pass[receiver_col, jnp.minimum(position, FOLD - 1)]
    return jnp.where(alive_mask[..., None], picked, jnp.zeros_like(picked))
```

```python
import functools

import jax
import jax.numpy as jnp
from jax import lax
from jax.experimental import pallas as pl
from jax.experimental.pallas import tpu as pltpu
from jax.sharding import PartitionSpec as P

LANES = 128
CHUNKS = 8
BF16 = jnp.bfloat16
F32 = jnp.float32


def lane_index(shape):
    return lax.broadcasted_iota(jnp.int32, shape, len(shape) - 1)


def build_table(kernel_ref, table_ref):
    taps = kernel_ref.shape[2]
    tap = lax.broadcasted_iota(jnp.int32, (taps, LANES), 0)
    lane = lax.broadcasted_iota(jnp.int32, (taps, LANES), 1)
    place_low = (lane == LANES - 1 - tap).astype(BF16)
    place_high = (lane == LANES // 2 - 1 - tap).astype(BF16)
    even = (lane_index((64, LANES)) // 32) % 2 == 0
    for half in range(2):
        base = jnp.dot(kernel_ref[2 * half], place_low, preferred_element_type=F32) + jnp.dot(
            kernel_ref[2 * half + 1], place_high, preferred_element_type=F32
        )
        before = jnp.zeros((64, LANES), F32)
        for step in range(16):
            if step < 15:
                row = jnp.broadcast_to(base[step : step + 1], (64, LANES))
                here = pltpu.roll(row, 0, 1, stride=1, stride_axis=0)
            else:
                here = jnp.zeros((64, LANES), F32)
            block = jnp.where(even, here, pltpu.roll(before, 32, 1))
            table_ref[step * 64 : (step + 1) * 64, half * LANES : (half + 1) * LANES] = block.astype(BF16)
            before = here


def windows(first, second):
    shape = first.shape
    lane = lane_index(shape)
    chunk = lax.broadcasted_iota(jnp.int32, shape, 1)
    low = lane < 64

    def both(x):
        left = jnp.where(chunk == 0, 0.0, pltpu.roll(x, 1, 1))
        right = jnp.where(chunk == CHUNKS - 1, 0.0, pltpu.roll(x, CHUNKS - 1, 1))
        early = pltpu.roll(jnp.where(lane < 112, x, left), 16, 2)
        late = pltpu.roll(jnp.where(lane >= 16, x, right), 112, 2)
        return early, late

    early_a, late_a = both(first)
    early_b, late_b = both(second)
    return (
        jnp.where(low, early_a, pltpu.roll(early_b, 64, 2)),
        jnp.where(low, late_a, pltpu.roll(late_b, 64, 2)),
        jnp.where(low, pltpu.roll(early_a, 64, 2), early_b),
        jnp.where(low, pltpu.roll(late_a, 64, 2), late_b),
    )


def fan_terms(window_ref, table_ref, start, pairs):
    rows = pairs * 16
    left = jnp.concatenate(
        [
            jnp.concatenate(
                [window_ref[quarter, pl.ds(start + step, pairs)].reshape(rows, LANES) for step in range(8)],
                axis=1,
            )
            for quarter in range(4)
        ],
        axis=0,
    )
    coherent = jnp.dot(left, table_ref[...], preferred_element_type=F32)
    squares, cubes = [], []
    for quarter in range(4):
        part = coherent[quarter * rows : (quarter + 1) * rows]
        one, two = part[:, :LANES], part[:, LANES:]
        one_sq, two_sq = one * one, two * two
        squares.append(one_sq + two_sq)
        cubes.append(one_sq * one + two_sq * two)
    lane = lane_index((rows, LANES))
    low = lane < 64
    even = (lane // 32) % 2 == 0

    def merged(s):
        s02, s20 = jnp.where(low, s[0], s[2]), jnp.where(low, s[2], s[0])
        s13, s31 = jnp.where(low, s[1], s[3]), jnp.where(low, s[3], s[1])
        a = jnp.where(even, s02, s13) + pltpu.roll(jnp.where(even, s20, s31), 64, 1)
        b = jnp.where(even, s13, s02) + pltpu.roll(jnp.where(even, s31, s20), 64, 1)
        return a, b

    square_a, square_b = merged(squares)
    cube_a, cube_b = merged(cubes)
    term_a = cube_a / (square_a + 1.0)
    term_b = cube_b / (square_b + 1.0)
    return (
        jnp.where(even, term_a, pltpu.roll(term_b, 32, 1)),
        jnp.where(even, pltpu.roll(term_b, 96, 1), term_a),
    )


def shot_kernel(x_ref, kernel_ref, out_ref, window_ref, table_ref):
    build_table(kernel_ref, table_ref)
    groups, padded = x_ref.shape[0], x_ref.shape[1]
    step_pairs = 5
    pairs = 8

    @pl.loop(0, groups)
    def _(g):
        @pl.loop(0, padded // (2 * step_pairs))
        def _(i):
            x = x_ref[g, pl.ds(i * 2 * step_pairs, 2 * step_pairs)].astype(F32)
            x = x.reshape(step_pairs, 2, 2, CHUNKS, LANES)
            first = x[:, 0].reshape(step_pairs * 2, CHUNKS, LANES)
            second = x[:, 1].reshape(step_pairs * 2, CHUNKS, LANES)
            for quarter, tile in enumerate(windows(first, second)):
                window_ref[quarter, pl.ds(i * step_pairs, step_pairs)] = tile.reshape(
                    step_pairs, 16, LANES
                ).astype(BF16)

        @pl.loop(0, out_ref.shape[1] // (2 * pairs))
        def _(i):
            start = i * pairs
            even, odd = fan_terms(window_ref, table_ref, start, pairs)
            terms = jnp.stack(
                [even.reshape(pairs, 16, LANES), odd.reshape(pairs, 16, LANES)], axis=1
            ).reshape(2 * pairs, 16, LANES)
            centre = x_ref[g, pl.ds(2 * start + 7, 2 * pairs)].astype(F32)
            out_ref[g, pl.ds(2 * start, 2 * pairs)] = (centre - terms).astype(BF16)


def receiver_kernel(x_ref, fold_ref, kernel_ref, out_ref, window_ref, table_ref, stack_ref, pick_ref):
    build_table(kernel_ref, table_ref)
    sources, groups, receivers = x_ref.shape[0], x_ref.shape[1], x_ref.shape[2]
    shots = sources * groups * 2
    rows = shots * CHUNKS
    pairs = shots // 2
    stack_ref[0:7] = jnp.zeros((7, 16, LANES), F32)
    stack_ref[7 + shots : 16 + shots] = jnp.zeros((9, 16, LANES), F32)
    place = lax.broadcasted_iota(jnp.int32, (rows, rows), 0)

    @pl.loop(0, receivers // 2)
    def _(g):
        gains = []
        for side in range(2):
            k = 2 * g + side
            labels = fold_ref[k]
            pick = (labels == place).astype(F32).astype(BF16)
            pick_ref[side] = pick
            live = jnp.sum((labels >= 0).astype(F32), axis=1, keepdims=True) / CHUNKS
            gains.append(jnp.sqrt(shots / live))
            x = x_ref[:, :, k].reshape(rows, LANES)
            stack = jnp.dot(pick, x, preferred_element_type=F32).reshape(shots, CHUNKS, LANES)
            stack_ref[7 : 7 + shots, side * CHUNKS : (side + 1) * CHUNKS] = stack
        step_pairs = 6

        @pl.loop(0, 4)
        def _(i):
            x = stack_ref[pl.ds(i * 2 * step_pairs, 2 * step_pairs)]
            x = x.reshape(step_pairs, 2, 2, CHUNKS, LANES)
            first = x[:, 0].reshape(step_pairs * 2, CHUNKS, LANES)
            second = x[:, 1].reshape(step_pairs * 2, CHUNKS, LANES)
            for quarter, tile in enumerate(windows(first, second)):
                window_ref[quarter, pl.ds(i * step_pairs, step_pairs)] = tile.reshape(
                    step_pairs, 16, LANES
                ).astype(BF16)

        value = []
        for half in range(2):
            count = pairs // 2
            start = half * count
            even, odd = fan_terms(window_ref, table_ref, start, count)
            terms = jnp.stack(
                [even.reshape(count, 16, LANES), odd.reshape(count, 16, LANES)], axis=1
            ).reshape(2 * count, 16, LANES)
            value.append(stack_ref[7 + 2 * start : 7 + 2 * start + 2 * count] - terms)
        value = jnp.concatenate(value, axis=0)
        for side in range(2):
            k = 2 * g + side
            own = value[:, side * CHUNKS : (side + 1) * CHUNKS].reshape(rows, LANES) * gains[side]
            back = lax.dot_general(
                pick_ref[side], own.astype(BF16), (((0,), (0,)), ((), ())), preferred_element_type=F32
            )
            out_ref[:, :, k] = back.astype(BF16).reshape(sources, groups, 16, LANES)


def vmem():
    return pl.BlockSpec(memory_space=pltpu.VMEM)


def shards(traces, kernels_shot, kernels_rcv, dest, gather, fold, counts):
    shot_dev, rcv_dev, samples = traces.shape
    shot_size = lax.axis_size("shot")
    rline_size = lax.axis_size("rline")
    shots = shot_dev * shot_size
    own = rcv_dev // shot_size
    rim = 7
    limit = 48 << 20

    fold_all = lax.all_gather(fold, "shot", axis=0, tiled=True)
    cleaned = jnp.where((dest >= 0)[..., None], traces, jnp.zeros_like(traces))
    head, tail = cleaned[:, :rim], cleaned[:, rcv_dev - rim :]
    ends = rline_size - 1
    padded = jnp.concatenate(
        [
            lax.ppermute(tail, "rline", [(i, i + 1) for i in range(ends)]),
            cleaned,
            lax.ppermute(head, "rline", [(i + 1, i) for i in range(ends)]),
        ],
        axis=1,
    )
    groups = shot_dev // 2
    x = padded.reshape(groups, 2, rcv_dev + 2 * rim, CHUNKS, LANES).transpose(0, 2, 1, 3, 4)
    x = x.reshape(groups, rcv_dev + 2 * rim, 16, LANES)
    pair_count = (rcv_dev + 2 * rim) // 2
    first_pass = pl.pallas_call(
        shot_kernel,
        out_shape=jax.ShapeDtypeStruct((groups, rcv_dev, 16, LANES), BF16),
        in_specs=[vmem(), vmem()],
        out_specs=vmem(),
        scratch_shapes=[
            pltpu.VMEM((4, pair_count, 16, LANES), BF16),
            pltpu.VMEM((1024, 256), BF16),
        ],
        compiler_params=pltpu.CompilerParams(vmem_limit_bytes=limit),
    )(x, kernels_shot)

    mine = lax.dynamic_slice_in_dim(fold_all, lax.axis_index("shot") * own, own, 1)
    spread = jnp.where(mine >= 0, mine * CHUNKS, -64).T[:, :, None] + jnp.arange(CHUNKS, dtype=jnp.int32)
    labels = spread.reshape(own, 1, shots * CHUNKS)

    sent = first_pass.reshape(groups, shot_size, own, 16, LANES)
    arrived = lax.all_to_all(sent, "shot", split_axis=1, concat_axis=0, tiled=False)
    back = pl.pallas_call(
        receiver_kernel,
        out_shape=jax.ShapeDtypeStruct((shot_size, groups, own, 16, LANES), BF16),
        in_specs=[vmem(), vmem(), vmem()],
        out_specs=vmem(),
        scratch_shapes=[
            pltpu.VMEM((4, shots // 2 + 8, 16, LANES), BF16),
            pltpu.VMEM((1024, 256), BF16),
            pltpu.VMEM((shots + 16, 16, LANES), F32),
            pltpu.VMEM((2, shots * CHUNKS, shots * CHUNKS), BF16),
        ],
        compiler_params=pltpu.CompilerParams(vmem_limit_bytes=limit),
    )(arrived, labels, kernels_rcv)
    returned = lax.all_to_all(back, "shot", split_axis=0, concat_axis=1, tiled=False)
    result = returned.reshape(groups, rcv_dev, 2, CHUNKS, LANES).transpose(0, 2, 1, 3, 4)
    return result.reshape(shot_dev, rcv_dev, samples).astype(F32)


def solution(mesh):
    in_specs = (
        P("shot", "rline", None),
        P(),
        P(),
        P("shot", "rline"),
        P("shot", "rline"),
        P("shot", "rline"),
        P(("shot", "rline")),
    )
    out_specs = P("shot", "rline", None)
    return jax.shard_map(shards, mesh=mesh, in_specs=in_specs, out_specs=out_specs, check_vma=False)
```

```python
import functools

import jax
import jax.numpy as jnp
from jax import lax
from jax.experimental import pallas as pl
from jax.experimental.pallas import tpu as pltpu
from jax.sharding import PartitionSpec as P

LANES = 128
CHUNKS = 8
BF16 = jnp.bfloat16
F32 = jnp.float32
RIM = 7
MESH = pl.DeviceIdType.MESH


def lane_index(shape):
    return lax.broadcasted_iota(jnp.int32, shape, len(shape) - 1)


def build_table(kernel_ref, table_ref):
    taps = kernel_ref.shape[2]
    tap = lax.broadcasted_iota(jnp.int32, (taps, LANES), 0)
    lane = lax.broadcasted_iota(jnp.int32, (taps, LANES), 1)
    place_low = (lane == LANES - 1 - tap).astype(BF16)
    place_high = (lane == LANES // 2 - 1 - tap).astype(BF16)
    even = (lane_index((64, LANES)) // 32) % 2 == 0
    for half in range(2):
        base = jnp.dot(kernel_ref[2 * half], place_low, preferred_element_type=F32) + jnp.dot(
            kernel_ref[2 * half + 1], place_high, preferred_element_type=F32
        )
        before = jnp.zeros((64, LANES), F32)
        for step in range(16):
            if step < 15:
                row = jnp.broadcast_to(base[step : step + 1], (64, LANES))
                here = pltpu.roll(row, 0, 1, stride=1, stride_axis=0)
            else:
                here = jnp.zeros((64, LANES), F32)
            block = jnp.where(even, here, pltpu.roll(before, 32, 1))
            table_ref[step * 64 : (step + 1) * 64, half * LANES : (half + 1) * LANES] = block.astype(BF16)
            before = here


def windows(first, second):
    shape = first.shape
    lane = lane_index(shape)
    chunk = lax.broadcasted_iota(jnp.int32, shape, 1)
    low = lane < 64

    def both(x):
        left = jnp.where(chunk == 0, 0.0, pltpu.roll(x, 1, 1))
        right = jnp.where(chunk == CHUNKS - 1, 0.0, pltpu.roll(x, CHUNKS - 1, 1))
        early = pltpu.roll(jnp.where(lane < 112, x, left), 16, 2)
        late = pltpu.roll(jnp.where(lane >= 16, x, right), 112, 2)
        return early, late

    early_a, late_a = both(first)
    early_b, late_b = both(second)
    return (
        jnp.where(low, early_a, pltpu.roll(early_b, 64, 2)),
        jnp.where(low, late_a, pltpu.roll(late_b, 64, 2)),
        jnp.where(low, pltpu.roll(early_a, 64, 2), early_b),
        jnp.where(low, pltpu.roll(late_a, 64, 2), late_b),
    )


def fan_terms(window_ref, table_ref, start, pairs):
    rows = pairs * 16
    left = jnp.concatenate(
        [
            jnp.concatenate(
                [window_ref[quarter, pl.ds(start + step, pairs)].reshape(rows, LANES) for step in range(8)],
                axis=1,
            )
            for quarter in range(4)
        ],
        axis=0,
    )
    coherent = jnp.dot(left, table_ref[...], preferred_element_type=F32)
    squares, cubes = [], []
    for quarter in range(4):
        part = coherent[quarter * rows : (quarter + 1) * rows]
        one, two = part[:, :LANES], part[:, LANES:]
        one_sq, two_sq = one * one, two * two
        squares.append(one_sq + two_sq)
        cubes.append(one_sq * one + two_sq * two)
    lane = lane_index((rows, LANES))
    low = lane < 64
    even = (lane // 32) % 2 == 0

    def merged(s):
        s02, s20 = jnp.where(low, s[0], s[2]), jnp.where(low, s[2], s[0])
        s13, s31 = jnp.where(low, s[1], s[3]), jnp.where(low, s[3], s[1])
        a = jnp.where(even, s02, s13) + pltpu.roll(jnp.where(even, s20, s31), 64, 1)
        b = jnp.where(even, s13, s02) + pltpu.roll(jnp.where(even, s31, s20), 64, 1)
        return a, b

    square_a, square_b = merged(squares)
    cube_a, cube_b = merged(cubes)
    term_a = cube_a / (square_a + 1.0)
    term_b = cube_b / (square_b + 1.0)
    return (
        jnp.where(even, term_a, pltpu.roll(term_b, 32, 1)),
        jnp.where(even, pltpu.roll(term_b, 96, 1), term_a),
    )


def fill_windows(source, window_ref, first, pairs):
    x = source.reshape(pairs, 2, 2, CHUNKS, LANES)
    one = x[:, 0].reshape(pairs * 2, CHUNKS, LANES)
    two = x[:, 1].reshape(pairs * 2, CHUNKS, LANES)
    for quarter, tile in enumerate(windows(one, two)):
        window_ref[quarter, pl.ds(first, pairs)] = tile.reshape(pairs, 16, LANES).astype(BF16)


def interleaved(even, odd, pairs):
    return jnp.stack(
        [even.reshape(pairs, 16, LANES), odd.reshape(pairs, 16, LANES)], axis=1
    ).reshape(2 * pairs, 16, LANES)


def survey_kernel(
    shot_size,
    rline_size,
    x_ref,
    fold_ref,
    shot_taps_ref,
    rcv_taps_ref,
    out_ref,
    padded_ref,
    window_ref,
    shot_table_ref,
    rcv_table_ref,
    fold_own_ref,
    fold_ref_all,
    label_ref,
    pick_ref,
    sent_ref,
    held_ref,
    stack_ref,
    rcv_window_ref,
    back_ref,
    halo_send,
    halo_recv,
    fold_send,
    fold_recv,
    out_send,
    out_recv,
    own_sem,
    back_send,
    back_recv,
    back_own,
):
    groups, receivers = x_ref.shape[0], x_ref.shape[1]
    share = receivers // shot_size
    peers = shot_size - 1
    shots = shot_size * groups * 2
    rows = shots * CHUNKS
    me = lax.axis_index("shot")
    line = lax.axis_index("rline")
    right, left = lax.rem(line + 1, rline_size), lax.rem(line + rline_size - 1, rline_size)

    def peer(step):
        return lax.rem(me + 1 + step, shot_size)

    def source(step):
        return lax.rem(me + shot_size - 1 - step, shot_size)

    barrier = pltpu.get_barrier_semaphore()
    for step in range(peers):
        pl.semaphore_signal(barrier, inc=1, device_id={"shot": peer(step)}, device_id_type=MESH)
    for side in (left, right):
        pl.semaphore_signal(barrier, inc=1, device_id={"rline": side}, device_id_type=MESH)
    pl.semaphore_wait(barrier, peers + 2)

    def halo(side):
        begin = receivers - RIM if side == 0 else 0
        land = 0 if side == 0 else RIM + receivers
        return pltpu.make_async_remote_copy(
            src_ref=x_ref.at[:, pl.ds(begin, RIM)],
            dst_ref=padded_ref.at[:, pl.ds(land, RIM)],
            send_sem=halo_send.at[side],
            recv_sem=halo_recv.at[side],
            device_id={"rline": right if side == 0 else left},
            device_id_type=MESH,
        )

    def fold_copy(step, slot):
        return pltpu.make_async_remote_copy(
            src_ref=fold_own_ref,
            dst_ref=fold_ref_all.at[slot],
            send_sem=fold_send.at[step],
            recv_sem=fold_recv.at[step],
            device_id={"shot": peer(step)},
            device_id_type=MESH,
        )

    for side in range(2):
        halo(side).start()
    fold_own_ref[...] = jnp.full(fold_own_ref.shape, -1, jnp.int32)
    fold_own_ref[0 : fold_ref.shape[0], 0:receivers] = fold_ref[...]
    for step in range(peers):
        fold_copy(step, me).start()
    fold_ref_all[me] = fold_own_ref[...]

    for g in range(groups):
        padded_ref[g, RIM : RIM + receivers] = x_ref[g]
    build_table(shot_taps_ref, shot_table_ref)
    build_table(rcv_taps_ref, rcv_table_ref)

    for side in range(2):
        halo(side).wait_recv()
    keep_left = (line > 0).astype(F32)
    keep_right = (line < rline_size - 1).astype(F32)
    for g in range(groups):
        padded_ref[g, 0:RIM] = (padded_ref[g, 0:RIM].astype(F32) * keep_left).astype(BF16)
        tail = pl.ds(RIM + receivers, RIM)
        padded_ref[g, tail] = (padded_ref[g, tail].astype(F32) * keep_right).astype(BF16)

    step_pairs = 5
    for g in range(groups):

        @pl.loop(0, (receivers + 2 * RIM) // (2 * step_pairs))
        def _(i):
            x = padded_ref[g, pl.ds(i * 2 * step_pairs, 2 * step_pairs)].astype(F32)
            fill_windows(x, window_ref.at[g], i * step_pairs, step_pairs)

    def out_copy(step, target, slot):
        return pltpu.make_async_remote_copy(
            src_ref=sent_ref.at[target],
            dst_ref=held_ref.at[slot],
            send_sem=out_send.at[step],
            recv_sem=out_recv.at[step],
            device_id={"shot": peer(step)},
            device_id_type=MESH,
        )

    pairs = share // 2

    @pl.loop(0, shot_size)
    def _(step):
        target = peer(step)
        for g in range(groups):
            even, odd = fan_terms(window_ref.at[g], shot_table_ref, target * pairs, pairs)
            centre = padded_ref[g, pl.ds(target * share + RIM, share)].astype(F32)
            sent_ref[target, g] = (centre - interleaved(even, odd, pairs)).astype(BF16)

        @pl.when(step < peers)
        def _():
            out_copy(step, target, me).start()

        @pl.when(step == peers)
        def _():
            pltpu.make_async_copy(sent_ref.at[me], held_ref.at[me], own_sem).start()

    for step in range(peers):
        fold_copy(step, source(step)).wait_recv()
    folds = fold_ref_all[...].reshape(shot_size * 8, LANES).astype(F32)
    take = lax.broadcasted_iota(jnp.int32, (16, LANES), 1) == (
        me * share + lax.broadcasted_iota(jnp.int32, (16, LANES), 0)
    )
    mine = lax.dot_general(
        take.astype(F32), folds, (((1,), (1,)), ((), ())), preferred_element_type=F32
    )
    entry = lax.broadcasted_iota(jnp.int32, (shot_size * 8, rows), 0)
    shot = lax.broadcasted_iota(jnp.int32, (shot_size * 8, rows), 1) // CHUNKS
    per = groups * 2
    spread = ((entry // 8) * per + entry % 8 == shot) & (entry % 8 < per)
    lane = lax.broadcasted_iota(jnp.int32, (16, rows), 1)
    labels = jnp.dot(mine, spread.astype(F32), preferred_element_type=F32)
    labels = jnp.where(labels >= 0.0, labels * CHUNKS + (lane % CHUNKS).astype(F32), -1.0)
    place = lax.broadcasted_iota(jnp.int32, (rows, rows), 0).astype(F32)
    for k in range(share):
        label_ref[k] = labels[k : k + 1]

    @pl.loop(0, share)
    def _(k):
        pick_ref[k] = jnp.where(label_ref[k] == place, 1.0, 0.0).astype(BF16)

    stack_ref[0:RIM] = jnp.zeros((RIM, 16, LANES), F32)
    stack_ref[RIM + shots : 16 + shots] = jnp.zeros((16 - RIM, 16, LANES), F32)
    pltpu.make_async_copy(sent_ref.at[me], held_ref.at[me], own_sem).wait()
    for step in range(peers):
        out_copy(step, peer(step), source(step)).wait_recv()

    def back_copy(g, step, owner):
        return pltpu.make_async_remote_copy(
            src_ref=back_ref.at[g, peer(step)],
            dst_ref=out_ref.at[:, pl.ds(owner * share + 2 * g, 2)],
            send_sem=back_send.at[g, step],
            recv_sem=back_recv.at[g, step],
            device_id={"shot": peer(step)},
            device_id_type=MESH,
        )

    def back_local(g):
        return pltpu.make_async_copy(
            back_ref.at[g, me], out_ref.at[:, pl.ds(me * share + 2 * g, 2)], back_own.at[g]
        )

    @pl.loop(0, pairs)
    def _(g):
        gains = []
        for side in range(2):
            k = 2 * g + side
            live = jnp.sum((label_ref[k] >= 0.0).astype(F32), axis=1, keepdims=True) / CHUNKS
            gains.append(jnp.sqrt(shots / live))
            x = held_ref[:, :, k].reshape(rows, LANES)
            stack = jnp.dot(pick_ref[k], x, preferred_element_type=F32).reshape(shots, CHUNKS, LANES)
            stack_ref[RIM : RIM + shots, side * CHUNKS : (side + 1) * CHUNKS] = stack

        @pl.loop(0, 4)
        def _(i):
            fill_windows(stack_ref[pl.ds(i * 12, 12)], rcv_window_ref, i * 6, 6)

        value = []
        count = shots // 4
        for half in range(2):
            even, odd = fan_terms(rcv_window_ref, rcv_table_ref, half * count, count)
            begin = RIM + 2 * half * count
            value.append(stack_ref[begin : begin + 2 * count] - interleaved(even, odd, count))
        value = jnp.concatenate(value, axis=0)
        for side in range(2):
            own = value[:, side * CHUNKS : (side + 1) * CHUNKS].reshape(rows, LANES) * gains[side]
            back = lax.dot_general(
                pick_ref[2 * g + side], own.astype(BF16), (((0,), (0,)), ((), ())), preferred_element_type=F32
            )
            back_ref[g, :, :, side] = back.astype(BF16).reshape(shot_size, groups, 16, LANES)
        for step in range(peers):
            back_copy(g, step, me).start()
        back_local(g).start()

    for side in range(2):
        halo(side).wait_send()
    for step in range(peers):
        fold_copy(step, me).wait_send()
        out_copy(step, peer(step), me).wait_send()

    @pl.loop(0, pairs)
    def _(g):
        back_local(g).wait()
        for step in range(peers):
            back_copy(g, step, me).wait_send()
            back_copy(g, step, source(step)).wait_recv()


def vmem():
    return pl.BlockSpec(memory_space=pltpu.VMEM)


def shards(traces, kernels_shot, kernels_rcv, dest, gather, fold, counts):
    shot_dev, rcv_dev, samples = traces.shape
    shot_size = lax.axis_size("shot")
    rline_size = lax.axis_size("rline")
    shots = shot_dev * shot_size
    share = rcv_dev // shot_size
    rows = shots * CHUNKS
    groups = shot_dev // 2
    peers = shot_size - 1
    pairs = share // 2
    span = rcv_dev + 2 * RIM

    cleaned = jnp.where((dest >= 0)[..., None], traces, jnp.zeros_like(traces))
    x = cleaned.reshape(groups, 2, rcv_dev, CHUNKS, LANES).transpose(0, 2, 1, 3, 4)
    x = x.reshape(groups, rcv_dev, 16, LANES)
    dma = pltpu.SemaphoreType.DMA
    returned = pl.pallas_call(
        functools.partial(survey_kernel, shot_size, rline_size),
        out_shape=jax.ShapeDtypeStruct((groups, rcv_dev, 16, LANES), BF16),
        in_specs=[vmem()] * 4,
        out_specs=vmem(),
        scratch_shapes=[
            pltpu.VMEM((groups, span, 16, LANES), BF16),
            pltpu.VMEM((groups, 4, span // 2, 16, LANES), BF16),
            pltpu.VMEM((1024, 256), BF16),
            pltpu.VMEM((1024, 256), BF16),
            pltpu.VMEM((8, LANES), jnp.int32),
            pltpu.VMEM((shot_size, 8, LANES), jnp.int32),
            pltpu.VMEM((share, 1, rows), F32),
            pltpu.VMEM((share, rows, rows), BF16),
            pltpu.VMEM((shot_size, groups, share, 16, LANES), BF16),
            pltpu.VMEM((shot_size, groups, share, 16, LANES), BF16),
            pltpu.VMEM((shots + 16, 16, LANES), F32),
            pltpu.VMEM((4, shots // 2 + 8, 16, LANES), BF16),
            pltpu.VMEM((pairs, shot_size, groups, 2, 16, LANES), BF16),
            dma((2,)),
            dma((2,)),
            dma((peers,)),
            dma((peers,)),
            dma((peers,)),
            dma((peers,)),
            dma,
            dma((pairs, peers)),
            dma((pairs, peers)),
            dma((pairs,)),
        ],
        compiler_params=pltpu.CompilerParams(
            vmem_limit_bytes=48 << 20, collective_id=0, has_side_effects=True
        ),
        cost_estimate=pl.CostEstimate(flops=7 * 10**9, bytes_accessed=4 * 10**6, transcendentals=0),
    )(x, fold, kernels_shot, kernels_rcv)
    result = returned.reshape(groups, rcv_dev, 2, CHUNKS, LANES).transpose(0, 2, 1, 3, 4)
    return result.reshape(shot_dev, rcv_dev, samples).astype(F32)


def solution(mesh):
    in_specs = (
        P("shot", "rline", None),
        P(),
        P(),
        P("shot", "rline"),
        P("shot", "rline"),
        P("shot", "rline"),
        P(("shot", "rline")),
    )
    out_specs = P("shot", "rline", None)
    return jax.shard_map(shards, mesh=mesh, in_specs=in_specs, out_specs=out_specs, check_vma=False)
```

```python
import functools

import jax
import jax.numpy as jnp
from jax import lax
from jax.experimental import pallas as pl
from jax.experimental.pallas import tpu as pltpu
from jax.sharding import PartitionSpec as P

LANES = 128
CHUNKS = 8
BF16 = jnp.bfloat16
F32 = jnp.float32
RIM = 7
PIECES = 3
MESH = pl.DeviceIdType.MESH


def lane_index(shape):
    return lax.broadcasted_iota(jnp.int32, shape, len(shape) - 1)


def build_table(kernel_ref, table_ref):
    taps = kernel_ref.shape[2]
    tap = lax.broadcasted_iota(jnp.int32, (taps, LANES), 0)
    lane = lax.broadcasted_iota(jnp.int32, (taps, LANES), 1)
    place_low = (lane == LANES - 1 - tap).astype(BF16)
    place_high = (lane == LANES // 2 - 1 - tap).astype(BF16)
    even = (lane_index((64, LANES)) // 32) % 2 == 0
    for half in range(2):
        base = jnp.dot(kernel_ref[2 * half], place_low, preferred_element_type=F32) + jnp.dot(
            kernel_ref[2 * half + 1], place_high, preferred_element_type=F32
        )
        before = jnp.zeros((64, LANES), F32)
        columns = slice(half * LANES, (half + 1) * LANES)
        for step in range(16):
            if step < 15:
                row = jnp.broadcast_to(base[step : step + 1], (64, LANES))
                here = pltpu.roll(row, 0, 1, stride=1, stride_axis=0)
            else:
                here = jnp.zeros((64, LANES), F32)
            block = jnp.where(even, here, pltpu.roll(before, 32, 1)).astype(BF16)
            table_ref[0, step * 64 : (step + 1) * 64, columns] = block
            other = step + 1 if step % 2 == 0 else step - 1
            table_ref[1, other * 64 : (other + 1) * 64, columns] = block
            before = here


def fill_windows(source_ref, window_ref, first, pairs):
    rows = pairs * 32
    begin = first * 32 + 8
    shape = (pairs, 2, 16, LANES)
    lane = lane_index(shape)
    chunk = lax.broadcasted_iota(jnp.int32, shape, 2) % CHUNKS
    own = source_ref[pl.ds(begin, rows)].reshape(shape)
    left = source_ref[pl.ds(begin - 1, rows)].reshape(shape)
    right = source_ref[pl.ds(begin + 1, rows)].reshape(shape)
    early = jnp.where(lane < 112, own, jnp.where(chunk == 0, 0.0, left))
    late = jnp.where(lane >= 16, own, jnp.where(chunk == CHUNKS - 1, 0.0, right))
    low = lane_index((pairs * 16, LANES)) < 64

    def turned(x, shift):
        return pltpu.roll(x.reshape(pairs * 16, LANES), shift, 1)

    early_a, early_b = turned(early[:, 0], 16), turned(early[:, 1], 80)
    late_a, late_b = turned(late[:, 0], 112), turned(late[:, 1], 48)
    tiles = (
        jnp.where(low, early_a, early_b),
        jnp.where(low, late_a, late_b),
        jnp.where(low, early_b, early_a),
        jnp.where(low, late_b, late_a),
    )
    for quarter, tile in enumerate(tiles):
        window_ref[quarter, pl.ds(first, pairs)] = tile.reshape(pairs, 16, LANES).astype(BF16)


def fan_terms(blocks, table_ref, pairs):
    rows = pairs * 16
    total = len(blocks) * rows
    parts = []
    for half in range(2):
        left = jnp.concatenate(
            [
                jnp.concatenate(
                    [ref[quarter, pl.ds(first + step, pairs)].reshape(rows, LANES) for step in range(8)],
                    axis=1,
                )
                for quarter in (2 * half, 2 * half + 1)
                for ref, first in blocks
            ],
            axis=0,
        )
        coherent = jnp.dot(left, table_ref[half], preferred_element_type=F32)
        parts += [coherent[:total], coherent[total:]]
    squares, cubes = [], []
    for part in parts:
        one, two = part[:, :LANES], part[:, LANES:]
        one_sq, two_sq = one * one, two * two
        squares.append(one_sq + two_sq)
        cubes.append(one_sq * one + two_sq * two)
    lane = lane_index((total, LANES))
    low = lane < 64
    even = (lane // 32) % 2 == 0

    def merged(s):
        s02, s20 = jnp.where(low, s[0], s[2]), jnp.where(low, s[2], s[0])
        s13, s31 = jnp.where(low, s[1], s[3]), jnp.where(low, s[3], s[1])
        a = jnp.where(even, s02, s13) + pltpu.roll(jnp.where(even, s20, s31), 64, 1)
        b = jnp.where(even, s13, s02) + pltpu.roll(jnp.where(even, s31, s20), 64, 1)
        return a, b

    square_a, square_b = merged(squares)
    cube_a, cube_b = merged(cubes)
    term_a = cube_a / (square_a + 1.0)
    term_b = cube_b / (square_b + 1.0)
    first_trace = jnp.where(even, term_a, pltpu.roll(term_b, 32, 1))
    second_trace = jnp.where(even, pltpu.roll(term_b, 96, 1), term_a)
    shape = (len(blocks) * pairs, 16, LANES)
    both = jnp.stack([first_trace.reshape(shape), second_trace.reshape(shape)], axis=1)
    both = both.reshape(len(blocks), 2 * pairs, 16, LANES)
    return [both[i] for i in range(len(blocks))]


def survey_kernel(
    shot_size,
    rline_size,
    traces_hbm,
    dest_hbm,
    fold_hbm,
    shot_taps_hbm,
    rcv_taps_hbm,
    out_ref,
    traces_ref,
    dest_ref,
    fold_ref,
    shot_taps_ref,
    rcv_taps_ref,
    alive_ref,
    mask_ref,
    plain_ref,
    window_ref,
    shot_table_ref,
    rcv_table_ref,
    halo_out_ref,
    halo_in_ref,
    fold_own_ref,
    fold_all_ref,
    gain_ref,
    pick_ref,
    unpick_ref,
    sent_ref,
    held_ref,
    stack_ref,
    rcv_window_ref,
    back_ref,
    load_sem,
    halo_send,
    halo_recv,
    fold_send,
    fold_recv,
    out_send,
    out_recv,
    back_send,
    back_recv,
):
    shot_dev, receivers = traces_ref.shape[0], traces_ref.shape[1]
    groups = shot_dev // 2
    share = receivers // shot_size
    peers = shot_size - 1
    shots = shot_size * shot_dev
    rows = shots * CHUNKS
    me = lax.axis_index("shot")
    line = lax.axis_index("rline")
    right, left = lax.rem(line + 1, rline_size), lax.rem(line + rline_size - 1, rline_size)

    def peer(step):
        return lax.rem(me + 1 + step, shot_size)

    def source(step):
        return lax.rem(me + shot_size - 1 - step, shot_size)

    loads = [
        pltpu.make_async_copy(a, b, load_sem.at[i])
        for i, (a, b) in enumerate(
            [
                (shot_taps_hbm, shot_taps_ref),
                (rcv_taps_hbm, rcv_taps_ref),
                (dest_hbm, dest_ref),
                (fold_hbm, fold_ref),
                (traces_hbm, traces_ref),
            ]
        )
    ]
    for load in loads:
        load.start()
    barrier = pltpu.get_barrier_semaphore()
    for step in range(peers):
        pl.semaphore_signal(barrier, inc=1, device_id={"shot": peer(step)}, device_id_type=MESH)
    for side in (left, right):
        pl.semaphore_signal(barrier, inc=1, device_id={"rline": side}, device_id_type=MESH)

    alive_ref[...] = jnp.zeros(alive_ref.shape, F32)
    fold_own_ref[...] = jnp.full(fold_own_ref.shape, -1, jnp.int32)
    loads[0].wait()
    build_table(shot_taps_ref, shot_table_ref)
    loads[2].wait()
    alive_ref[0:shot_dev, 0:receivers] = (dest_ref[...] >= 0).astype(F32)
    pick_shot = lax.broadcasted_iota(jnp.int32, (8, shot_dev * LANES), 0) == (
        lax.broadcasted_iota(jnp.int32, (8, shot_dev * LANES), 1) // LANES
    )
    mask_ref[...] = lax.dot_general(
        alive_ref[...], pick_shot.astype(F32), (((0,), (0,)), ((), ())), preferred_element_type=F32
    )
    loads[4].wait()
    for s in range(shot_dev):

        @pl.loop(0, receivers // 16)
        def _(i):
            x = traces_ref[s, pl.ds(i * 16, 16)].astype(F32)
            for half in range(2):
                mask = mask_ref[pl.ds(i * 16 + half * 8, 8), s * LANES : (s + 1) * LANES]
                begin = (i * 16 + half * 8 + RIM) * 16 + 8 + (s % 2) * CHUNKS
                for c in range(CHUNKS):
                    piece = x[half * 8 : half * 8 + 8, c * LANES : (c + 1) * LANES]
                    plain_ref[s // 2, pl.ds(begin + c, 8, stride=16)] = piece * mask

    for g in range(groups):
        for side, begin in enumerate((receivers - RIM, 0)):
            edge = plain_ref[g, (RIM + begin) * 16 + 8 : (2 * RIM + begin) * 16 + 8]
            halo_out_ref[side, g] = edge.astype(BF16).reshape(RIM, 16, LANES)
    loads[3].wait()
    fold_own_ref[0:shot_dev, 0:receivers] = fold_ref[...]

    step_pairs = 5
    span_pairs = (receivers + 2 * RIM) // 2
    for g in range(groups):

        @pl.loop(1, span_pairs // step_pairs - 1)
        def _(i):
            fill_windows(plain_ref.at[g], window_ref.at[g], i * step_pairs, step_pairs)

    def halo(side):
        return pltpu.make_async_remote_copy(
            src_ref=halo_out_ref.at[side],
            dst_ref=halo_in_ref.at[side],
            send_sem=halo_send.at[side],
            recv_sem=halo_recv.at[side],
            device_id={"rline": right if side == 0 else left},
            device_id_type=MESH,
        )

    def fold_copy(step, slot):
        return pltpu.make_async_remote_copy(
            src_ref=fold_own_ref,
            dst_ref=fold_all_ref.at[slot],
            send_sem=fold_send.at[step],
            recv_sem=fold_recv.at[step],
            device_id={"shot": peer(step)},
            device_id_type=MESH,
        )

    piece = share // PIECES

    def out_copy(target, p, slot):
        return pltpu.make_async_remote_copy(
            src_ref=sent_ref.at[target, p],
            dst_ref=held_ref.at[slot, p],
            send_sem=out_send.at[target, p],
            recv_sem=out_recv.at[slot, p],
            device_id={"shot": target},
            device_id_type=MESH,
        )

    pl.semaphore_wait(barrier, peers + 2)
    for side in range(2):
        halo(side).start()
    for step in range(peers):
        fold_copy(step, me).start()
    fold_all_ref[me] = fold_own_ref[...]

    def shot_blocks(items):
        blocks = [
            (window_ref.at[g], (target * share + p * piece) // 2) for target, p in items for g in range(groups)
        ]
        terms = fan_terms(blocks, shot_table_ref, piece // 2)
        for n, (target, p) in enumerate(items):
            for g in range(groups):
                begin = (target * share + p * piece + RIM) * 16 + 8
                centre = plain_ref[g, begin : begin + piece * 16].reshape(piece, 16, LANES)
                sent_ref[target, p, g] = (centre - terms[n * groups + g]).astype(BF16)
        for target, p in items:

            @pl.when(me != target)
            def _(target=target, p=p):
                out_copy(target, p, me).start()

    inner = range(1, shot_size - 1)
    for p in range(PIECES - 1):
        shot_blocks([(target, p) for target in inner])

    keeps = ((line > 0).astype(F32), (line < rline_size - 1).astype(F32))
    for side in range(2):
        halo(side).wait_recv()
        land = (RIM + receivers) * 16 + 8 if side else 8
        for g in range(groups):
            edge = halo_in_ref[side, g].astype(F32).reshape(RIM * 16, LANES)
            plain_ref[g, land : land + RIM * 16] = edge * keeps[side]
    for g in range(groups):
        for first in (0, span_pairs - step_pairs):
            fill_windows(plain_ref.at[g], window_ref.at[g], first, step_pairs)
    shot_blocks([(target, p) for p in range(PIECES) for target in (0, shot_size - 1)])
    shot_blocks([(target, PIECES - 1) for target in inner])
    held_ref[me] = sent_ref[me]

    loads[1].wait()
    build_table(rcv_taps_ref, rcv_table_ref)
    for step in range(peers):
        fold_copy(step, source(step)).wait_recv()
    folds = fold_all_ref[...].reshape(shot_size * 8, LANES).astype(F32)
    take = lax.broadcasted_iota(jnp.int32, (16, LANES), 1) == (
        me * share + lax.broadcasted_iota(jnp.int32, (16, LANES), 0)
    )
    mine = lax.dot_general(
        take.astype(F32), folds, (((1,), (1,)), ((), ())), preferred_element_type=F32
    )
    entry = lax.broadcasted_iota(jnp.int32, (shot_size * 8, rows), 0)
    shot = lax.broadcasted_iota(jnp.int32, (shot_size * 8, rows), 1) // CHUNKS
    spread = ((entry // 8) * shot_dev + entry % 8 == shot) & (entry % 8 < shot_dev)
    spread = spread.astype(F32)
    labels = jnp.dot(mine, spread, preferred_element_type=F32)
    live = jnp.sum((labels >= 0.0).astype(F32), axis=1, keepdims=True) / CHUNKS
    gains = jnp.broadcast_to(jnp.sqrt(shots / live), (16, LANES))
    chunk = (lax.broadcasted_iota(jnp.int32, (16, rows), 1) % CHUNKS).astype(F32)
    labels = jnp.where(labels >= 0.0, labels * CHUNKS + chunk, -1.0)
    columns = lax.dot_general(spread, mine, (((0,), (1,)), ((), ())), preferred_element_type=F32)
    chunk = (lax.broadcasted_iota(jnp.int32, (rows, 16), 0) % CHUNKS).astype(F32)
    columns = jnp.where(columns >= 0.0, columns * CHUNKS + chunk, -1.0)
    down = lax.broadcasted_iota(jnp.int32, (rows, rows), 0).astype(F32)
    across = lax.broadcasted_iota(jnp.int32, (rows, rows), 1).astype(F32)
    for k in range(share):
        gain_ref[k] = jnp.broadcast_to(gains[k : k + 1], (CHUNKS, LANES))
        pick_ref[k] = jnp.where(labels[k : k + 1] == down, 1.0, 0.0).astype(BF16)
        unpick_ref[k] = jnp.where(columns[:, k : k + 1] == across, 1.0, 0.0).astype(BF16)

    for slot in range(2):
        stack_ref[slot, 0 : RIM * 16 + 8] = jnp.zeros((RIM * 16 + 8, LANES), F32)
        end = (RIM + shots) * 16 + 8
        stack_ref[slot, end:] = jnp.zeros((stack_ref.shape[1] - end, LANES), F32)

    def back_copy(pair, step, owner):
        return pltpu.make_async_remote_copy(
            src_ref=back_ref.at[pair, peer(step)],
            dst_ref=out_ref.at[:, pl.ds(owner * share + 2 * pair, 2)],
            send_sem=back_send.at[pair, step],
            recv_sem=back_recv.at[pair, step],
            device_id={"shot": peer(step)},
            device_id_type=MESH,
        )

    def prepare(pair):
        slot = pair % 2
        for side in range(2):
            k = 2 * pair + side
            x = held_ref[:, k // piece, :, k % piece].reshape(rows, LANES)
            stack = jnp.dot(pick_ref[k], x, preferred_element_type=F32)
            for p in range(shots):
                begin = (RIM + p) * 16 + 8 + side * CHUNKS
                stack_ref[slot, begin : begin + CHUNKS] = stack[p * CHUNKS : (p + 1) * CHUNKS]
        for i in range(4):
            fill_windows(stack_ref.at[slot], rcv_window_ref.at[slot], i * 6, 6)

    def finish(pair):
        slot = pair % 2
        (terms,) = fan_terms([(rcv_window_ref.at[slot], 0)], rcv_table_ref, shots // 2)
        begin = RIM * 16 + 8
        value = stack_ref[slot, begin : begin + shots * 16].reshape(shots, 16, LANES) - terms
        for side in range(2):
            k = 2 * pair + side
            own = value[:, side * CHUNKS : (side + 1) * CHUNKS] * gain_ref[k][None]
            back = jnp.dot(
                unpick_ref[k], own.reshape(rows, LANES).astype(BF16), preferred_element_type=F32
            )
            back_ref[pair, :, :, side] = back.astype(BF16).reshape(shot_size, groups, 16, LANES)
        for step in range(peers):
            back_copy(pair, step, me).start()
        out_ref[:, pl.ds(me * share + 2 * pair, 2)] = back_ref[pair, me]

    def arrive(p):
        for step in range(peers):
            out_copy(peer(step), p, source(step)).wait_recv()

    pairs = share // 2
    arrive(0)
    prepare(0)
    for pair in range(pairs):
        if pair + 1 < pairs:
            if (2 * (pair + 1)) % piece == 0:
                arrive((2 * (pair + 1)) // piece)
            prepare(pair + 1)
        finish(pair)

    for side in range(2):
        halo(side).wait_send()
    for step in range(peers):
        fold_copy(step, me).wait_send()
        for p in range(PIECES):
            out_copy(peer(step), p, me).wait_send()
    for pair in range(pairs):
        for step in range(peers):
            back_copy(pair, step, me).wait_send()
            back_copy(pair, step, source(step)).wait_recv()


def shards(traces, kernels_shot, kernels_rcv, dest, gather, fold, counts):
    shot_dev, rcv_dev, samples = traces.shape
    shot_size = lax.axis_size("shot")
    rline_size = lax.axis_size("rline")
    shots = shot_dev * shot_size
    share = rcv_dev // shot_size
    rows = shots * CHUNKS
    groups = shot_dev // 2
    peers = shot_size - 1
    pairs = share // 2
    span = rcv_dev + 2 * RIM
    dma = pltpu.SemaphoreType.DMA
    vmem = pltpu.VMEM
    returned = pl.pallas_call(
        functools.partial(survey_kernel, shot_size, rline_size),
        out_shape=jax.ShapeDtypeStruct((groups, rcv_dev, 16, LANES), BF16),
        in_specs=[pl.BlockSpec(memory_space=pl.ANY)] * 5,
        out_specs=pl.BlockSpec(memory_space=vmem),
        scratch_shapes=[
            vmem(traces.shape, BF16),
            vmem(dest.shape, jnp.int32),
            vmem(fold.shape, jnp.int32),
            vmem(kernels_shot.shape, BF16),
            vmem(kernels_rcv.shape, BF16),
            vmem((8, LANES), F32),
            vmem((LANES, shot_dev * LANES), F32),
            vmem((groups, span * 16 + 16, LANES), F32),
            vmem((groups, 4, span // 2, 16, LANES), BF16),
            vmem((2, 1024, 256), BF16),
            vmem((2, 1024, 256), BF16),
            vmem((2, groups, RIM, 16, LANES), BF16),
            vmem((2, groups, RIM, 16, LANES), BF16),
            vmem((8, LANES), jnp.int32),
            vmem((shot_size, 8, LANES), jnp.int32),
            vmem((share, CHUNKS, LANES), F32),
            vmem((share, rows, rows), BF16),
            vmem((share, rows, rows), BF16),
            vmem((shot_size, PIECES, groups, share // PIECES, 16, LANES), BF16),
            vmem((shot_size, PIECES, groups, share // PIECES, 16, LANES), BF16),
            vmem((2, (shots + 16) * 16 + 16, LANES), F32),
            vmem((2, 4, shots // 2 + 8, 16, LANES), BF16),
            vmem((pairs, shot_size, groups, 2, 16, LANES), BF16),
            dma((5,)),
            dma((2,)),
            dma((2,)),
            dma((peers,)),
            dma((peers,)),
            dma((shot_size, PIECES)),
            dma((shot_size, PIECES)),
            dma((pairs, peers)),
            dma((pairs, peers)),
        ],
        compiler_params=pltpu.CompilerParams(
            vmem_limit_bytes=48 << 20, collective_id=0, has_side_effects=True
        ),
        cost_estimate=pl.CostEstimate(flops=7 * 10**9, bytes_accessed=4 * 10**6, transcendentals=0),
    )(traces, dest, fold, kernels_shot, kernels_rcv)
    result = returned.reshape(groups, rcv_dev, 2, CHUNKS, LANES).transpose(0, 2, 1, 3, 4)
    return result.reshape(shot_dev, rcv_dev, samples).astype(F32)


def solution(mesh):
    in_specs = (
        P("shot", "rline", None),
        P(),
        P(),
        P("shot", "rline"),
        P("shot", "rline"),
        P("shot", "rline"),
        P(("shot", "rline")),
    )
    out_specs = P("shot", "rline", None)
    return jax.shard_map(shards, mesh=mesh, in_specs=in_specs, out_specs=out_specs, check_vma=False)
```

```python
import functools

import jax
import jax.numpy as jnp
from jax import lax
from jax.experimental import pallas as pl
from jax.experimental.pallas import tpu as pltpu
from jax.sharding import PartitionSpec as P

LANES = 128
CHUNKS = 8
BF16 = jnp.bfloat16
F32 = jnp.float32
RIM = 7
PIECES = 3
MESH = pl.DeviceIdType.MESH


def lane_index(shape):
    return lax.broadcasted_iota(jnp.int32, shape, len(shape) - 1)


def build_table(kernel_ref, rows_ref, table_ref):
    reach, fans, taps = kernel_ref.shape
    rows_ref[...] = jnp.zeros(rows_ref.shape, F32)
    for step in range(reach):
        rows_ref[step * 8 : step * 8 + fans, 0:taps] = kernel_ref[step].astype(F32)
    tap = lax.broadcasted_iota(jnp.int32, (LANES, LANES), 0)
    lane = lax.broadcasted_iota(jnp.int32, (LANES, LANES), 1)
    flat = rows_ref[...].astype(BF16)
    low = jnp.dot(flat, (lane == LANES - 1 - tap).astype(BF16), preferred_element_type=F32)
    high = jnp.dot(flat, (lane == LANES // 2 - 1 - tap).astype(BF16), preferred_element_type=F32)
    even = (lane_index((64, LANES)) // 32) % 2 == 0
    for half in range(2):
        before = jnp.zeros((64, LANES), F32)
        columns = slice(half * LANES, (half + 1) * LANES)
        for step in range(16):
            if step < reach:
                at = step * 8 + 2 * half
                row = jnp.broadcast_to(low[at : at + 1] + high[at + 1 : at + 2], (64, LANES))
                here = pltpu.roll(row, 0, 1, stride=1, stride_axis=0)
            else:
                here = jnp.zeros((64, LANES), F32)
            block = jnp.where(even, here, pltpu.roll(before, 32, 1)).astype(BF16)
            table_ref[0, step * 64 : (step + 1) * 64, columns] = block
            other = step + 1 if step % 2 == 0 else step - 1
            table_ref[1, other * 64 : (other + 1) * 64, columns] = block
            before = here


def fill_windows(source_ref, window_ref, first, pairs):
    rows = pairs * 32
    begin = first * 32 + 8
    shape = (pairs, 2, 16, LANES)
    lane = lane_index(shape)
    chunk = lax.broadcasted_iota(jnp.int32, shape, 2) % CHUNKS
    own = source_ref[pl.ds(begin, rows)].reshape(shape)
    left = source_ref[pl.ds(begin - 1, rows)].reshape(shape)
    right = source_ref[pl.ds(begin + 1, rows)].reshape(shape)
    early = jnp.where(lane < 112, own, jnp.where(chunk == 0, 0.0, left))
    late = jnp.where(lane >= 16, own, jnp.where(chunk == CHUNKS - 1, 0.0, right))
    low = lane_index((pairs * 16, LANES)) < 64

    def turned(x, shift):
        return pltpu.roll(x.reshape(pairs * 16, LANES), shift, 1)

    early_a, early_b = turned(early[:, 0], 16), turned(early[:, 1], 80)
    late_a, late_b = turned(late[:, 0], 112), turned(late[:, 1], 48)
    tiles = (
        jnp.where(low, early_a, early_b),
        jnp.where(low, late_a, late_b),
        jnp.where(low, early_b, early_a),
        jnp.where(low, late_b, late_a),
    )
    for quarter, tile in enumerate(tiles):
        window_ref[quarter, pl.ds(first, pairs)] = tile.reshape(pairs, 16, LANES).astype(BF16)


def fan_terms(blocks, table_ref, pairs):
    rows = pairs * 16
    total = len(blocks) * rows
    parts = []
    for half in range(2):
        left = jnp.concatenate(
            [
                jnp.concatenate(
                    [ref[quarter, pl.ds(first + step, pairs)].reshape(rows, LANES) for step in range(8)],
                    axis=1,
                )
                for quarter in (2 * half, 2 * half + 1)
                for ref, first in blocks
            ],
            axis=0,
        )
        coherent = jnp.dot(left, table_ref[half], preferred_element_type=F32)
        parts += [coherent[:total], coherent[total:]]
    squares, cubes = [], []
    for part in parts:
        one, two = part[:, :LANES], part[:, LANES:]
        one_sq, two_sq = one * one, two * two
        squares.append(one_sq + two_sq)
        cubes.append(one_sq * one + two_sq * two)
    lane = lane_index((total, LANES))
    low = lane < 64
    even = (lane // 32) % 2 == 0

    def merged(s):
        s02, s20 = jnp.where(low, s[0], s[2]), jnp.where(low, s[2], s[0])
        s13, s31 = jnp.where(low, s[1], s[3]), jnp.where(low, s[3], s[1])
        a = jnp.where(even, s02, s13) + pltpu.roll(jnp.where(even, s20, s31), 64, 1)
        b = jnp.where(even, s13, s02) + pltpu.roll(jnp.where(even, s31, s20), 64, 1)
        return a, b

    square_a, square_b = merged(squares)
    cube_a, cube_b = merged(cubes)
    term_a = cube_a / (square_a + 1.0)
    term_b = cube_b / (square_b + 1.0)
    first_trace = jnp.where(even, term_a, pltpu.roll(term_b, 32, 1))
    second_trace = jnp.where(even, pltpu.roll(term_b, 96, 1), term_a)
    shape = (len(blocks) * pairs, 16, LANES)
    both = jnp.stack([first_trace.reshape(shape), second_trace.reshape(shape)], axis=1)
    both = both.reshape(len(blocks), 2 * pairs, 16, LANES)
    return [both[i] for i in range(len(blocks))]


def survey_kernel(
    shot_size,
    rline_size,
    traces_hbm,
    dest_hbm,
    fold_hbm,
    shot_taps_hbm,
    rcv_taps_hbm,
    out_ref,
    traces_ref,
    dest_ref,
    fold_ref,
    shot_taps_ref,
    rcv_taps_ref,
    taps_rows_ref,
    alive_ref,
    mask_ref,
    plain_ref,
    window_ref,
    shot_table_ref,
    rcv_table_ref,
    halo_out_ref,
    halo_in_ref,
    fold_own_ref,
    fold_all_ref,
    gain_ref,
    pick_ref,
    unpick_ref,
    sent_ref,
    held_ref,
    stack_ref,
    rcv_window_ref,
    back_ref,
    load_sem,
    halo_send,
    halo_recv,
    fold_send,
    fold_recv,
    out_send,
    out_recv,
    back_send,
    back_recv,
    own_sem,
):
    shot_dev, receivers = traces_ref.shape[0], traces_ref.shape[1]
    groups = shot_dev // 2
    share = receivers // shot_size
    peers = shot_size - 1
    shots = shot_size * shot_dev
    rows = shots * CHUNKS
    me = lax.axis_index("shot")
    line = lax.axis_index("rline")
    has = (line > 0, line < rline_size - 1)
    beside = (jnp.maximum(line - 1, 0), jnp.minimum(line + 1, rline_size - 1))

    def peer(step):
        return lax.rem(me + 1 + step, shot_size)

    def source(step):
        return lax.rem(me + shot_size - 1 - step, shot_size)

    loads = [
        pltpu.make_async_copy(a, b, load_sem.at[i])
        for i, (a, b) in enumerate(
            [
                (shot_taps_hbm, shot_taps_ref),
                (rcv_taps_hbm, rcv_taps_ref),
                (dest_hbm, dest_ref),
                (fold_hbm, fold_ref),
                (traces_hbm, traces_ref),
            ]
        )
    ]
    for load in loads:
        load.start()
    barrier = pltpu.get_barrier_semaphore()
    for step in range(peers):
        pl.semaphore_signal(barrier, inc=1, device_id={"shot": peer(step)}, device_id_type=MESH)
    for side in range(2):

        @pl.when(has[side])
        def _(side=side):
            pl.semaphore_signal(barrier, inc=1, device_id={"rline": beside[side]}, device_id_type=MESH)

    alive_ref[...] = jnp.zeros(alive_ref.shape, F32)
    fold_own_ref[...] = jnp.full(fold_own_ref.shape, -1, jnp.int32)
    loads[0].wait()
    build_table(shot_taps_ref, taps_rows_ref, shot_table_ref)
    loads[2].wait()
    alive_ref[0:shot_dev, 0:receivers] = (dest_ref[...] >= 0).astype(F32)
    pick_shot = lax.broadcasted_iota(jnp.int32, (8, shot_dev * LANES), 0) == (
        lax.broadcasted_iota(jnp.int32, (8, shot_dev * LANES), 1) // LANES
    )
    mask_ref[...] = lax.dot_general(
        alive_ref[...], pick_shot.astype(F32), (((0,), (0,)), ((), ())), preferred_element_type=F32
    )
    loads[4].wait()
    for s in range(shot_dev):

        @pl.loop(0, receivers // 16)
        def _(i):
            x = traces_ref[s, pl.ds(i * 16, 16)].astype(F32)
            for half in range(2):
                mask = mask_ref[pl.ds(i * 16 + half * 8, 8), s * LANES : (s + 1) * LANES]
                begin = (i * 16 + half * 8 + RIM) * 16 + 8 + (s % 2) * CHUNKS
                for c in range(CHUNKS):
                    piece = x[half * 8 : half * 8 + 8, c * LANES : (c + 1) * LANES]
                    plain_ref[s // 2, pl.ds(begin + c, 8, stride=16)] = piece * mask

    for g in range(groups):
        for side, begin in enumerate((receivers - RIM, 0)):
            edge = plain_ref[g, (RIM + begin) * 16 + 8 : (2 * RIM + begin) * 16 + 8]
            halo_out_ref[side, g] = edge.astype(BF16).reshape(RIM, 16, LANES)
    loads[3].wait()
    fold_own_ref[0:shot_dev, 0:receivers] = fold_ref[...]

    step_pairs = 5
    span_pairs = (receivers + 2 * RIM) // 2
    for g in range(groups):

        @pl.loop(1, span_pairs // step_pairs - 1)
        def _(i):
            fill_windows(plain_ref.at[g], window_ref.at[g], i * step_pairs, step_pairs)

    def halo(side):
        return pltpu.make_async_remote_copy(
            src_ref=halo_out_ref.at[side],
            dst_ref=halo_in_ref.at[side],
            send_sem=halo_send.at[side],
            recv_sem=halo_recv.at[side],
            device_id={"rline": beside[1 - side]},
            device_id_type=MESH,
        )

    def fold_copy(step, slot):
        return pltpu.make_async_remote_copy(
            src_ref=fold_own_ref,
            dst_ref=fold_all_ref.at[slot],
            send_sem=fold_send.at[step],
            recv_sem=fold_recv.at[step],
            device_id={"shot": peer(step)},
            device_id_type=MESH,
        )

    piece = share // PIECES

    def out_copy(target, p, slot):
        return pltpu.make_async_remote_copy(
            src_ref=sent_ref.at[target, p],
            dst_ref=held_ref.at[slot, p],
            send_sem=out_send.at[target, p],
            recv_sem=out_recv.at[slot, p],
            device_id={"shot": target},
            device_id_type=MESH,
        )

    pl.semaphore_wait(barrier, peers + has[0].astype(jnp.int32) + has[1].astype(jnp.int32))
    for side in range(2):

        @pl.when(has[1 - side])
        def _(side=side):
            halo(side).start()
    for step in range(peers):
        fold_copy(step, me).start()
    fold_all_ref[me] = fold_own_ref[...]

    def shot_blocks(items):
        blocks = [
            (window_ref.at[g], (target * share + p * piece) // 2) for target, p in items for g in range(groups)
        ]
        terms = fan_terms(blocks, shot_table_ref, piece // 2)
        for n, (target, p) in enumerate(items):
            for g in range(groups):
                begin = (target * share + p * piece + RIM) * 16 + 8
                centre = plain_ref[g, begin : begin + piece * 16].reshape(piece, 16, LANES)
                sent_ref[target, p, g] = (centre - terms[n * groups + g]).astype(BF16)
        for target, p in items:

            @pl.when(me != target)
            def _(target=target, p=p):
                out_copy(target, p, me).start()

    inner = range(1, shot_size - 1)
    for p in range(PIECES - 1):
        shot_blocks([(target, p) for target in inner])

    for side in range(2):
        land = (RIM + receivers) * 16 + 8 if side else 8

        @pl.when(has[side])
        def _(side=side, land=land):
            halo(side).wait_recv()
            for g in range(groups):
                edge = halo_in_ref[side, g].astype(F32).reshape(RIM * 16, LANES)
                plain_ref[g, land : land + RIM * 16] = edge

        @pl.when(jnp.logical_not(has[side]))
        def _(land=land):
            for g in range(groups):
                plain_ref[g, land : land + RIM * 16] = jnp.zeros((RIM * 16, LANES), F32)

    for g in range(groups):
        for first in (0, span_pairs - step_pairs):
            fill_windows(plain_ref.at[g], window_ref.at[g], first, step_pairs)
    shot_blocks([(target, p) for p in range(PIECES) for target in (0, shot_size - 1)])
    shot_blocks([(target, PIECES - 1) for target in inner])
    held_ref[me] = sent_ref[me]

    loads[1].wait()
    build_table(rcv_taps_ref, taps_rows_ref, rcv_table_ref)
    for step in range(peers):
        fold_copy(step, source(step)).wait_recv()
    folds = fold_all_ref[...].reshape(shot_size * 8, LANES).astype(F32)
    take = lax.broadcasted_iota(jnp.int32, (16, LANES), 1) == (
        me * share + lax.broadcasted_iota(jnp.int32, (16, LANES), 0)
    )
    mine = lax.dot_general(
        take.astype(F32), folds, (((1,), (1,)), ((), ())), preferred_element_type=F32
    )
    entry = lax.broadcasted_iota(jnp.int32, (shot_size * 8, rows), 0)
    shot = lax.broadcasted_iota(jnp.int32, (shot_size * 8, rows), 1) // CHUNKS
    spread = ((entry // 8) * shot_dev + entry % 8 == shot) & (entry % 8 < shot_dev)
    spread = spread.astype(F32)
    labels = jnp.dot(mine, spread, preferred_element_type=F32)
    live = jnp.sum((labels >= 0.0).astype(F32), axis=1, keepdims=True) / CHUNKS
    gains = jnp.broadcast_to(jnp.sqrt(shots / live), (16, LANES))
    chunk = (lax.broadcasted_iota(jnp.int32, (16, rows), 1) % CHUNKS).astype(F32)
    labels = jnp.where(labels >= 0.0, labels * CHUNKS + chunk, -1.0)
    columns = lax.dot_general(spread, mine, (((0,), (1,)), ((), ())), preferred_element_type=F32)
    chunk = (lax.broadcasted_iota(jnp.int32, (rows, 16), 0) % CHUNKS).astype(F32)
    columns = jnp.where(columns >= 0.0, columns * CHUNKS + chunk, -1.0)
    down = lax.broadcasted_iota(jnp.int32, (rows, rows), 0).astype(F32)
    across = lax.broadcasted_iota(jnp.int32, (rows, rows), 1).astype(F32)
    for k in range(share):
        gain_ref[k] = jnp.broadcast_to(gains[k : k + 1], (CHUNKS, LANES))
        pick_ref[k] = jnp.where(labels[k : k + 1] == down, 1.0, 0.0).astype(BF16)
        unpick_ref[k] = jnp.where(columns[:, k : k + 1] == across, 1.0, 0.0).astype(BF16)

    for slot in range(2):
        stack_ref[slot, 0 : RIM * 16 + 8] = jnp.zeros((RIM * 16 + 8, LANES), F32)
        end = (RIM + shots) * 16 + 8
        stack_ref[slot, end:] = jnp.zeros((stack_ref.shape[1] - end, LANES), F32)

    def back_copy(pair, step, owner):
        return pltpu.make_async_remote_copy(
            src_ref=back_ref.at[pair, peer(step)],
            dst_ref=out_ref.at[:, pl.ds(owner * share + 2 * pair, 2)],
            send_sem=back_send.at[pair, step],
            recv_sem=back_recv.at[pair, step],
            device_id={"shot": peer(step)},
            device_id_type=MESH,
        )

    def back_own(pair):
        return pltpu.make_async_copy(
            back_ref.at[pair, me], out_ref.at[:, pl.ds(me * share + 2 * pair, 2)], own_sem.at[pair]
        )

    def prepare(pair):
        slot = pair % 2
        for side in range(2):
            k = 2 * pair + side
            x = held_ref[:, k // piece, :, k % piece].reshape(rows, LANES)
            stack = jnp.dot(pick_ref[k], x, preferred_element_type=F32)
            for p in range(shots):
                begin = (RIM + p) * 16 + 8 + side * CHUNKS
                stack_ref[slot, begin : begin + CHUNKS] = stack[p * CHUNKS : (p + 1) * CHUNKS]
        for i in range(4):
            fill_windows(stack_ref.at[slot], rcv_window_ref.at[slot], i * 6, 6)

    def finish(pair):
        slot = pair % 2
        (terms,) = fan_terms([(rcv_window_ref.at[slot], 0)], rcv_table_ref, shots // 2)
        begin = RIM * 16 + 8
        value = stack_ref[slot, begin : begin + shots * 16].reshape(shots, 16, LANES) - terms
        for side in range(2):
            k = 2 * pair + side
            own = value[:, side * CHUNKS : (side + 1) * CHUNKS] * gain_ref[k][None]
            back = jnp.dot(
                unpick_ref[k], own.reshape(rows, LANES).astype(BF16), preferred_element_type=F32
            )
            back_ref[pair, :, :, side] = back.astype(BF16).reshape(shot_size, groups, 16, LANES)
        for step in range(peers):
            back_copy(pair, step, me).start()
        back_own(pair).start()

    def arrive(p):
        for step in range(peers):
            out_copy(peer(step), p, source(step)).wait_recv()

    pairs = share // 2
    arrive(0)
    prepare(0)
    for pair in range(pairs):
        if pair + 1 < pairs:
            if (2 * (pair + 1)) % piece == 0:
                arrive((2 * (pair + 1)) // piece)
            prepare(pair + 1)
        finish(pair)

    for side in range(2):

        @pl.when(has[1 - side])
        def _(side=side):
            halo(side).wait_send()

    for step in range(peers):
        fold_copy(step, me).wait_send()
        for p in range(PIECES):
            out_copy(peer(step), p, me).wait_send()
    for pair in range(pairs):
        back_own(pair).wait()
        for step in range(peers):
            back_copy(pair, step, me).wait_send()
            back_copy(pair, step, source(step)).wait_recv()


def shards(traces, kernels_shot, kernels_rcv, dest, gather, fold, counts):
    shot_dev, rcv_dev, samples = traces.shape
    shot_size = lax.axis_size("shot")
    rline_size = lax.axis_size("rline")
    shots = shot_dev * shot_size
    share = rcv_dev // shot_size
    rows = shots * CHUNKS
    groups = shot_dev // 2
    peers = shot_size - 1
    pairs = share // 2
    span = rcv_dev + 2 * RIM
    fans, trace_taps, sample_taps = kernels_shot.shape
    dma = pltpu.SemaphoreType.DMA
    vmem = pltpu.VMEM
    returned = pl.pallas_call(
        functools.partial(survey_kernel, shot_size, rline_size),
        out_shape=jax.ShapeDtypeStruct((groups, rcv_dev, 16, LANES), BF16),
        in_specs=[pl.BlockSpec(memory_space=pltpu.HBM)] * 5,
        out_specs=pl.BlockSpec(memory_space=pltpu.HBM),
        scratch_shapes=[
            vmem(traces.shape, BF16),
            vmem(dest.shape, jnp.int32),
            vmem(fold.shape, jnp.int32),
            vmem((trace_taps, fans, sample_taps), BF16),
            vmem((trace_taps, fans, sample_taps), BF16),
            vmem((LANES, LANES), F32),
            vmem((8, LANES), F32),
            vmem((LANES, shot_dev * LANES), F32),
            vmem((groups, span * 16 + 16, LANES), F32),
            vmem((groups, 4, span // 2, 16, LANES), BF16),
            vmem((2, 1024, 256), BF16),
            vmem((2, 1024, 256), BF16),
            vmem((2, groups, RIM, 16, LANES), BF16),
            vmem((2, groups, RIM, 16, LANES), BF16),
            vmem((8, LANES), jnp.int32),
            vmem((shot_size, 8, LANES), jnp.int32),
            vmem((share, CHUNKS, LANES), F32),
            vmem((share, rows, rows), BF16),
            vmem((share, rows, rows), BF16),
            vmem((shot_size, PIECES, groups, share // PIECES, 16, LANES), BF16),
            vmem((shot_size, PIECES, groups, share // PIECES, 16, LANES), BF16),
            vmem((2, (shots + 16) * 16 + 16, LANES), F32),
            vmem((2, 4, shots // 2 + 8, 16, LANES), BF16),
            vmem((pairs, shot_size, groups, 2, 16, LANES), BF16),
            dma((5,)),
            dma((2,)),
            dma((2,)),
            dma((peers,)),
            dma((peers,)),
            dma((shot_size, PIECES)),
            dma((shot_size, PIECES)),
            dma((pairs, peers)),
            dma((pairs, peers)),
            dma((pairs,)),
        ],
        compiler_params=pltpu.CompilerParams(
            vmem_limit_bytes=61 << 20, collective_id=0, has_side_effects=True
        ),
        cost_estimate=pl.CostEstimate(flops=7 * 10**9, bytes_accessed=4 * 10**6, transcendentals=0),
    )(traces, dest, fold, kernels_shot.transpose(1, 0, 2), kernels_rcv.transpose(1, 0, 2))
    result = returned.reshape(groups, rcv_dev, 2, CHUNKS, LANES).transpose(0, 2, 1, 3, 4)
    return result.reshape(shot_dev, rcv_dev, samples).astype(F32)


def solution(mesh):
    in_specs = (
        P("shot", "rline", None),
        P(),
        P(),
        P("shot", "rline"),
        P("shot", "rline"),
        P("shot", "rline"),
        P(("shot", "rline")),
    )
    out_specs = P("shot", "rline", None)
    return jax.shard_map(shards, mesh=mesh, in_specs=in_specs, out_specs=out_specs, check_vma=False)
```

```python
import functools

import jax
import jax.numpy as jnp
from jax import lax
from jax.experimental import pallas as pl
from jax.experimental.pallas import tpu as pltpu
from jax.sharding import PartitionSpec as P

LANES = 128
CHUNKS = 8
BF16 = jnp.bfloat16
F32 = jnp.float32
RIM = 7
PIECES = 3
MESH = pl.DeviceIdType.MESH


def lane_index(shape):
    return lax.broadcasted_iota(jnp.int32, shape, len(shape) - 1)


def build_table(kernel_ref, rows_ref, table_ref):
    reach, fans, taps = kernel_ref.shape
    rows_ref[...] = jnp.zeros(rows_ref.shape, F32)
    for step in range(reach):
        rows_ref[step * 8 : step * 8 + fans, 0:taps] = kernel_ref[step].astype(F32)
    tap = lax.broadcasted_iota(jnp.int32, (LANES, LANES), 0)
    lane = lax.broadcasted_iota(jnp.int32, (LANES, LANES), 1)
    flat = rows_ref[...].astype(BF16)
    low = jnp.dot(flat, (lane == LANES - 1 - tap).astype(BF16), preferred_element_type=F32)
    high = jnp.dot(flat, (lane == LANES // 2 - 1 - tap).astype(BF16), preferred_element_type=F32)
    even = (lane_index((64, LANES)) // 32) % 2 == 0
    for half in range(2):
        before = jnp.zeros((64, LANES), F32)
        columns = slice(half * LANES, (half + 1) * LANES)
        for step in range(16):
            if step < reach:
                at = step * 8 + 2 * half
                row = jnp.broadcast_to(low[at : at + 1] + high[at + 1 : at + 2], (64, LANES))
                here = pltpu.roll(row, 0, 1, stride=1, stride_axis=0)
            else:
                here = jnp.zeros((64, LANES), F32)
            block = jnp.where(even, here, pltpu.roll(before, 32, 1)).astype(BF16)
            table_ref[0, step * 64 : (step + 1) * 64, columns] = block
            other = step + 1 if step % 2 == 0 else step - 1
            table_ref[1, other * 64 : (other + 1) * 64, columns] = block
            before = here


def fill_windows(source_ref, window_ref, first, pairs):
    rows = pairs * 32
    begin = first * 32 + 8
    shape = (pairs, 2, 16, LANES)
    lane = lane_index(shape)
    chunk = lax.broadcasted_iota(jnp.int32, shape, 2) % CHUNKS
    own = source_ref[pl.ds(begin, rows)].reshape(shape)
    left = source_ref[pl.ds(begin - 1, rows)].reshape(shape)
    right = source_ref[pl.ds(begin + 1, rows)].reshape(shape)
    early = jnp.where(lane < 112, own, jnp.where(chunk == 0, 0.0, left))
    late = jnp.where(lane >= 16, own, jnp.where(chunk == CHUNKS - 1, 0.0, right))
    low = lane_index((pairs * 16, LANES)) < 64

    def turned(x, shift):
        return pltpu.roll(x.reshape(pairs * 16, LANES), shift, 1)

    early_a, early_b = turned(early[:, 0], 16), turned(early[:, 1], 80)
    late_a, late_b = turned(late[:, 0], 112), turned(late[:, 1], 48)
    tiles = (
        jnp.where(low, early_a, early_b),
        jnp.where(low, late_a, late_b),
        jnp.where(low, early_b, early_a),
        jnp.where(low, late_b, late_a),
    )
    for quarter, tile in enumerate(tiles):
        window_ref[quarter, pl.ds(first, pairs)] = tile.reshape(pairs, 16, LANES).astype(BF16)


def fan_terms(blocks, table_ref, pairs):
    rows = pairs * 16
    total = len(blocks) * rows
    parts = []
    for half in range(2):
        left = jnp.concatenate(
            [
                jnp.concatenate(
                    [ref[quarter, pl.ds(first + step, pairs)].reshape(rows, LANES) for step in range(8)],
                    axis=1,
                )
                for quarter in (2 * half, 2 * half + 1)
                for ref, first in blocks
            ],
            axis=0,
        )
        coherent = jnp.dot(left, table_ref[half], preferred_element_type=F32)
        parts += [coherent[:total], coherent[total:]]
    squares, cubes = [], []
    for part in parts:
        one, two = part[:, :LANES], part[:, LANES:]
        one_sq, two_sq = one * one, two * two
        squares.append(one_sq + two_sq)
        cubes.append(one_sq * one + two_sq * two)
    lane = lane_index((total, LANES))
    low = lane < 64
    even = (lane // 32) % 2 == 0

    def merged(s):
        s02, s20 = jnp.where(low, s[0], s[2]), jnp.where(low, s[2], s[0])
        s13, s31 = jnp.where(low, s[1], s[3]), jnp.where(low, s[3], s[1])
        a = jnp.where(even, s02, s13) + pltpu.roll(jnp.where(even, s20, s31), 64, 1)
        b = jnp.where(even, s13, s02) + pltpu.roll(jnp.where(even, s31, s20), 64, 1)
        return a, b

    square_a, square_b = merged(squares)
    cube_a, cube_b = merged(cubes)
    term_a = cube_a / (square_a + 1.0)
    term_b = cube_b / (square_b + 1.0)
    first_trace = jnp.where(even, term_a, pltpu.roll(term_b, 32, 1))
    second_trace = jnp.where(even, pltpu.roll(term_b, 96, 1), term_a)
    shape = (len(blocks) * pairs, 16, LANES)
    both = jnp.stack([first_trace.reshape(shape), second_trace.reshape(shape)], axis=1)
    both = both.reshape(len(blocks), 2 * pairs, 16, LANES)
    return [both[i] for i in range(len(blocks))]


def survey_kernel(
    shot_size,
    rline_size,
    traces_hbm,
    dest_hbm,
    fold_hbm,
    shot_taps_hbm,
    rcv_taps_hbm,
    out_ref,
    traces_ref,
    dest_ref,
    fold_ref,
    shot_taps_ref,
    rcv_taps_ref,
    taps_rows_ref,
    alive_ref,
    mask_ref,
    plain_ref,
    window_ref,
    shot_table_ref,
    rcv_table_ref,
    halo_out_ref,
    halo_in_ref,
    fold_own_ref,
    fold_all_ref,
    gain_ref,
    unpick_ref,
    sent_ref,
    held_ref,
    stack_ref,
    rcv_window_ref,
    back_ref,
    load_sem,
    halo_send,
    halo_recv,
    fold_send,
    fold_recv,
    out_send,
    out_recv,
    back_send,
    back_recv,
    own_sem,
):
    shot_dev, receivers = traces_ref.shape[0], traces_ref.shape[1]
    groups = shot_dev // 2
    share = receivers // shot_size
    peers = shot_size - 1
    shots = shot_size * shot_dev
    rows = shots * CHUNKS
    me = lax.axis_index("shot")
    line = lax.axis_index("rline")
    has = (line > 0, line < rline_size - 1)
    beside = (jnp.maximum(line - 1, 0), jnp.minimum(line + 1, rline_size - 1))

    def peer(step):
        return lax.rem(me + 1 + step, shot_size)

    def source(step):
        return lax.rem(me + shot_size - 1 - step, shot_size)

    loads = [
        pltpu.make_async_copy(a, b, load_sem.at[i])
        for i, (a, b) in enumerate(
            [
                (shot_taps_hbm, shot_taps_ref),
                (rcv_taps_hbm, rcv_taps_ref),
                (dest_hbm, dest_ref),
                (fold_hbm, fold_ref),
            ]
            + [(traces_hbm.at[s], traces_ref.at[s]) for s in range(shot_dev)]
        )
    ]
    for load in loads:
        load.start()
    barrier = pltpu.get_barrier_semaphore()
    for step in range(peers):
        pl.semaphore_signal(barrier, inc=1, device_id={"shot": peer(step)}, device_id_type=MESH)
    for side in range(2):

        @pl.when(has[side])
        def _(side=side):
            pl.semaphore_signal(barrier, inc=1, device_id={"rline": beside[side]}, device_id_type=MESH)

    alive_ref[...] = jnp.zeros(alive_ref.shape, F32)
    fold_own_ref[...] = jnp.full(fold_own_ref.shape, -1, jnp.int32)
    loads[0].wait()
    build_table(shot_taps_ref, taps_rows_ref, shot_table_ref)
    loads[1].wait()
    build_table(rcv_taps_ref, taps_rows_ref, rcv_table_ref)
    loads[2].wait()
    alive_ref[0:shot_dev, 0:receivers] = (dest_ref[...] >= 0).astype(F32)
    pick_shot = lax.broadcasted_iota(jnp.int32, (8, shot_dev * LANES), 0) == (
        lax.broadcasted_iota(jnp.int32, (8, shot_dev * LANES), 1) // LANES
    )
    mask_ref[...] = lax.dot_general(
        alive_ref[...], pick_shot.astype(F32), (((0,), (0,)), ((), ())), preferred_element_type=F32
    )
    for s in range(shot_dev):
        loads[4 + s].wait()
        for i in range(receivers // 16):
            x = traces_ref[s, pl.ds(i * 16, 16)].astype(F32)
            for half in range(2):
                mask = mask_ref[i * 16 + half * 8 : i * 16 + half * 8 + 8, s * LANES : (s + 1) * LANES]
                begin = (i * 16 + half * 8 + RIM) * 16 + 8 + (s % 2) * CHUNKS
                for c in range(CHUNKS):
                    piece = x[half * 8 : half * 8 + 8, c * LANES : (c + 1) * LANES]
                    plain_ref[s // 2, pl.ds(begin + c, 8, stride=16)] = piece * mask

    for g in range(groups):
        for side, begin in enumerate((receivers - RIM, 0)):
            edge = plain_ref[g, (RIM + begin) * 16 + 8 : (2 * RIM + begin) * 16 + 8]
            halo_out_ref[side, g] = edge.astype(BF16).reshape(RIM, 16, LANES)
    loads[3].wait()
    fold_own_ref[0:shot_dev, 0:receivers] = fold_ref[...]

    step_pairs = 5
    span_pairs = (receivers + 2 * RIM) // 2
    for g in range(groups):

        for i in range(1, span_pairs // step_pairs - 1):
            fill_windows(plain_ref.at[g], window_ref.at[g], i * step_pairs, step_pairs)

    def halo(side):
        return pltpu.make_async_remote_copy(
            src_ref=halo_out_ref.at[side],
            dst_ref=halo_in_ref.at[side],
            send_sem=halo_send.at[side],
            recv_sem=halo_recv.at[side],
            device_id={"rline": beside[1 - side]},
            device_id_type=MESH,
        )

    def fold_copy(step, slot):
        return pltpu.make_async_remote_copy(
            src_ref=fold_own_ref,
            dst_ref=fold_all_ref.at[slot],
            send_sem=fold_send.at[step],
            recv_sem=fold_recv.at[step],
            device_id={"shot": peer(step)},
            device_id_type=MESH,
        )

    piece = share // PIECES

    def out_copy(target, p, slot):
        return pltpu.make_async_remote_copy(
            src_ref=sent_ref.at[target, p],
            dst_ref=held_ref.at[slot, p],
            send_sem=out_send.at[target, p],
            recv_sem=out_recv.at[slot, p],
            device_id={"shot": target},
            device_id_type=MESH,
        )

    pl.semaphore_wait(barrier, peers + has[0].astype(jnp.int32) + has[1].astype(jnp.int32))
    for side in range(2):

        @pl.when(has[1 - side])
        def _(side=side):
            halo(side).start()
    for step in range(peers):
        fold_copy(step, me).start()
    fold_all_ref[me] = fold_own_ref[...]

    def shot_blocks(items):
        blocks = [
            (window_ref.at[g], (target * share + p * piece) // 2) for target, p in items for g in range(groups)
        ]
        terms = fan_terms(blocks, shot_table_ref, piece // 2)
        for n, (target, p) in enumerate(items):
            for g in range(groups):
                begin = (target * share + p * piece + RIM) * 16 + 8
                centre = plain_ref[g, begin : begin + piece * 16].reshape(piece, 16, LANES)
                sent_ref[target, p, g] = (centre - terms[n * groups + g]).astype(BF16)
        for target, p in items:

            @pl.when(me != target)
            def _(target=target, p=p):
                out_copy(target, p, me).start()

    inner = range(1, shot_size - 1)
    for p in range(PIECES - 1):
        shot_blocks([(target, p) for target in inner])

    for side in range(2):
        land = (RIM + receivers) * 16 + 8 if side else 8

        @pl.when(has[side])
        def _(side=side, land=land):
            halo(side).wait_recv()
            for g in range(groups):
                edge = halo_in_ref[side, g].astype(F32).reshape(RIM * 16, LANES)
                plain_ref[g, land : land + RIM * 16] = edge

        @pl.when(jnp.logical_not(has[side]))
        def _(land=land):
            for g in range(groups):
                plain_ref[g, land : land + RIM * 16] = jnp.zeros((RIM * 16, LANES), F32)

    for g in range(groups):
        for first in (0, span_pairs - step_pairs):
            fill_windows(plain_ref.at[g], window_ref.at[g], first, step_pairs)
    shot_blocks([(target, p) for p in range(PIECES) for target in (0, shot_size - 1)])
    shot_blocks([(target, PIECES - 1) for target in inner])
    held_ref[me] = sent_ref[me]

    for step in range(peers):
        fold_copy(step, source(step)).wait_recv()
    folds = fold_all_ref[...].reshape(shot_size * 8, LANES).astype(F32)
    take = lax.broadcasted_iota(jnp.int32, (16, LANES), 1) == (
        me * share + lax.broadcasted_iota(jnp.int32, (16, LANES), 0)
    )
    mine = lax.dot_general(
        take.astype(F32), folds, (((1,), (1,)), ((), ())), preferred_element_type=F32
    )
    entry = lax.broadcasted_iota(jnp.int32, (shot_size * 8, rows), 0)
    shot = lax.broadcasted_iota(jnp.int32, (shot_size * 8, rows), 1) // CHUNKS
    spread = ((entry // 8) * shot_dev + entry % 8 == shot) & (entry % 8 < shot_dev)
    spread = spread.astype(F32)
    labels = jnp.dot(mine, spread, preferred_element_type=F32)
    live = jnp.sum((labels >= 0.0).astype(F32), axis=1, keepdims=True) / CHUNKS
    gains = jnp.broadcast_to(jnp.sqrt(shots / live), (16, LANES))
    chunk = (lax.broadcasted_iota(jnp.int32, (16, rows), 1) % CHUNKS).astype(F32)
    labels = jnp.where(labels >= 0.0, labels * CHUNKS + chunk, -1.0)
    columns = lax.dot_general(spread, mine, (((0,), (1,)), ((), ())), preferred_element_type=F32)
    chunk = (lax.broadcasted_iota(jnp.int32, (rows, 16), 0) % CHUNKS).astype(F32)
    columns = jnp.where(columns >= 0.0, columns * CHUNKS + chunk, -1.0)
    down = lax.broadcasted_iota(jnp.int32, (rows, rows), 0).astype(F32)
    across = lax.broadcasted_iota(jnp.int32, (rows, rows), 1).astype(F32)
    for k in range(share):
        gain_ref[k] = jnp.broadcast_to(gains[k : k + 1], (CHUNKS, LANES))

    for slot in range(2):
        stack_ref[slot, 0 : RIM * 16 + 8] = jnp.zeros((RIM * 16 + 8, LANES), F32)
        end = (RIM + shots) * 16 + 8
        stack_ref[slot, end:] = jnp.zeros((stack_ref.shape[1] - end, LANES), F32)

    def back_copy(pair, step, owner):
        return pltpu.make_async_remote_copy(
            src_ref=back_ref.at[pair, peer(step)],
            dst_ref=out_ref.at[:, pl.ds(owner * share + 2 * pair, 2)],
            send_sem=back_send.at[pair, step],
            recv_sem=back_recv.at[pair, step],
            device_id={"shot": peer(step)},
            device_id_type=MESH,
        )

    def back_own(pair):
        return pltpu.make_async_copy(
            back_ref.at[pair, me], out_ref.at[:, pl.ds(me * share + 2 * pair, 2)], own_sem.at[pair]
        )

    def prepare(pair):
        slot = pair % 2
        for side in range(2):
            k = 2 * pair + side
            x = held_ref[:, k // piece, :, k % piece].reshape(rows, LANES)
            pick = jnp.where(labels[k : k + 1] == down, 1.0, 0.0).astype(BF16)
            unpick_ref[k] = jnp.where(columns[:, k : k + 1] == across, 1.0, 0.0).astype(BF16)
            stack = jnp.dot(pick, x, preferred_element_type=F32)
            for p in range(shots):
                begin = (RIM + p) * 16 + 8 + side * CHUNKS
                stack_ref[slot, begin : begin + CHUNKS] = stack[p * CHUNKS : (p + 1) * CHUNKS]
        for i in range(4):
            fill_windows(stack_ref.at[slot], rcv_window_ref.at[slot], i * 6, 6)

    def finish(pair):
        slot = pair % 2
        (terms,) = fan_terms([(rcv_window_ref.at[slot], 0)], rcv_table_ref, shots // 2)
        begin = RIM * 16 + 8
        value = stack_ref[slot, begin : begin + shots * 16].reshape(shots, 16, LANES) - terms
        for side in range(2):
            k = 2 * pair + side
            own = value[:, side * CHUNKS : (side + 1) * CHUNKS] * gain_ref[k][None]
            back = jnp.dot(
                unpick_ref[k], own.reshape(rows, LANES).astype(BF16), preferred_element_type=F32
            )
            back_ref[pair, :, :, side] = back.astype(BF16).reshape(shot_size, groups, 16, LANES)
        for step in range(peers):
            back_copy(pair, step, me).start()
        back_own(pair).start()

    def arrive(p):
        for step in range(peers):
            out_copy(peer(step), p, source(step)).wait_recv()

    pairs = share // 2
    arrive(0)
    prepare(0)
    for pair in range(pairs):
        if pair + 1 < pairs:
            if (2 * (pair + 1)) % piece == 0:
                arrive((2 * (pair + 1)) // piece)
            prepare(pair + 1)
        finish(pair)

    for side in range(2):

        @pl.when(has[1 - side])
        def _(side=side):
            halo(side).wait_send()

    for step in range(peers):
        fold_copy(step, me).wait_send()
        for p in range(PIECES):
            out_copy(peer(step), p, me).wait_send()
    for pair in range(pairs):
        back_own(pair).wait()
        for step in range(peers):
            back_copy(pair, step, me).wait_send()
            back_copy(pair, step, source(step)).wait_recv()


def shards(traces, kernels_shot, kernels_rcv, dest, gather, fold, counts):
    shot_dev, rcv_dev, samples = traces.shape
    shot_size = lax.axis_size("shot")
    rline_size = lax.axis_size("rline")
    shots = shot_dev * shot_size
    share = rcv_dev // shot_size
    rows = shots * CHUNKS
    groups = shot_dev // 2
    peers = shot_size - 1
    pairs = share // 2
    span = rcv_dev + 2 * RIM
    fans, trace_taps, sample_taps = kernels_shot.shape
    dma = pltpu.SemaphoreType.DMA
    vmem = pltpu.VMEM
    returned = pl.pallas_call(
        functools.partial(survey_kernel, shot_size, rline_size),
        out_shape=jax.ShapeDtypeStruct((groups, rcv_dev, 16, LANES), BF16),
        in_specs=[pl.BlockSpec(memory_space=pltpu.HBM)] * 5,
        out_specs=pl.BlockSpec(memory_space=pltpu.HBM),
        scratch_shapes=[
            vmem(traces.shape, BF16),
            vmem(dest.shape, jnp.int32),
            vmem(fold.shape, jnp.int32),
            vmem((trace_taps, fans, sample_taps), BF16),
            vmem((trace_taps, fans, sample_taps), BF16),
            vmem((LANES, LANES), F32),
            vmem((8, LANES), F32),
            vmem((LANES, shot_dev * LANES), F32),
            vmem((groups, span * 16 + 16, LANES), F32),
            vmem((groups, 4, span // 2, 16, LANES), BF16),
            vmem((2, 1024, 256), BF16),
            vmem((2, 1024, 256), BF16),
            vmem((2, groups, RIM, 16, LANES), BF16),
            vmem((2, groups, RIM, 16, LANES), BF16),
            vmem((8, LANES), jnp.int32),
            vmem((shot_size, 8, LANES), jnp.int32),
            vmem((share, CHUNKS, LANES), F32),
            vmem((share, rows, rows), BF16),
            vmem((shot_size, PIECES, groups, share // PIECES, 16, LANES), BF16),
            vmem((shot_size, PIECES, groups, share // PIECES, 16, LANES), BF16),
            vmem((2, (shots + 16) * 16 + 16, LANES), F32),
            vmem((2, 4, shots // 2 + 8, 16, LANES), BF16),
            vmem((pairs, shot_size, groups, 2, 16, LANES), BF16),
            dma((4 + shot_dev,)),
            dma((2,)),
            dma((2,)),
            dma((peers,)),
            dma((peers,)),
            dma((shot_size, PIECES)),
            dma((shot_size, PIECES)),
            dma((pairs, peers)),
            dma((pairs, peers)),
            dma((pairs,)),
        ],
        compiler_params=pltpu.CompilerParams(
            vmem_limit_bytes=61 << 20, collective_id=0, has_side_effects=True
        ),
        cost_estimate=pl.CostEstimate(flops=7 * 10**9, bytes_accessed=4 * 10**6, transcendentals=0),
    )(traces, dest, fold, kernels_shot.transpose(1, 0, 2), kernels_rcv.transpose(1, 0, 2))
    result = returned.reshape(groups, rcv_dev, 2, CHUNKS, LANES).transpose(0, 2, 1, 3, 4)
    return result.reshape(shot_dev, rcv_dev, samples).astype(F32)


def solution(mesh):
    in_specs = (
        P("shot", "rline", None),
        P(),
        P(),
        P("shot", "rline"),
        P("shot", "rline"),
        P("shot", "rline"),
        P(("shot", "rline")),
    )
    out_specs = P("shot", "rline", None)
    return jax.shard_map(shards, mesh=mesh, in_specs=in_specs, out_specs=out_specs, check_vma=False)
```

```python
import functools

import jax
import jax.numpy as jnp
from jax import lax
from jax.experimental import pallas as pl
from jax.experimental.pallas import tpu as pltpu
from jax.sharding import PartitionSpec as P

LANES = 128
CHUNKS = 8
BF16 = jnp.bfloat16
F32 = jnp.float32
RIM = 7
MESH = pl.DeviceIdType.MESH


def lane_index(shape):
    return lax.broadcasted_iota(jnp.int32, shape, len(shape) - 1)


def build_table(kernel_ref, rows_ref, table_ref):
    reach, fans, taps = kernel_ref.shape
    rows_ref[...] = jnp.zeros(rows_ref.shape, F32)
    for step in range(reach):
        rows_ref[step * 8 : step * 8 + fans, 0:taps] = kernel_ref[step].astype(F32)
    tap = lax.broadcasted_iota(jnp.int32, (LANES, LANES), 0)
    lane = lax.broadcasted_iota(jnp.int32, (LANES, LANES), 1)
    flat = rows_ref[...].astype(BF16)
    low = jnp.dot(flat, (lane == LANES - 1 - tap).astype(BF16), preferred_element_type=F32)
    high = jnp.dot(flat, (lane == LANES // 2 - 1 - tap).astype(BF16), preferred_element_type=F32)
    even = (lane_index((64, LANES)) // 32) % 2 == 0
    for half in range(2):
        before = jnp.zeros((64, LANES), F32)
        columns = slice(half * LANES, (half + 1) * LANES)
        for step in range(16):
            if step < reach:
                at = step * 8 + 2 * half
                row = jnp.broadcast_to(low[at : at + 1] + high[at + 1 : at + 2], (64, LANES))
                here = pltpu.roll(row, 0, 1, stride=1, stride_axis=0)
            else:
                here = jnp.zeros((64, LANES), F32)
            block = jnp.where(even, here, pltpu.roll(before, 32, 1)).astype(BF16)
            table_ref[0, step * 64 : (step + 1) * 64, columns] = block
            other = step + 1 if step % 2 == 0 else step - 1
            table_ref[1, other * 64 : (other + 1) * 64, columns] = block
            before = here


def fill_windows(source_ref, window_ref, first, pairs):
    rows = pairs * 32
    begin = first * 32 + 8
    shape = (pairs, 2, 16, LANES)
    lane = lane_index(shape)
    chunk = lax.broadcasted_iota(jnp.int32, shape, 2) % CHUNKS
    own = source_ref[pl.ds(begin, rows)].reshape(shape)
    left = source_ref[pl.ds(begin - 1, rows)].reshape(shape)
    right = source_ref[pl.ds(begin + 1, rows)].reshape(shape)
    early = jnp.where(lane < 112, own, jnp.where(chunk == 0, 0.0, left))
    late = jnp.where(lane >= 16, own, jnp.where(chunk == CHUNKS - 1, 0.0, right))
    low = lane_index((pairs * 16, LANES)) < 64

    def turned(x, shift):
        return pltpu.roll(x.reshape(pairs * 16, LANES), shift, 1)

    early_a, early_b = turned(early[:, 0], 16), turned(early[:, 1], 80)
    late_a, late_b = turned(late[:, 0], 112), turned(late[:, 1], 48)
    tiles = (
        jnp.where(low, early_a, early_b),
        jnp.where(low, late_a, late_b),
        jnp.where(low, early_b, early_a),
        jnp.where(low, late_b, late_a),
    )
    for quarter, tile in enumerate(tiles):
        window_ref[quarter, pl.ds(first, pairs)] = tile.reshape(pairs, 16, LANES).astype(BF16)


def fan_terms(blocks, table_ref, pairs):
    rows = pairs * 16
    total = len(blocks) * rows
    parts = []
    for half in range(2):
        left = jnp.concatenate(
            [
                jnp.concatenate(
                    [ref[quarter, pl.ds(first + step, pairs)].reshape(rows, LANES) for step in range(8)],
                    axis=1,
                )
                for quarter in (2 * half, 2 * half + 1)
                for ref, first in blocks
            ],
            axis=0,
        )
        coherent = jnp.dot(left, table_ref[half], preferred_element_type=F32)
        parts += [coherent[:total], coherent[total:]]
    squares, cubes = [], []
    for part in parts:
        one, two = part[:, :LANES], part[:, LANES:]
        one_sq, two_sq = one * one, two * two
        squares.append(one_sq + two_sq)
        cubes.append(one_sq * one + two_sq * two)
    lane = lane_index((total, LANES))
    low = lane < 64
    even = (lane // 32) % 2 == 0

    def merged(s):
        s02, s20 = jnp.where(low, s[0], s[2]), jnp.where(low, s[2], s[0])
        s13, s31 = jnp.where(low, s[1], s[3]), jnp.where(low, s[3], s[1])
        a = jnp.where(even, s02, s13) + pltpu.roll(jnp.where(even, s20, s31), 64, 1)
        b = jnp.where(even, s13, s02) + pltpu.roll(jnp.where(even, s31, s20), 64, 1)
        return a, b

    square_a, square_b = merged(squares)
    cube_a, cube_b = merged(cubes)
    term_a = cube_a / (square_a + 1.0)
    term_b = cube_b / (square_b + 1.0)
    first_trace = jnp.where(even, term_a, pltpu.roll(term_b, 32, 1))
    second_trace = jnp.where(even, pltpu.roll(term_b, 96, 1), term_a)
    shape = (len(blocks) * pairs, 16, LANES)
    both = jnp.stack([first_trace.reshape(shape), second_trace.reshape(shape)], axis=1)
    both = both.reshape(len(blocks), 2 * pairs, 16, LANES)
    return [both[i] for i in range(len(blocks))]


def survey_kernel(
    shot_size,
    rline_size,
    traces_hbm,
    dest_hbm,
    fold_hbm,
    shot_taps_hbm,
    rcv_taps_hbm,
    out_ref,
    traces_ref,
    dest_ref,
    fold_ref,
    shot_taps_ref,
    rcv_taps_ref,
    taps_rows_ref,
    alive_ref,
    mask_ref,
    plain_ref,
    window_ref,
    shot_table_ref,
    rcv_table_ref,
    halo_out_ref,
    halo_in_ref,
    fold_own_ref,
    fold_all_ref,
    gain_ref,
    unpick_ref,
    sent_ref,
    held_ref,
    stack_ref,
    rcv_window_ref,
    back_ref,
    load_sem,
    halo_send,
    halo_recv,
    fold_send,
    fold_recv,
    out_send,
    out_recv,
    back_send,
    back_recv,
    own_sem,
):
    shot_dev, receivers = traces_ref.shape[0], traces_ref.shape[1]
    groups = shot_dev // 2
    share = receivers // shot_size
    peers = shot_size - 1
    shots = shot_size * shot_dev
    rows = shots * CHUNKS
    order = list(range(1, share - 1)) + [0, share - 1]
    cuts = [0, 4, 8, share - 2, share]
    portions = list(zip(cuts, cuts[1:]))
    me = lax.axis_index("shot")
    line = lax.axis_index("rline")
    has = (line > 0, line < rline_size - 1)
    beside = (jnp.maximum(line - 1, 0), jnp.minimum(line + 1, rline_size - 1))

    def peer(step):
        return lax.rem(me + 1 + step, shot_size)

    def source(step):
        return lax.rem(me + shot_size - 1 - step, shot_size)

    loads = [
        pltpu.make_async_copy(a, b, load_sem.at[i])
        for i, (a, b) in enumerate(
            [
                (shot_taps_hbm, shot_taps_ref),
                (rcv_taps_hbm, rcv_taps_ref),
                (dest_hbm, dest_ref),
                (fold_hbm, fold_ref),
            ]
            + [(traces_hbm.at[s], traces_ref.at[s]) for s in range(shot_dev)]
        )
    ]
    for load in loads:
        load.start()
    barrier = pltpu.get_barrier_semaphore()
    for step in range(peers):
        pl.semaphore_signal(barrier, inc=1, device_id={"shot": peer(step)}, device_id_type=MESH)
    for side in range(2):

        @pl.when(has[side])
        def _(side=side):
            pl.semaphore_signal(barrier, inc=1, device_id={"rline": beside[side]}, device_id_type=MESH)

    alive_ref[...] = jnp.zeros(alive_ref.shape, F32)
    fold_own_ref[...] = jnp.full(fold_own_ref.shape, -1, jnp.int32)
    loads[0].wait()
    build_table(shot_taps_ref, taps_rows_ref, shot_table_ref)
    loads[1].wait()
    build_table(rcv_taps_ref, taps_rows_ref, rcv_table_ref)
    loads[2].wait()
    alive_ref[0:shot_dev, 0:receivers] = (dest_ref[...] >= 0).astype(F32)
    pick_shot = lax.broadcasted_iota(jnp.int32, (8, shot_dev * LANES), 0) == (
        lax.broadcasted_iota(jnp.int32, (8, shot_dev * LANES), 1) // LANES
    )
    mask_ref[...] = lax.dot_general(
        alive_ref[...], pick_shot.astype(F32), (((0,), (0,)), ((), ())), preferred_element_type=F32
    )
    for s in range(shot_dev):
        loads[4 + s].wait()
        for i in range(receivers // 16):
            x = traces_ref[s, pl.ds(i * 16, 16)].astype(F32)
            for half in range(2):
                mask = mask_ref[i * 16 + half * 8 : i * 16 + half * 8 + 8, s * LANES : (s + 1) * LANES]
                begin = (i * 16 + half * 8 + RIM) * 16 + 8 + (s % 2) * CHUNKS
                for c in range(CHUNKS):
                    piece = x[half * 8 : half * 8 + 8, c * LANES : (c + 1) * LANES]
                    plain_ref[s // 2, pl.ds(begin + c, 8, stride=16)] = piece * mask

    for g in range(groups):
        for side, begin in enumerate((receivers - RIM, 0)):
            edge = plain_ref[g, (RIM + begin) * 16 + 8 : (2 * RIM + begin) * 16 + 8]
            halo_out_ref[side, g] = edge.astype(BF16).reshape(RIM, 16, LANES)
    loads[3].wait()
    fold_own_ref[0:shot_dev, 0:receivers] = fold_ref[...]

    span_pairs = (receivers + 2 * RIM) // 2
    edge_pairs = shot_size // 2
    inner = list(range(edge_pairs, span_pairs - edge_pairs, 5)) + [span_pairs - edge_pairs]
    for g in range(groups):
        for first, end in zip(inner, inner[1:]):
            fill_windows(plain_ref.at[g], window_ref.at[g], first, end - first)

    def halo(side):
        return pltpu.make_async_remote_copy(
            src_ref=halo_out_ref.at[side],
            dst_ref=halo_in_ref.at[side],
            send_sem=halo_send.at[side],
            recv_sem=halo_recv.at[side],
            device_id={"rline": beside[1 - side]},
            device_id_type=MESH,
        )

    def fold_copy(step, slot):
        return pltpu.make_async_remote_copy(
            src_ref=fold_own_ref,
            dst_ref=fold_all_ref.at[slot],
            send_sem=fold_send.at[step],
            recv_sem=fold_recv.at[step],
            device_id={"shot": peer(step)},
            device_id_type=MESH,
        )

    def out_copy(target, n, slot):
        part = pl.ds(portions[n][0], portions[n][1] - portions[n][0])
        return pltpu.make_async_remote_copy(
            src_ref=sent_ref.at[target, part],
            dst_ref=held_ref.at[slot, part],
            send_sem=out_send.at[target, n],
            recv_sem=out_recv.at[slot, n],
            device_id={"shot": target},
            device_id_type=MESH,
        )

    pl.semaphore_wait(barrier, peers + has[0].astype(jnp.int32) + has[1].astype(jnp.int32))
    for side in range(2):

        @pl.when(has[1 - side])
        def _(side=side):
            halo(side).start()
    for step in range(peers):
        fold_copy(step, me).start()
    fold_all_ref[me] = fold_own_ref[...]

    def shot_blocks(starts, pairs, n):
        blocks = [(window_ref.at[g], first) for first in starts for g in range(groups)]
        terms = fan_terms(blocks, shot_table_ref, pairs)
        for i, first in enumerate(starts):
            for g in range(groups):
                begin = (2 * first + RIM) * 16 + 8
                centre = plain_ref[g, begin : begin + pairs * 32].reshape(2 * pairs, 16, LANES)
                value = (centre - terms[i * groups + g]).astype(BF16)
                for m in range(2 * pairs):
                    row, target = divmod(2 * first + m, shot_size)
                    sent_ref[target, order.index(row), g] = value[m]
        for step in range(peers):
            out_copy(peer(step), n, me).start()

    for n, (begin, end) in enumerate(portions[:-1]):
        shot_blocks([order[begin] * shot_size // 2], (end - begin) * shot_size // 2, n)

    for side in range(2):
        land = (RIM + receivers) * 16 + 8 if side else 8

        @pl.when(has[side])
        def _(side=side, land=land):
            halo(side).wait_recv()
            for g in range(groups):
                edge = halo_in_ref[side, g].astype(F32).reshape(RIM * 16, LANES)
                plain_ref[g, land : land + RIM * 16] = edge

        @pl.when(jnp.logical_not(has[side]))
        def _(land=land):
            for g in range(groups):
                plain_ref[g, land : land + RIM * 16] = jnp.zeros((RIM * 16, LANES), F32)

    for g in range(groups):
        for first in (0, span_pairs - edge_pairs):
            fill_windows(plain_ref.at[g], window_ref.at[g], first, edge_pairs)
    shot_blocks([0, (receivers - shot_size) // 2], shot_size // 2, len(portions) - 1)
    held_ref[me] = sent_ref[me]

    for step in range(peers):
        fold_copy(step, source(step)).wait_recv()
    folds = fold_all_ref[...].reshape(shot_size * 8, LANES).astype(F32)
    place = lax.broadcasted_iota(jnp.int32, (16, LANES), 0)
    place = jnp.where(place < share - 2, place + 1, jnp.where(place == share - 2, 0, place))
    take = lax.broadcasted_iota(jnp.int32, (16, LANES), 1) == place * shot_size + me
    mine = lax.dot_general(
        take.astype(F32), folds, (((1,), (1,)), ((), ())), preferred_element_type=F32
    )
    entry = lax.broadcasted_iota(jnp.int32, (shot_size * 8, rows), 0)
    shot = lax.broadcasted_iota(jnp.int32, (shot_size * 8, rows), 1) // CHUNKS
    spread = ((entry // 8) * shot_dev + entry % 8 == shot) & (entry % 8 < shot_dev)
    spread = spread.astype(F32)
    labels = jnp.dot(mine, spread, preferred_element_type=F32)
    live = jnp.sum((labels >= 0.0).astype(F32), axis=1, keepdims=True) / CHUNKS
    gains = jnp.broadcast_to(jnp.sqrt(shots / live), (16, LANES))
    chunk = (lax.broadcasted_iota(jnp.int32, (16, rows), 1) % CHUNKS).astype(F32)
    labels = jnp.where(labels >= 0.0, labels * CHUNKS + chunk, -1.0)
    columns = lax.dot_general(spread, mine, (((0,), (1,)), ((), ())), preferred_element_type=F32)
    chunk = (lax.broadcasted_iota(jnp.int32, (rows, 16), 0) % CHUNKS).astype(F32)
    columns = jnp.where(columns >= 0.0, columns * CHUNKS + chunk, -1.0)
    down = lax.broadcasted_iota(jnp.int32, (rows, rows), 0).astype(F32)
    across = lax.broadcasted_iota(jnp.int32, (rows, rows), 1).astype(F32)
    for k in range(share):
        gain_ref[k] = jnp.broadcast_to(gains[k : k + 1], (CHUNKS, LANES))

    for slot in range(2):
        stack_ref[slot, 0 : RIM * 16 + 8] = jnp.zeros((RIM * 16 + 8, LANES), F32)
        end = (RIM + shots) * 16 + 8
        stack_ref[slot, end:] = jnp.zeros((stack_ref.shape[1] - end, LANES), F32)

    def parts(pair):
        one, two = order[2 * pair], order[2 * pair + 1]
        return [(0, one, 2)] if two == one + 1 else [(0, one, 1), (1, two, 1)]

    def back_copies(pair, step, owner):
        return [
            pltpu.make_async_remote_copy(
                src_ref=back_ref.at[pair, peer(step), pl.ds(at, count)],
                dst_ref=out_ref.at[pl.ds(row, count), owner],
                send_sem=back_send.at[pair + at, step],
                recv_sem=back_recv.at[pair + at, step],
                device_id={"shot": peer(step)},
                device_id_type=MESH,
            )
            for at, row, count in parts(pair)
        ]

    def back_own(pair):
        return [
            pltpu.make_async_copy(
                back_ref.at[pair, me, pl.ds(at, count)], out_ref.at[pl.ds(row, count), me], own_sem.at[pair + at]
            )
            for at, row, count in parts(pair)
        ]

    def prepare(pair):
        slot = pair % 2
        for side in range(2):
            k = 2 * pair + side
            x = held_ref[:, k].reshape(rows, LANES)
            pick = jnp.where(labels[k : k + 1] == down, 1.0, 0.0).astype(BF16)
            unpick_ref[k] = jnp.where(columns[:, k : k + 1] == across, 1.0, 0.0).astype(BF16)
            stack = jnp.dot(pick, x, preferred_element_type=F32)
            for p in range(shots):
                begin = (RIM + p) * 16 + 8 + side * CHUNKS
                stack_ref[slot, begin : begin + CHUNKS] = stack[p * CHUNKS : (p + 1) * CHUNKS]
        for i in range(4):
            fill_windows(stack_ref.at[slot], rcv_window_ref.at[slot], i * 6, 6)

    def finish(pair):
        slot = pair % 2
        (terms,) = fan_terms([(rcv_window_ref.at[slot], 0)], rcv_table_ref, shots // 2)
        begin = RIM * 16 + 8
        value = stack_ref[slot, begin : begin + shots * 16].reshape(shots, 16, LANES) - terms
        for side in range(2):
            k = 2 * pair + side
            own = value[:, side * CHUNKS : (side + 1) * CHUNKS] * gain_ref[k][None]
            back = jnp.dot(
                unpick_ref[k], own.reshape(rows, LANES).astype(BF16), preferred_element_type=F32
            )
            back_ref[pair, :, side] = back.astype(BF16).reshape(shot_size, groups, 16, LANES)
        for step in range(peers):
            for copy in back_copies(pair, step, me):
                copy.start()
        for copy in back_own(pair):
            copy.start()

    def arrive(n):
        for step in range(peers):
            out_copy(peer(step), n, source(step)).wait_recv()

    pairs = share // 2
    arrive(0)
    prepare(0)
    for pair in range(pairs):
        if pair + 1 < pairs:
            for n, (begin, _) in enumerate(portions):
                if begin == 2 * (pair + 1):
                    arrive(n)
            prepare(pair + 1)
        finish(pair)

    for side in range(2):

        @pl.when(has[1 - side])
        def _(side=side):
            halo(side).wait_send()

    for step in range(peers):
        fold_copy(step, me).wait_send()
        for n in range(len(portions)):
            out_copy(peer(step), n, me).wait_send()
    for pair in range(pairs):
        for copy in back_own(pair):
            copy.wait()
        for step in range(peers):
            for copy in back_copies(pair, step, me):
                copy.wait_send()
            for copy in back_copies(pair, step, source(step)):
                copy.wait_recv()


def shards(traces, kernels_shot, kernels_rcv, dest, gather, fold, counts):
    shot_dev, rcv_dev, samples = traces.shape
    shot_size = lax.axis_size("shot")
    rline_size = lax.axis_size("rline")
    shots = shot_dev * shot_size
    share = rcv_dev // shot_size
    rows = shots * CHUNKS
    groups = shot_dev // 2
    peers = shot_size - 1
    pairs = share // 2
    span = rcv_dev + 2 * RIM
    fans, trace_taps, sample_taps = kernels_shot.shape
    dma = pltpu.SemaphoreType.DMA
    vmem = pltpu.VMEM
    returned = pl.pallas_call(
        functools.partial(survey_kernel, shot_size, rline_size),
        out_shape=jax.ShapeDtypeStruct((share, shot_size, groups, 16, LANES), BF16),
        in_specs=[pl.BlockSpec(memory_space=pltpu.HBM)] * 5,
        out_specs=pl.BlockSpec(memory_space=pltpu.HBM),
        scratch_shapes=[
            vmem(traces.shape, BF16),
            vmem(dest.shape, jnp.int32),
            vmem(fold.shape, jnp.int32),
            vmem((trace_taps, fans, sample_taps), BF16),
            vmem((trace_taps, fans, sample_taps), BF16),
            vmem((LANES, LANES), F32),
            vmem((8, LANES), F32),
            vmem((LANES, shot_dev * LANES), F32),
            vmem((groups, span * 16 + 16, LANES), F32),
            vmem((groups, 4, span // 2, 16, LANES), BF16),
            vmem((2, 1024, 256), BF16),
            vmem((2, 1024, 256), BF16),
            vmem((2, groups, RIM, 16, LANES), BF16),
            vmem((2, groups, RIM, 16, LANES), BF16),
            vmem((8, LANES), jnp.int32),
            vmem((shot_size, 8, LANES), jnp.int32),
            vmem((share, CHUNKS, LANES), F32),
            vmem((share, rows, rows), BF16),
            vmem((shot_size, share, groups, 16, LANES), BF16),
            vmem((shot_size, share, groups, 16, LANES), BF16),
            vmem((2, (shots + 16) * 16 + 16, LANES), F32),
            vmem((2, 4, shots // 2 + 8, 16, LANES), BF16),
            vmem((pairs, shot_size, 2, groups, 16, LANES), BF16),
            dma((4 + shot_dev,)),
            dma((2,)),
            dma((2,)),
            dma((peers,)),
            dma((peers,)),
            dma((shot_size, 4)),
            dma((shot_size, 4)),
            dma((pairs + 1, peers)),
            dma((pairs + 1, peers)),
            dma((pairs + 1,)),
        ],
        compiler_params=pltpu.CompilerParams(
            vmem_limit_bytes=61 << 20, collective_id=0, has_side_effects=True
        ),
        cost_estimate=pl.CostEstimate(flops=7 * 10**9, bytes_accessed=4 * 10**6, transcendentals=0),
    )(traces, dest, fold, kernels_shot.transpose(1, 0, 2), kernels_rcv.transpose(1, 0, 2))
    result = returned.reshape(rcv_dev, shot_dev, CHUNKS, LANES).transpose(1, 0, 2, 3)
    return result.reshape(shot_dev, rcv_dev, samples).astype(F32)


def solution(mesh):
    in_specs = (
        P("shot", "rline", None),
        P(),
        P(),
        P("shot", "rline"),
        P("shot", "rline"),
        P("shot", "rline"),
        P(("shot", "rline")),
    )
    out_specs = P("shot", "rline", None)
    return jax.shard_map(shards, mesh=mesh, in_specs=in_specs, out_specs=out_specs, check_vma=False)
```

```python
import functools

import jax
import jax.numpy as jnp
from jax import lax
from jax.experimental import pallas as pl
from jax.experimental.pallas import tpu as pltpu
from jax.sharding import PartitionSpec as P

LANES = 128
CHUNKS = 8
BF16 = jnp.bfloat16
F32 = jnp.float32
RIM = 7
MESH = pl.DeviceIdType.MESH


def lane_index(shape):
    return lax.broadcasted_iota(jnp.int32, shape, len(shape) - 1)


def build_table(kernel_ref, rows_ref, table_ref):
    reach, fans, taps = kernel_ref.shape
    rows_ref[...] = jnp.zeros(rows_ref.shape, F32)
    for step in range(reach):
        rows_ref[step * 8 : step * 8 + fans, 0:taps] = kernel_ref[step].astype(F32)
    tap = lax.broadcasted_iota(jnp.int32, (LANES, LANES), 0)
    lane = lax.broadcasted_iota(jnp.int32, (LANES, LANES), 1)
    flat = rows_ref[...].astype(BF16)
    low = jnp.dot(flat, (lane == LANES - 1 - tap).astype(BF16), preferred_element_type=F32)
    high = jnp.dot(flat, (lane == LANES // 2 - 1 - tap).astype(BF16), preferred_element_type=F32)
    even = (lane_index((64, LANES)) // 32) % 2 == 0
    for half in range(2):
        before = jnp.zeros((64, LANES), F32)
        columns = slice(half * LANES, (half + 1) * LANES)
        for step in range(16):
            if step < reach:
                at = step * 8 + 2 * half
                row = jnp.broadcast_to(low[at : at + 1] + high[at + 1 : at + 2], (64, LANES))
                here = pltpu.roll(row, 0, 1, stride=1, stride_axis=0)
            else:
                here = jnp.zeros((64, LANES), F32)
            block = jnp.where(even, here, pltpu.roll(before, 32, 1)).astype(BF16)
            table_ref[0, step * 64 : (step + 1) * 64, columns] = block
            other = step + 1 if step % 2 == 0 else step - 1
            table_ref[1, other * 64 : (other + 1) * 64, columns] = block
            before = here


def fill_windows(source_ref, window_ref, first, pairs):
    rows = pairs * 32
    begin = first * 32 + 8
    shape = (pairs, 2, 16, LANES)
    lane = lane_index(shape)
    chunk = lax.broadcasted_iota(jnp.int32, shape, 2) % CHUNKS
    own = source_ref[pl.ds(begin, rows)].reshape(shape)
    left = source_ref[pl.ds(begin - 1, rows)].reshape(shape)
    right = source_ref[pl.ds(begin + 1, rows)].reshape(shape)
    early = jnp.where(lane < 112, own, jnp.where(chunk == 0, 0.0, left))
    late = jnp.where(lane >= 16, own, jnp.where(chunk == CHUNKS - 1, 0.0, right))
    low = lane_index((pairs * 16, LANES)) < 64

    def turned(x, shift):
        return pltpu.roll(x.reshape(pairs * 16, LANES), shift, 1)

    early_a, early_b = turned(early[:, 0], 16), turned(early[:, 1], 80)
    late_a, late_b = turned(late[:, 0], 112), turned(late[:, 1], 48)
    tiles = (
        jnp.where(low, early_a, early_b),
        jnp.where(low, late_a, late_b),
        jnp.where(low, early_b, early_a),
        jnp.where(low, late_b, late_a),
    )
    for quarter, tile in enumerate(tiles):
        window_ref[quarter, pl.ds(first, pairs)] = tile.reshape(pairs, 16, LANES).astype(BF16)


def fan_terms(blocks, table_ref, pairs):
    rows = pairs * 16
    total = len(blocks) * rows
    parts = []
    for half in range(2):
        left = jnp.concatenate(
            [
                jnp.concatenate(
                    [ref[quarter, pl.ds(first + step, pairs)].reshape(rows, LANES) for step in range(8)],
                    axis=1,
                )
                for quarter in (2 * half, 2 * half + 1)
                for ref, first in blocks
            ],
            axis=0,
        )
        coherent = jnp.dot(left, table_ref[half], preferred_element_type=F32)
        parts += [coherent[:total], coherent[total:]]
    squares, cubes = [], []
    for part in parts:
        one, two = part[:, :LANES], part[:, LANES:]
        one_sq, two_sq = one * one, two * two
        squares.append(one_sq + two_sq)
        cubes.append(one_sq * one + two_sq * two)
    lane = lane_index((total, LANES))
    low = lane < 64
    even = (lane // 32) % 2 == 0

    def merged(s):
        s02, s20 = jnp.where(low, s[0], s[2]), jnp.where(low, s[2], s[0])
        s13, s31 = jnp.where(low, s[1], s[3]), jnp.where(low, s[3], s[1])
        a = jnp.where(even, s02, s13) + pltpu.roll(jnp.where(even, s20, s31), 64, 1)
        b = jnp.where(even, s13, s02) + pltpu.roll(jnp.where(even, s31, s20), 64, 1)
        return a, b

    square_a, square_b = merged(squares)
    cube_a, cube_b = merged(cubes)
    term_a = cube_a / (square_a + 1.0)
    term_b = cube_b / (square_b + 1.0)
    first_trace = jnp.where(even, term_a, pltpu.roll(term_b, 32, 1))
    second_trace = jnp.where(even, pltpu.roll(term_b, 96, 1), term_a)
    shape = (len(blocks) * pairs, 16, LANES)
    both = jnp.stack([first_trace.reshape(shape), second_trace.reshape(shape)], axis=1)
    both = both.reshape(len(blocks), 2 * pairs, 16, LANES)
    return [both[i] for i in range(len(blocks))]


def survey_kernel(
    shot_size,
    rline_size,
    traces_hbm,
    dest_hbm,
    fold_hbm,
    shot_taps_hbm,
    rcv_taps_hbm,
    out_ref,
    traces_ref,
    dest_ref,
    fold_ref,
    shot_taps_ref,
    rcv_taps_ref,
    taps_rows_ref,
    alive_ref,
    mask_ref,
    plain_ref,
    window_ref,
    shot_table_ref,
    rcv_table_ref,
    halo_out_ref,
    halo_in_ref,
    fold_own_ref,
    fold_all_ref,
    gain_ref,
    unpick_ref,
    sent_ref,
    held_ref,
    stack_ref,
    rcv_window_ref,
    back_ref,
    load_sem,
    halo_send,
    halo_recv,
    fold_send,
    fold_recv,
    out_send,
    out_recv,
    back_send,
    back_recv,
    own_sem,
):
    shot_dev, receivers = traces_ref.shape[0], traces_ref.shape[1]
    groups = shot_dev // 2
    share = receivers // shot_size
    peers = shot_size - 1
    shots = shot_size * shot_dev
    rows = shots * CHUNKS
    order = list(range(1, share - 1)) + [0, share - 1]
    cuts = [0, 4, 8, share - 2, share]
    portions = list(zip(cuts, cuts[1:]))
    me = lax.axis_index("shot")
    line = lax.axis_index("rline")
    has = (line > 0, line < rline_size - 1)
    beside = (jnp.maximum(line - 1, 0), jnp.minimum(line + 1, rline_size - 1))

    def peer(step):
        return lax.rem(me + 1 + step, shot_size)

    def source(step):
        return lax.rem(me + shot_size - 1 - step, shot_size)

    loads = [
        pltpu.make_async_copy(a, b, load_sem.at[i])
        for i, (a, b) in enumerate(
            [
                (shot_taps_hbm, shot_taps_ref),
                (rcv_taps_hbm, rcv_taps_ref),
                (dest_hbm, dest_ref),
                (fold_hbm, fold_ref),
            ]
            + [(traces_hbm.at[s], traces_ref.at[s]) for s in range(shot_dev)]
        )
    ]
    for load in loads:
        load.start()
    barrier = pltpu.get_barrier_semaphore()
    for step in range(peers):
        pl.semaphore_signal(barrier, inc=1, device_id={"shot": peer(step)}, device_id_type=MESH)
    for side in range(2):

        @pl.when(has[side])
        def _(side=side):
            pl.semaphore_signal(barrier, inc=1, device_id={"rline": beside[side]}, device_id_type=MESH)

    alive_ref[...] = jnp.zeros(alive_ref.shape, F32)
    fold_own_ref[...] = jnp.full(fold_own_ref.shape, -1, jnp.int32)
    loads[0].wait()
    build_table(shot_taps_ref, taps_rows_ref, shot_table_ref)
    loads[1].wait()
    build_table(rcv_taps_ref, taps_rows_ref, rcv_table_ref)
    loads[2].wait()
    alive_ref[0:shot_dev, 0:receivers] = (dest_ref[...] >= 0).astype(F32)
    pick_shot = lax.broadcasted_iota(jnp.int32, (8, shot_dev * LANES), 0) == (
        lax.broadcasted_iota(jnp.int32, (8, shot_dev * LANES), 1) // LANES
    )
    mask_ref[...] = lax.dot_general(
        alive_ref[...], pick_shot.astype(F32), (((0,), (0,)), ((), ())), preferred_element_type=F32
    )
    for s in range(shot_dev):
        loads[4 + s].wait()
        for i in range(receivers // 16):
            x = traces_ref[s, pl.ds(i * 16, 16)].astype(F32)
            for half in range(2):
                mask = mask_ref[i * 16 + half * 8 : i * 16 + half * 8 + 8, s * LANES : (s + 1) * LANES]
                begin = (i * 16 + half * 8 + RIM) * 16 + 8 + (s % 2) * CHUNKS
                for c in range(CHUNKS):
                    piece = x[half * 8 : half * 8 + 8, c * LANES : (c + 1) * LANES]
                    plain_ref[s // 2, pl.ds(begin + c, 8, stride=16)] = piece * mask

    for g in range(groups):
        for side, begin in enumerate((receivers - RIM, 0)):
            edge = plain_ref[g, (RIM + begin) * 16 + 8 : (2 * RIM + begin) * 16 + 8]
            halo_out_ref[side, g] = edge.astype(BF16).reshape(RIM, 16, LANES)
    loads[3].wait()
    fold_own_ref[0:shot_dev, 0:receivers] = fold_ref[...]

    span_pairs = (receivers + 2 * RIM) // 2
    edge_pairs = shot_size // 2
    inner = list(range(edge_pairs, span_pairs - edge_pairs, 5)) + [span_pairs - edge_pairs]
    for g in range(groups):
        for first, end in zip(inner, inner[1:]):
            fill_windows(plain_ref.at[g], window_ref.at[g], first, end - first)

    def halo(side):
        return pltpu.make_async_remote_copy(
            src_ref=halo_out_ref.at[side],
            dst_ref=halo_in_ref.at[side],
            send_sem=halo_send.at[side],
            recv_sem=halo_recv.at[side],
            device_id={"rline": beside[1 - side]},
            device_id_type=MESH,
        )

    def fold_copy(step, slot):
        return pltpu.make_async_remote_copy(
            src_ref=fold_own_ref,
            dst_ref=fold_all_ref.at[slot],
            send_sem=fold_send.at[step],
            recv_sem=fold_recv.at[step],
            device_id={"shot": peer(step)},
            device_id_type=MESH,
        )

    def out_copy(target, n, slot):
        part = pl.ds(portions[n][0], portions[n][1] - portions[n][0])
        return pltpu.make_async_remote_copy(
            src_ref=sent_ref.at[target, part],
            dst_ref=held_ref.at[slot, part],
            send_sem=out_send.at[target, n],
            recv_sem=out_recv.at[slot, n],
            device_id={"shot": target},
            device_id_type=MESH,
        )

    def shot_blocks(starts, pairs):
        blocks = [(window_ref.at[g], first) for first in starts for g in range(groups)]
        terms = fan_terms(blocks, shot_table_ref, pairs)
        for i, first in enumerate(starts):
            for g in range(groups):
                begin = (2 * first + RIM) * 16 + 8
                centre = plain_ref[g, begin : begin + pairs * 32].reshape(2 * pairs, 16, LANES)
                value = (centre - terms[i * groups + g]).astype(BF16)
                for m in range(2 * pairs):
                    row, target = divmod(2 * first + m, shot_size)
                    sent_ref[target, order.index(row), g] = value[m]

    def send_out(n):
        for step in range(peers):
            out_copy(peer(step), n, me).start()

    def inner_blocks(n):
        begin, end = portions[n]
        shot_blocks([order[begin] * shot_size // 2], (end - begin) * shot_size // 2)

    inner_blocks(0)
    pl.semaphore_wait(barrier, peers + has[0].astype(jnp.int32) + has[1].astype(jnp.int32))
    for side in range(2):

        @pl.when(has[1 - side])
        def _(side=side):
            halo(side).start()
    for step in range(peers):
        fold_copy(step, me).start()
    fold_all_ref[me] = fold_own_ref[...]

    for n in range(len(portions) - 1):
        if n > 0:
            inner_blocks(n)
        send_out(n)

    for side in range(2):
        land = (RIM + receivers) * 16 + 8 if side else 8

        @pl.when(has[side])
        def _(side=side, land=land):
            halo(side).wait_recv()
            for g in range(groups):
                edge = halo_in_ref[side, g].astype(F32).reshape(RIM * 16, LANES)
                plain_ref[g, land : land + RIM * 16] = edge

        @pl.when(jnp.logical_not(has[side]))
        def _(land=land):
            for g in range(groups):
                plain_ref[g, land : land + RIM * 16] = jnp.zeros((RIM * 16, LANES), F32)

    for g in range(groups):
        for first in (0, span_pairs - edge_pairs):
            fill_windows(plain_ref.at[g], window_ref.at[g], first, edge_pairs)
    shot_blocks([0, (receivers - shot_size) // 2], shot_size // 2)
    send_out(len(portions) - 1)
    held_ref[me] = sent_ref[me]

    for step in range(peers):
        fold_copy(step, source(step)).wait_recv()
    folds = fold_all_ref[...].reshape(shot_size * 8, LANES).astype(F32)
    place = lax.broadcasted_iota(jnp.int32, (16, LANES), 0)
    place = jnp.where(place < share - 2, place + 1, jnp.where(place == share - 2, 0, place))
    take = lax.broadcasted_iota(jnp.int32, (16, LANES), 1) == place * shot_size + me
    mine = lax.dot_general(
        take.astype(F32), folds, (((1,), (1,)), ((), ())), preferred_element_type=F32
    )
    entry = lax.broadcasted_iota(jnp.int32, (shot_size * 8, rows), 0)
    shot = lax.broadcasted_iota(jnp.int32, (shot_size * 8, rows), 1) // CHUNKS
    spread = ((entry // 8) * shot_dev + entry % 8 == shot) & (entry % 8 < shot_dev)
    spread = spread.astype(F32)
    labels = jnp.dot(mine, spread, preferred_element_type=F32)
    live = jnp.sum((labels >= 0.0).astype(F32), axis=1, keepdims=True) / CHUNKS
    gains = jnp.broadcast_to(jnp.sqrt(shots / live), (16, LANES))
    chunk = (lax.broadcasted_iota(jnp.int32, (16, rows), 1) % CHUNKS).astype(F32)
    labels = jnp.where(labels >= 0.0, labels * CHUNKS + chunk, -1.0)
    columns = lax.dot_general(spread, mine, (((0,), (1,)), ((), ())), preferred_element_type=F32)
    chunk = (lax.broadcasted_iota(jnp.int32, (rows, 16), 0) % CHUNKS).astype(F32)
    columns = jnp.where(columns >= 0.0, columns * CHUNKS + chunk, -1.0)
    down = lax.broadcasted_iota(jnp.int32, (rows, rows), 0).astype(F32)
    across = lax.broadcasted_iota(jnp.int32, (rows, rows), 1).astype(F32)
    for k in range(share):
        gain_ref[k] = jnp.broadcast_to(gains[k : k + 1], (CHUNKS, LANES))

    for slot in range(2):
        stack_ref[slot, 0 : RIM * 16 + 8] = jnp.zeros((RIM * 16 + 8, LANES), F32)
        end = (RIM + shots) * 16 + 8
        stack_ref[slot, end:] = jnp.zeros((stack_ref.shape[1] - end, LANES), F32)

    def parts(pair):
        one, two = order[2 * pair], order[2 * pair + 1]
        return [(0, one, 2)] if two == one + 1 else [(0, one, 1), (1, two, 1)]

    def back_copies(pair, step, owner):
        return [
            pltpu.make_async_remote_copy(
                src_ref=back_ref.at[pair, peer(step), :, pl.ds(at, count)],
                dst_ref=out_ref.at[:, pl.ds(row, count), owner],
                send_sem=back_send.at[pair + at, step],
                recv_sem=back_recv.at[pair + at, step],
                device_id={"shot": peer(step)},
                device_id_type=MESH,
            )
            for at, row, count in parts(pair)
        ]

    def back_own(pair):
        return [
            pltpu.make_async_copy(
                back_ref.at[pair, me, :, pl.ds(at, count)],
                out_ref.at[:, pl.ds(row, count), me],
                own_sem.at[pair + at],
            )
            for at, row, count in parts(pair)
        ]

    def prepare(pair):
        slot = pair % 2
        for side in range(2):
            k = 2 * pair + side
            x = held_ref[:, k].reshape(rows, LANES)
            pick = jnp.where(labels[k : k + 1] == down, 1.0, 0.0).astype(BF16)
            unpick_ref[k] = jnp.where(columns[:, k : k + 1] == across, 1.0, 0.0).astype(BF16)
            stack = jnp.dot(pick, x, preferred_element_type=F32)
            for p in range(shots):
                begin = (RIM + p) * 16 + 8 + side * CHUNKS
                stack_ref[slot, begin : begin + CHUNKS] = stack[p * CHUNKS : (p + 1) * CHUNKS]
        for i in range(4):
            fill_windows(stack_ref.at[slot], rcv_window_ref.at[slot], i * 6, 6)

    def finish(pair):
        slot = pair % 2
        (terms,) = fan_terms([(rcv_window_ref.at[slot], 0)], rcv_table_ref, shots // 2)
        begin = RIM * 16 + 8
        value = stack_ref[slot, begin : begin + shots * 16].reshape(shots, 16, LANES) - terms
        for side in range(2):
            k = 2 * pair + side
            own = value[:, side * CHUNKS : (side + 1) * CHUNKS] * gain_ref[k][None]
            back = jnp.dot(
                unpick_ref[k], own.reshape(rows, LANES).astype(BF16), preferred_element_type=F32
            )
            back_ref[pair, :, :, side] = back.astype(BF16).reshape(shot_size, groups, 16, LANES)
        for step in range(peers):
            for copy in back_copies(pair, step, me):
                copy.start()
        for copy in back_own(pair):
            copy.start()

    def arrive(n):
        for step in range(peers):
            out_copy(peer(step), n, source(step)).wait_recv()

    pairs = share // 2
    arrive(0)
    prepare(0)
    for pair in range(pairs):
        if pair + 1 < pairs:
            for n, (begin, _) in enumerate(portions):
                if begin == 2 * (pair + 1):
                    arrive(n)
            prepare(pair + 1)
        finish(pair)

    for side in range(2):

        @pl.when(has[1 - side])
        def _(side=side):
            halo(side).wait_send()

    for step in range(peers):
        fold_copy(step, me).wait_send()
        for n in range(len(portions)):
            out_copy(peer(step), n, me).wait_send()
    for pair in range(pairs):
        for copy in back_own(pair):
            copy.wait()
        for step in range(peers):
            for copy in back_copies(pair, step, me):
                copy.wait_send()
            for copy in back_copies(pair, step, source(step)):
                copy.wait_recv()


def shards(traces, kernels_shot, kernels_rcv, dest, gather, fold, counts):
    shot_dev, rcv_dev, samples = traces.shape
    shot_size = lax.axis_size("shot")
    rline_size = lax.axis_size("rline")
    shots = shot_dev * shot_size
    share = rcv_dev // shot_size
    rows = shots * CHUNKS
    groups = shot_dev // 2
    peers = shot_size - 1
    pairs = share // 2
    span = rcv_dev + 2 * RIM
    fans, trace_taps, sample_taps = kernels_shot.shape
    dma = pltpu.SemaphoreType.DMA
    vmem = pltpu.VMEM
    returned = pl.pallas_call(
        functools.partial(survey_kernel, shot_size, rline_size),
        out_shape=jax.ShapeDtypeStruct((groups, share, shot_size, 16, LANES), BF16),
        in_specs=[pl.BlockSpec(memory_space=pltpu.HBM)] * 5,
        out_specs=pl.BlockSpec(memory_space=pltpu.HBM),
        scratch_shapes=[
            vmem(traces.shape, BF16),
            vmem(dest.shape, jnp.int32),
            vmem(fold.shape, jnp.int32),
            vmem((trace_taps, fans, sample_taps), BF16),
            vmem((trace_taps, fans, sample_taps), BF16),
            vmem((LANES, LANES), F32),
            vmem((8, LANES), F32),
            vmem((LANES, shot_dev * LANES), F32),
            vmem((groups, span * 16 + 16, LANES), F32),
            vmem((groups, 4, span // 2, 16, LANES), BF16),
            vmem((2, 1024, 256), BF16),
            vmem((2, 1024, 256), BF16),
            vmem((2, groups, RIM, 16, LANES), BF16),
            vmem((2, groups, RIM, 16, LANES), BF16),
            vmem((8, LANES), jnp.int32),
            vmem((shot_size, 8, LANES), jnp.int32),
            vmem((share, CHUNKS, LANES), F32),
            vmem((share, rows, rows), BF16),
            vmem((shot_size, share, groups, 16, LANES), BF16),
            vmem((shot_size, share, groups, 16, LANES), BF16),
            vmem((2, (shots + 16) * 16 + 16, LANES), F32),
            vmem((2, 4, shots // 2 + 8, 16, LANES), BF16),
            vmem((pairs, shot_size, groups, 2, 16, LANES), BF16),
            dma((4 + shot_dev,)),
            dma((2,)),
            dma((2,)),
            dma((peers,)),
            dma((peers,)),
            dma((shot_size, 4)),
            dma((shot_size, 4)),
            dma((pairs + 1, peers)),
            dma((pairs + 1, peers)),
            dma((pairs + 1,)),
        ],
        compiler_params=pltpu.CompilerParams(
            vmem_limit_bytes=61 << 20, collective_id=0, has_side_effects=True
        ),
        cost_estimate=pl.CostEstimate(flops=7 * 10**9, bytes_accessed=4 * 10**6, transcendentals=0),
    )(traces, dest, fold, kernels_shot.transpose(1, 0, 2), kernels_rcv.transpose(1, 0, 2))
    result = returned.reshape(groups, rcv_dev, 2, CHUNKS, LANES).transpose(0, 2, 1, 3, 4)
    return result.reshape(shot_dev, rcv_dev, samples).astype(F32)


def solution(mesh):
    in_specs = (
        P("shot", "rline", None),
        P(),
        P(),
        P("shot", "rline"),
        P("shot", "rline"),
        P("shot", "rline"),
        P(("shot", "rline")),
    )
    out_specs = P("shot", "rline", None)
    return jax.shard_map(shards, mesh=mesh, in_specs=in_specs, out_specs=out_specs, check_vma=False)
```

```python
import functools

import jax
import jax.numpy as jnp
from jax import lax
from jax.experimental import pallas as pl
from jax.experimental.pallas import tpu as pltpu
from jax.sharding import PartitionSpec as P

LANES = 128
CHUNKS = 8
BF16 = jnp.bfloat16
F32 = jnp.float32
RIM = 7
MESH = pl.DeviceIdType.MESH


def lane_index(shape):
    return lax.broadcasted_iota(jnp.int32, shape, len(shape) - 1)


def build_table(kernel_ref, rows_ref, table_ref):
    reach, fans, taps = kernel_ref.shape
    rows_ref[...] = jnp.zeros(rows_ref.shape, F32)
    for step in range(reach):
        rows_ref[step * 8 : step * 8 + fans, 0:taps] = kernel_ref[step].astype(F32)
    tap = lax.broadcasted_iota(jnp.int32, (LANES, LANES), 0)
    lane = lax.broadcasted_iota(jnp.int32, (LANES, LANES), 1)
    flat = rows_ref[...].astype(BF16)
    low = jnp.dot(flat, (lane == LANES - 1 - tap).astype(BF16), preferred_element_type=F32)
    high = jnp.dot(flat, (lane == LANES // 2 - 1 - tap).astype(BF16), preferred_element_type=F32)
    even = (lane_index((64, LANES)) // 32) % 2 == 0
    for half in range(2):
        before = jnp.zeros((64, LANES), F32)
        columns = slice(half * LANES, (half + 1) * LANES)
        for step in range(16):
            if step < reach:
                at = step * 8 + 2 * half
                row = jnp.broadcast_to(low[at : at + 1] + high[at + 1 : at + 2], (64, LANES))
                here = pltpu.roll(row, 0, 1, stride=1, stride_axis=0)
            else:
                here = jnp.zeros((64, LANES), F32)
            block = jnp.where(even, here, pltpu.roll(before, 32, 1)).astype(BF16)
            table_ref[0, step * 64 : (step + 1) * 64, columns] = block
            other = step + 1 if step % 2 == 0 else step - 1
            table_ref[1, other * 64 : (other + 1) * 64, columns] = block
            before = here


def fill_windows(source_ref, window_ref, first, pairs):
    rows = pairs * 32
    begin = first * 32 + 8
    shape = (pairs, 2, 16, LANES)
    lane = lane_index(shape)
    chunk = lax.broadcasted_iota(jnp.int32, shape, 2) % CHUNKS
    own = source_ref[pl.ds(begin, rows)].reshape(shape)
    left = source_ref[pl.ds(begin - 1, rows)].reshape(shape)
    right = source_ref[pl.ds(begin + 1, rows)].reshape(shape)
    early = jnp.where(lane < 112, own, jnp.where(chunk == 0, 0.0, left))
    late = jnp.where(lane >= 16, own, jnp.where(chunk == CHUNKS - 1, 0.0, right))
    low = lane_index((pairs * 16, LANES)) < 64

    def turned(x, shift):
        return pltpu.roll(x.reshape(pairs * 16, LANES), shift, 1)

    early_a, early_b = turned(early[:, 0], 16), turned(early[:, 1], 80)
    late_a, late_b = turned(late[:, 0], 112), turned(late[:, 1], 48)
    tiles = (
        jnp.where(low, early_a, early_b),
        jnp.where(low, late_a, late_b),
        jnp.where(low, early_b, early_a),
        jnp.where(low, late_b, late_a),
    )
    for quarter, tile in enumerate(tiles):
        window_ref[quarter, pl.ds(first, pairs)] = tile.reshape(pairs, 16, LANES).astype(BF16)


def fan_terms(blocks, table_ref, pairs):
    rows = pairs * 16
    total = len(blocks) * rows
    parts = []
    for half in range(2):
        left = jnp.concatenate(
            [
                jnp.concatenate(
                    [ref[quarter, pl.ds(first + step, pairs)].reshape(rows, LANES) for step in range(8)],
                    axis=1,
                )
                for quarter in (2 * half, 2 * half + 1)
                for ref, first in blocks
            ],
            axis=0,
        )
        coherent = jnp.dot(left, table_ref[half], preferred_element_type=F32)
        parts += [coherent[:total], coherent[total:]]
    squares, cubes = [], []
    for part in parts:
        one, two = part[:, :LANES], part[:, LANES:]
        one_sq, two_sq = one * one, two * two
        squares.append(one_sq + two_sq)
        cubes.append(one_sq * one + two_sq * two)
    lane = lane_index((total, LANES))
    low = lane < 64
    even = (lane // 32) % 2 == 0

    def merged(s):
        s02, s20 = jnp.where(low, s[0], s[2]), jnp.where(low, s[2], s[0])
        s13, s31 = jnp.where(low, s[1], s[3]), jnp.where(low, s[3], s[1])
        a = jnp.where(even, s02, s13) + pltpu.roll(jnp.where(even, s20, s31), 64, 1)
        b = jnp.where(even, s13, s02) + pltpu.roll(jnp.where(even, s31, s20), 64, 1)
        return a, b

    square_a, square_b = merged(squares)
    cube_a, cube_b = merged(cubes)
    term_a = cube_a / (square_a + 1.0)
    term_b = cube_b / (square_b + 1.0)
    first_trace = jnp.where(even, term_a, pltpu.roll(term_b, 32, 1))
    second_trace = jnp.where(even, pltpu.roll(term_b, 96, 1), term_a)
    shape = (len(blocks) * pairs, 16, LANES)
    both = jnp.stack([first_trace.reshape(shape), second_trace.reshape(shape)], axis=1)
    both = both.reshape(len(blocks), 2 * pairs, 16, LANES)
    return [both[i] for i in range(len(blocks))]


def survey_kernel(
    shot_size,
    rline_size,
    traces_hbm,
    dest_hbm,
    fold_hbm,
    shot_taps_hbm,
    rcv_taps_hbm,
    out_ref,
    traces_ref,
    dest_ref,
    fold_ref,
    shot_taps_ref,
    rcv_taps_ref,
    taps_rows_ref,
    alive_ref,
    mask_ref,
    plain_ref,
    window_ref,
    shot_table_ref,
    rcv_table_ref,
    halo_out_ref,
    halo_in_ref,
    fold_own_ref,
    fold_all_ref,
    gain_ref,
    unpick_ref,
    sent_ref,
    held_ref,
    stack_ref,
    rcv_window_ref,
    back_ref,
    load_sem,
    halo_send,
    halo_recv,
    fold_send,
    fold_recv,
    out_send,
    out_recv,
    back_send,
    back_recv,
    own_sem,
):
    shot_dev, receivers = traces_ref.shape[0], traces_ref.shape[1]
    groups = shot_dev // 2
    share = receivers // shot_size
    peers = shot_size - 1
    shots = shot_size * shot_dev
    rows = shots * CHUNKS
    order = list(range(1, share - 1)) + [0, share - 1]
    cuts = [0, 2, 6, share - 2, share]
    portions = list(zip(cuts, cuts[1:]))
    me = lax.axis_index("shot")
    line = lax.axis_index("rline")
    has = (line > 0, line < rline_size - 1)
    beside = (jnp.maximum(line - 1, 0), jnp.minimum(line + 1, rline_size - 1))

    far = sorted(range(1, shot_size), key=lambda d: abs(d - shot_size // 2))

    def peer(step):
        return lax.rem(me + far[step], shot_size)

    def source(step):
        return lax.rem(me + shot_size - far[step], shot_size)

    loads = [
        pltpu.make_async_copy(a, b, load_sem.at[i])
        for i, (a, b) in enumerate(
            [
                (shot_taps_hbm, shot_taps_ref),
                (rcv_taps_hbm, rcv_taps_ref),
                (dest_hbm, dest_ref),
                (fold_hbm, fold_ref),
            ]
            + [(traces_hbm.at[s], traces_ref.at[s]) for s in range(shot_dev)]
        )
    ]
    for load in loads:
        load.start()
    barrier = pltpu.get_barrier_semaphore()
    for step in range(peers):
        pl.semaphore_signal(barrier, inc=1, device_id={"shot": peer(step)}, device_id_type=MESH)
    for side in range(2):

        @pl.when(has[side])
        def _(side=side):
            pl.semaphore_signal(barrier, inc=1, device_id={"rline": beside[side]}, device_id_type=MESH)

    alive_ref[...] = jnp.zeros(alive_ref.shape, F32)
    fold_own_ref[...] = jnp.full(fold_own_ref.shape, -1, jnp.int32)
    loads[0].wait()
    build_table(shot_taps_ref, taps_rows_ref, shot_table_ref)
    loads[2].wait()
    alive_ref[0:shot_dev, 0:receivers] = (dest_ref[...] >= 0).astype(F32)
    pick_shot = lax.broadcasted_iota(jnp.int32, (8, shot_dev * LANES), 0) == (
        lax.broadcasted_iota(jnp.int32, (8, shot_dev * LANES), 1) // LANES
    )
    mask_ref[...] = lax.dot_general(
        alive_ref[...], pick_shot.astype(F32), (((0,), (0,)), ((), ())), preferred_element_type=F32
    )
    for s in range(shot_dev):
        loads[4 + s].wait()
        for i in range(receivers // 16):
            x = traces_ref[s, pl.ds(i * 16, 16)].astype(F32)
            for half in range(2):
                mask = mask_ref[i * 16 + half * 8 : i * 16 + half * 8 + 8, s * LANES : (s + 1) * LANES]
                begin = (i * 16 + half * 8 + RIM) * 16 + 8 + (s % 2) * CHUNKS
                for c in range(CHUNKS):
                    piece = x[half * 8 : half * 8 + 8, c * LANES : (c + 1) * LANES]
                    plain_ref[s // 2, pl.ds(begin + c, 8, stride=16)] = piece * mask

    for g in range(groups):
        for side, begin in enumerate((receivers - RIM, 0)):
            edge = plain_ref[g, (RIM + begin) * 16 + 8 : (2 * RIM + begin) * 16 + 8]
            halo_out_ref[side, g] = edge.astype(BF16).reshape(RIM, 16, LANES)
    loads[3].wait()
    fold_own_ref[0:shot_dev, 0:receivers] = fold_ref[...]

    span_pairs = (receivers + 2 * RIM) // 2
    edge_pairs = shot_size // 2
    made = [edge_pairs]

    def make_tiles(limit):
        while made[0] < limit:
            count = min(5, limit - made[0])
            for g in range(groups):
                fill_windows(plain_ref.at[g], window_ref.at[g], made[0], count)
            made[0] += count

    def halo(side):
        return pltpu.make_async_remote_copy(
            src_ref=halo_out_ref.at[side],
            dst_ref=halo_in_ref.at[side],
            send_sem=halo_send.at[side],
            recv_sem=halo_recv.at[side],
            device_id={"rline": beside[1 - side]},
            device_id_type=MESH,
        )

    def fold_copy(step, slot):
        return pltpu.make_async_remote_copy(
            src_ref=fold_own_ref,
            dst_ref=fold_all_ref.at[slot],
            send_sem=fold_send.at[step],
            recv_sem=fold_recv.at[step],
            device_id={"shot": peer(step)},
            device_id_type=MESH,
        )

    def out_copy(target, n, slot):
        part = pl.ds(portions[n][0], portions[n][1] - portions[n][0])
        return pltpu.make_async_remote_copy(
            src_ref=sent_ref.at[target, part],
            dst_ref=held_ref.at[slot, part],
            send_sem=out_send.at[target, n],
            recv_sem=out_recv.at[slot, n],
            device_id={"shot": target},
            device_id_type=MESH,
        )

    def shot_blocks(starts, pairs):
        blocks = [(window_ref.at[g], first) for first in starts for g in range(groups)]
        terms = fan_terms(blocks, shot_table_ref, pairs)
        for i, first in enumerate(starts):
            for g in range(groups):
                begin = (2 * first + RIM) * 16 + 8
                centre = plain_ref[g, begin : begin + pairs * 32].reshape(2 * pairs, 16, LANES)
                value = (centre - terms[i * groups + g]).astype(BF16)
                for m in range(2 * pairs):
                    row, target = divmod(2 * first + m, shot_size)
                    sent_ref[target, order.index(row), g] = value[m]

    def send_out(n):
        for step in range(peers):
            out_copy(peer(step), n, me).start()

    def inner_blocks(n):
        begin, end = portions[n]
        make_tiles((order[end - 1] + 1) * shot_size // 2 + RIM)
        shot_blocks([order[begin] * shot_size // 2], (end - begin) * shot_size // 2)

    inner_blocks(0)
    pl.semaphore_wait(barrier, peers + has[0].astype(jnp.int32) + has[1].astype(jnp.int32))
    for side in range(2):

        @pl.when(has[1 - side])
        def _(side=side):
            halo(side).start()
    for step in range(peers):
        fold_copy(step, me).start()
    fold_all_ref[me] = fold_own_ref[...]

    for n in range(len(portions) - 1):
        if n > 0:
            inner_blocks(n)
        send_out(n)

    loads[1].wait()
    build_table(rcv_taps_ref, taps_rows_ref, rcv_table_ref)
    for side in range(2):
        land = (RIM + receivers) * 16 + 8 if side else 8

        @pl.when(has[side])
        def _(side=side, land=land):
            halo(side).wait_recv()
            for g in range(groups):
                edge = halo_in_ref[side, g].astype(F32).reshape(RIM * 16, LANES)
                plain_ref[g, land : land + RIM * 16] = edge

        @pl.when(jnp.logical_not(has[side]))
        def _(land=land):
            for g in range(groups):
                plain_ref[g, land : land + RIM * 16] = jnp.zeros((RIM * 16, LANES), F32)

    for g in range(groups):
        for first in (0, span_pairs - edge_pairs):
            fill_windows(plain_ref.at[g], window_ref.at[g], first, edge_pairs)
    shot_blocks([0, (receivers - shot_size) // 2], shot_size // 2)
    send_out(len(portions) - 1)
    held_ref[me] = sent_ref[me]

    for step in range(peers):
        fold_copy(step, source(step)).wait_recv()
    folds = fold_all_ref[...].reshape(shot_size * 8, LANES).astype(F32)
    place = lax.broadcasted_iota(jnp.int32, (16, LANES), 0)
    place = jnp.where(place < share - 2, place + 1, jnp.where(place == share - 2, 0, place))
    take = lax.broadcasted_iota(jnp.int32, (16, LANES), 1) == place * shot_size + me
    mine = lax.dot_general(
        take.astype(F32), folds, (((1,), (1,)), ((), ())), preferred_element_type=F32
    )
    entry = lax.broadcasted_iota(jnp.int32, (shot_size * 8, rows), 0)
    shot = lax.broadcasted_iota(jnp.int32, (shot_size * 8, rows), 1) // CHUNKS
    spread = ((entry // 8) * shot_dev + entry % 8 == shot) & (entry % 8 < shot_dev)
    spread = spread.astype(F32)
    labels = jnp.dot(mine, spread, preferred_element_type=F32)
    live = jnp.sum((labels >= 0.0).astype(F32), axis=1, keepdims=True) / CHUNKS
    gains = jnp.broadcast_to(jnp.sqrt(shots / live), (16, LANES))
    chunk = (lax.broadcasted_iota(jnp.int32, (16, rows), 1) % CHUNKS).astype(F32)
    labels = jnp.where(labels >= 0.0, labels * CHUNKS + chunk, -1.0)
    columns = lax.dot_general(spread, mine, (((0,), (1,)), ((), ())), preferred_element_type=F32)
    chunk = (lax.broadcasted_iota(jnp.int32, (rows, 16), 0) % CHUNKS).astype(F32)
    columns = jnp.where(columns >= 0.0, columns * CHUNKS + chunk, -1.0)
    down = lax.broadcasted_iota(jnp.int32, (rows, rows), 0).astype(F32)
    across = lax.broadcasted_iota(jnp.int32, (rows, rows), 1).astype(F32)
    for k in range(share):
        gain_ref[k] = jnp.broadcast_to(gains[k : k + 1], (CHUNKS, LANES))

    for slot in range(2):
        stack_ref[slot, 0 : RIM * 16 + 8] = jnp.zeros((RIM * 16 + 8, LANES), F32)
        end = (RIM + shots) * 16 + 8
        stack_ref[slot, end:] = jnp.zeros((stack_ref.shape[1] - end, LANES), F32)

    def parts(pair):
        one, two = order[2 * pair], order[2 * pair + 1]
        return [(0, one, 2)] if two == one + 1 else [(0, one, 1), (1, two, 1)]

    def back_copies(pair, step, owner):
        return [
            pltpu.make_async_remote_copy(
                src_ref=back_ref.at[pair, peer(step), :, pl.ds(at, count)],
                dst_ref=out_ref.at[:, pl.ds(row, count), owner],
                send_sem=back_send.at[pair + at, step],
                recv_sem=back_recv.at[pair + at, step],
                device_id={"shot": peer(step)},
                device_id_type=MESH,
            )
            for at, row, count in parts(pair)
        ]

    def back_own(pair):
        return [
            pltpu.make_async_copy(
                back_ref.at[pair, me, :, pl.ds(at, count)],
                out_ref.at[:, pl.ds(row, count), me],
                own_sem.at[pair + at],
            )
            for at, row, count in parts(pair)
        ]

    def prepare(pair):
        slot = pair % 2
        for side in range(2):
            k = 2 * pair + side
            x = held_ref[:, k].reshape(rows, LANES)
            pick = jnp.where(labels[k : k + 1] == down, 1.0, 0.0).astype(BF16)
            unpick_ref[k] = jnp.where(columns[:, k : k + 1] == across, 1.0, 0.0).astype(BF16)
            stack = jnp.dot(pick, x, preferred_element_type=F32)
            for p in range(shots):
                begin = (RIM + p) * 16 + 8 + side * CHUNKS
                stack_ref[slot, begin : begin + CHUNKS] = stack[p * CHUNKS : (p + 1) * CHUNKS]
        for i in range(4):
            fill_windows(stack_ref.at[slot], rcv_window_ref.at[slot], i * 6, 6)

    def finish(pair):
        slot = pair % 2
        (terms,) = fan_terms([(rcv_window_ref.at[slot], 0)], rcv_table_ref, shots // 2)
        begin = RIM * 16 + 8
        value = stack_ref[slot, begin : begin + shots * 16].reshape(shots, 16, LANES) - terms
        for side in range(2):
            k = 2 * pair + side
            own = value[:, side * CHUNKS : (side + 1) * CHUNKS] * gain_ref[k][None]
            back = jnp.dot(
                unpick_ref[k], own.reshape(rows, LANES).astype(BF16), preferred_element_type=F32
            )
            back_ref[pair, :, :, side] = back.astype(BF16).reshape(shot_size, groups, 16, LANES)
        for step in range(peers):
            for copy in back_copies(pair, step, me):
                copy.start()
        for copy in back_own(pair):
            copy.start()

    def arrive(n):
        for step in range(peers):
            out_copy(peer(step), n, source(step)).wait_recv()

    pairs = share // 2
    arrive(0)
    prepare(0)
    for pair in range(pairs):
        if pair + 1 < pairs:
            for n, (begin, _) in enumerate(portions):
                if begin == 2 * (pair + 1):
                    arrive(n)
            prepare(pair + 1)
        finish(pair)

    for side in range(2):

        @pl.when(has[1 - side])
        def _(side=side):
            halo(side).wait_send()

    for step in range(peers):
        fold_copy(step, me).wait_send()
        for n in range(len(portions)):
            out_copy(peer(step), n, me).wait_send()
    for pair in range(pairs):
        for copy in back_own(pair):
            copy.wait()
        for step in range(peers):
            for copy in back_copies(pair, step, me):
                copy.wait_send()
            for copy in back_copies(pair, step, source(step)):
                copy.wait_recv()


def shards(traces, kernels_shot, kernels_rcv, dest, gather, fold, counts):
    shot_dev, rcv_dev, samples = traces.shape
    shot_size = lax.axis_size("shot")
    rline_size = lax.axis_size("rline")
    shots = shot_dev * shot_size
    share = rcv_dev // shot_size
    rows = shots * CHUNKS
    groups = shot_dev // 2
    peers = shot_size - 1
    pairs = share // 2
    span = rcv_dev + 2 * RIM
    fans, trace_taps, sample_taps = kernels_shot.shape
    dma = pltpu.SemaphoreType.DMA
    vmem = pltpu.VMEM
    returned = pl.pallas_call(
        functools.partial(survey_kernel, shot_size, rline_size),
        out_shape=jax.ShapeDtypeStruct((groups, share, shot_size, 16, LANES), BF16),
        in_specs=[pl.BlockSpec(memory_space=pltpu.HBM)] * 5,
        out_specs=pl.BlockSpec(memory_space=pltpu.HBM),
        scratch_shapes=[
            vmem(traces.shape, BF16),
            vmem(dest.shape, jnp.int32),
            vmem(fold.shape, jnp.int32),
            vmem((trace_taps, fans, sample_taps), BF16),
            vmem((trace_taps, fans, sample_taps), BF16),
            vmem((LANES, LANES), F32),
            vmem((8, LANES), F32),
            vmem((LANES, shot_dev * LANES), F32),
            vmem((groups, span * 16 + 16, LANES), F32),
            vmem((groups, 4, span // 2, 16, LANES), BF16),
            vmem((2, 1024, 256), BF16),
            vmem((2, 1024, 256), BF16),
            vmem((2, groups, RIM, 16, LANES), BF16),
            vmem((2, groups, RIM, 16, LANES), BF16),
            vmem((8, LANES), jnp.int32),
            vmem((shot_size, 8, LANES), jnp.int32),
            vmem((share, CHUNKS, LANES), F32),
            vmem((share, rows, rows), BF16),
            vmem((shot_size, share, groups, 16, LANES), BF16),
            vmem((shot_size, share, groups, 16, LANES), BF16),
            vmem((2, (shots + 16) * 16 + 16, LANES), F32),
            vmem((2, 4, shots // 2 + 8, 16, LANES), BF16),
            vmem((pairs, shot_size, groups, 2, 16, LANES), BF16),
            dma((4 + shot_dev,)),
            dma((2,)),
            dma((2,)),
            dma((peers,)),
            dma((peers,)),
            dma((shot_size, 4)),
            dma((shot_size, 4)),
            dma((pairs + 1, peers)),
            dma((pairs + 1, peers)),
            dma((pairs + 1,)),
        ],
        compiler_params=pltpu.CompilerParams(
            vmem_limit_bytes=61 << 20, collective_id=0, has_side_effects=True
        ),
        cost_estimate=pl.CostEstimate(flops=7 * 10**9, bytes_accessed=4 * 10**6, transcendentals=0),
    )(traces, dest, fold, kernels_shot.transpose(1, 0, 2), kernels_rcv.transpose(1, 0, 2))
    result = returned.reshape(groups, rcv_dev, 2, CHUNKS, LANES).transpose(0, 2, 1, 3, 4)
    return result.reshape(shot_dev, rcv_dev, samples).astype(F32)


def solution(mesh):
    in_specs = (
        P("shot", "rline", None),
        P(),
        P(),
        P("shot", "rline"),
        P("shot", "rline"),
        P("shot", "rline"),
        P(("shot", "rline")),
    )
    out_specs = P("shot", "rline", None)
    return jax.shard_map(shards, mesh=mesh, in_specs=in_specs, out_specs=out_specs, check_vma=False)
```

```python
import functools

import jax
import jax.numpy as jnp
from jax import lax
from jax.experimental import pallas as pl
from jax.experimental.pallas import tpu as pltpu
from jax.sharding import PartitionSpec as P

LANES = 128
CHUNKS = 8
BF16 = jnp.bfloat16
F32 = jnp.float32
RIM = 7
MESH = pl.DeviceIdType.MESH


def lane_index(shape):
    return lax.broadcasted_iota(jnp.int32, shape, len(shape) - 1)


def build_table(kernel_ref, rows_ref, table_ref):
    reach, fans, taps = kernel_ref.shape
    rows_ref[...] = jnp.zeros(rows_ref.shape, F32)
    for step in range(reach):
        rows_ref[step * 8 : step * 8 + fans, 0:taps] = kernel_ref[step].astype(F32)
    tap = lax.broadcasted_iota(jnp.int32, (LANES, LANES), 0)
    lane = lax.broadcasted_iota(jnp.int32, (LANES, LANES), 1)
    flat = rows_ref[...].astype(BF16)
    low = jnp.dot(flat, (lane == LANES - 1 - tap).astype(BF16), preferred_element_type=F32)
    high = jnp.dot(flat, (lane == LANES // 2 - 1 - tap).astype(BF16), preferred_element_type=F32)
    even = (lane_index((64, LANES)) // 32) % 2 == 0
    for half in range(2):
        before = jnp.zeros((64, LANES), F32)
        columns = slice(half * LANES, (half + 1) * LANES)
        for step in range(16):
            if step < reach:
                at = step * 8 + 2 * half
                row = jnp.broadcast_to(low[at : at + 1] + high[at + 1 : at + 2], (64, LANES))
                here = pltpu.roll(row, 0, 1, stride=1, stride_axis=0)
            else:
                here = jnp.zeros((64, LANES), F32)
            block = jnp.where(even, here, pltpu.roll(before, 32, 1)).astype(BF16)
            table_ref[0, step * 64 : (step + 1) * 64, columns] = block
            other = step + 1 if step % 2 == 0 else step - 1
            table_ref[1, other * 64 : (other + 1) * 64, columns] = block
            before = here


def fill_windows(source_ref, window_ref, first, pairs):
    rows = pairs * 32
    begin = first * 32 + 8
    shape = (pairs, 2, 16, LANES)
    lane = lane_index(shape)
    chunk = lax.broadcasted_iota(jnp.int32, shape, 2) % CHUNKS
    own = source_ref[pl.ds(begin, rows)].reshape(shape)
    left = source_ref[pl.ds(begin - 1, rows)].reshape(shape)
    right = source_ref[pl.ds(begin + 1, rows)].reshape(shape)
    early = jnp.where(lane < 112, own, jnp.where(chunk == 0, 0.0, left))
    late = jnp.where(lane >= 16, own, jnp.where(chunk == CHUNKS - 1, 0.0, right))
    low = lane_index((pairs * 16, LANES)) < 64

    def turned(x, shift):
        return pltpu.roll(x.reshape(pairs * 16, LANES), shift, 1)

    early_a, early_b = turned(early[:, 0], 16), turned(early[:, 1], 80)
    late_a, late_b = turned(late[:, 0], 112), turned(late[:, 1], 48)
    tiles = (
        jnp.where(low, early_a, early_b),
        jnp.where(low, late_a, late_b),
        jnp.where(low, early_b, early_a),
        jnp.where(low, late_b, late_a),
    )
    for quarter, tile in enumerate(tiles):
        window_ref[quarter, pl.ds(first, pairs)] = tile.reshape(pairs, 16, LANES).astype(BF16)


def fan_terms(blocks, table_ref, pairs):
    rows = pairs * 16
    total = len(blocks) * rows
    parts = []
    for half in range(2):
        left = jnp.concatenate(
            [
                jnp.concatenate(
                    [ref[quarter, pl.ds(first + step, pairs)].reshape(rows, LANES) for step in range(8)],
                    axis=1,
                )
                for quarter in (2 * half, 2 * half + 1)
                for ref, first in blocks
            ],
            axis=0,
        )
        coherent = jnp.dot(left, table_ref[half], preferred_element_type=F32)
        parts += [coherent[:total], coherent[total:]]
    squares, cubes = [], []
    for part in parts:
        one, two = part[:, :LANES], part[:, LANES:]
        one_sq, two_sq = one * one, two * two
        squares.append(one_sq + two_sq)
        cubes.append(one_sq * one + two_sq * two)
    lane = lane_index((total, LANES))
    low = lane < 64
    even = (lane // 32) % 2 == 0

    def merged(s):
        s02, s20 = jnp.where(low, s[0], s[2]), jnp.where(low, s[2], s[0])
        s13, s31 = jnp.where(low, s[1], s[3]), jnp.where(low, s[3], s[1])
        a = jnp.where(even, s02, s13) + pltpu.roll(jnp.where(even, s20, s31), 64, 1)
        b = jnp.where(even, s13, s02) + pltpu.roll(jnp.where(even, s31, s20), 64, 1)
        return a, b

    square_a, square_b = merged(squares)
    cube_a, cube_b = merged(cubes)
    term_a = cube_a / (square_a + 1.0)
    term_b = cube_b / (square_b + 1.0)
    first_trace = jnp.where(even, term_a, pltpu.roll(term_b, 32, 1))
    second_trace = jnp.where(even, pltpu.roll(term_b, 96, 1), term_a)
    shape = (len(blocks) * pairs, 16, LANES)
    both = jnp.stack([first_trace.reshape(shape), second_trace.reshape(shape)], axis=1)
    both = both.reshape(len(blocks), 2 * pairs, 16, LANES)
    return [both[i] for i in range(len(blocks))]


def survey_kernel(
    shot_size,
    rline_size,
    traces_hbm,
    dest_hbm,
    fold_hbm,
    shot_taps_hbm,
    rcv_taps_hbm,
    out_ref,
    traces_ref,
    dest_ref,
    fold_ref,
    shot_taps_ref,
    rcv_taps_ref,
    taps_rows_ref,
    alive_ref,
    mask_ref,
    plain_ref,
    window_ref,
    shot_table_ref,
    rcv_table_ref,
    halo_out_ref,
    halo_in_ref,
    fold_own_ref,
    fold_all_ref,
    gain_ref,
    unpick_ref,
    sent_ref,
    held_ref,
    stack_ref,
    rcv_window_ref,
    back_ref,
    load_sem,
    halo_send,
    halo_recv,
    fold_send,
    fold_recv,
    out_send,
    out_recv,
    back_send,
    back_recv,
    own_sem,
):
    shot_dev, receivers = traces_ref.shape[0], traces_ref.shape[1]
    groups = shot_dev // 2
    share = receivers // shot_size
    peers = shot_size - 1
    shots = shot_size * shot_dev
    rows = shots * CHUNKS
    order = list(range(1, share - 1)) + [0, share - 1]
    cuts = [0, 2, 6, share - 2, share]
    portions = list(zip(cuts, cuts[1:]))
    me = lax.axis_index("shot")
    line = lax.axis_index("rline")
    has = (line > 0, line < rline_size - 1)
    beside = (jnp.maximum(line - 1, 0), jnp.minimum(line + 1, rline_size - 1))

    far = sorted(range(1, shot_size), key=lambda d: abs(d - shot_size // 2))

    def peer(step):
        return lax.rem(me + far[step], shot_size)

    def source(step):
        return lax.rem(me + shot_size - far[step], shot_size)

    loads = [
        pltpu.make_async_copy(a, b, load_sem.at[i])
        for i, (a, b) in enumerate(
            [
                (shot_taps_hbm, shot_taps_ref),
                (rcv_taps_hbm, rcv_taps_ref),
                (dest_hbm, dest_ref),
                (fold_hbm, fold_ref),
            ]
            + [(traces_hbm.at[s], traces_ref.at[s]) for s in range(shot_dev)]
        )
    ]
    for load in loads:
        load.start()
    barrier = pltpu.get_barrier_semaphore()
    for step in range(peers):
        pl.semaphore_signal(barrier, inc=1, device_id={"shot": peer(step)}, device_id_type=MESH)
    for side in range(2):

        @pl.when(has[side])
        def _(side=side):
            pl.semaphore_signal(barrier, inc=1, device_id={"rline": beside[side]}, device_id_type=MESH)

    alive_ref[...] = jnp.zeros(alive_ref.shape, F32)
    fold_own_ref[...] = jnp.full(fold_own_ref.shape, -1, jnp.int32)
    loads[0].wait()
    build_table(shot_taps_ref, taps_rows_ref, shot_table_ref)
    loads[2].wait()
    alive_ref[0:shot_dev, 0:receivers] = (dest_ref[...] >= 0).astype(F32)
    pick_shot = lax.broadcasted_iota(jnp.int32, (8, shot_dev * LANES), 0) == (
        lax.broadcasted_iota(jnp.int32, (8, shot_dev * LANES), 1) // LANES
    )
    mask_ref[...] = lax.dot_general(
        alive_ref[...], pick_shot.astype(F32), (((0,), (0,)), ((), ())), preferred_element_type=F32
    )
    for s in range(shot_dev):
        loads[4 + s].wait()
        for i in range(receivers // 16):
            x = traces_ref[s, pl.ds(i * 16, 16)].astype(F32)
            for half in range(2):
                mask = mask_ref[i * 16 + half * 8 : i * 16 + half * 8 + 8, s * LANES : (s + 1) * LANES]
                begin = (i * 16 + half * 8 + RIM) * 16 + 8 + (s % 2) * CHUNKS
                for c in range(CHUNKS):
                    piece = x[half * 8 : half * 8 + 8, c * LANES : (c + 1) * LANES]
                    plain_ref[s // 2, pl.ds(begin + c, 8, stride=16)] = piece * mask

    for g in range(groups):
        for side, begin in enumerate((receivers - RIM, 0)):
            edge = plain_ref[g, (RIM + begin) * 16 + 8 : (2 * RIM + begin) * 16 + 8]
            halo_out_ref[side, g] = edge.astype(BF16).reshape(RIM, 16, LANES)
    loads[3].wait()
    fold_own_ref[0:shot_dev, 0:receivers] = fold_ref[...]

    span_pairs = (receivers + 2 * RIM) // 2
    edge_pairs = shot_size // 2
    made = [edge_pairs]

    def make_tiles(limit):
        while made[0] < limit:
            count = min(5, limit - made[0])
            for g in range(groups):
                fill_windows(plain_ref.at[g], window_ref.at[g], made[0], count)
            made[0] += count

    def halo(side):
        return pltpu.make_async_remote_copy(
            src_ref=halo_out_ref.at[side],
            dst_ref=halo_in_ref.at[side],
            send_sem=halo_send.at[side],
            recv_sem=halo_recv.at[side],
            device_id={"rline": beside[1 - side]},
            device_id_type=MESH,
        )

    def fold_copy(step, slot):
        return pltpu.make_async_remote_copy(
            src_ref=fold_own_ref,
            dst_ref=fold_all_ref.at[slot],
            send_sem=fold_send.at[step],
            recv_sem=fold_recv.at[step],
            device_id={"shot": peer(step)},
            device_id_type=MESH,
        )

    def out_copy(target, n, slot):
        part = pl.ds(portions[n][0], portions[n][1] - portions[n][0])
        return pltpu.make_async_remote_copy(
            src_ref=sent_ref.at[target, part],
            dst_ref=held_ref.at[slot, part],
            send_sem=out_send.at[target, n],
            recv_sem=out_recv.at[slot, n],
            device_id={"shot": target},
            device_id_type=MESH,
        )

    def shot_blocks(starts, pairs):
        blocks = [(window_ref.at[g], first) for first in starts for g in range(groups)]
        terms = fan_terms(blocks, shot_table_ref, pairs)
        for i, first in enumerate(starts):
            for g in range(groups):
                begin = (2 * first + RIM) * 16 + 8
                centre = plain_ref[g, begin : begin + pairs * 32].reshape(2 * pairs, 16, LANES)
                value = (centre - terms[i * groups + g]).astype(BF16)
                for m in range(2 * pairs):
                    row, target = divmod(2 * first + m, shot_size)
                    sent_ref[target, order.index(row), g] = value[m]

    def send_out(n):
        for step in range(peers):
            out_copy(peer(step), n, me).start()

    def inner_blocks(n):
        begin, end = portions[n]
        make_tiles((order[end - 1] + 1) * shot_size // 2 + RIM)
        shot_blocks([order[begin] * shot_size // 2], (end - begin) * shot_size // 2)

    inner_blocks(0)
    pl.semaphore_wait(barrier, peers + has[0].astype(jnp.int32) + has[1].astype(jnp.int32))
    for side in range(2):

        @pl.when(has[1 - side])
        def _(side=side):
            halo(side).start()
    for step in range(peers):
        fold_copy(step, me).start()
    fold_all_ref[me] = fold_own_ref[...]

    for n in range(len(portions) - 1):
        if n > 0:
            inner_blocks(n)
        send_out(n)

    loads[1].wait()
    build_table(rcv_taps_ref, taps_rows_ref, rcv_table_ref)
    for side in range(2):
        land = (RIM + receivers) * 16 + 8 if side else 8

        @pl.when(has[side])
        def _(side=side, land=land):
            halo(side).wait_recv()
            for g in range(groups):
                edge = halo_in_ref[side, g].astype(F32).reshape(RIM * 16, LANES)
                plain_ref[g, land : land + RIM * 16] = edge

        @pl.when(jnp.logical_not(has[side]))
        def _(land=land):
            for g in range(groups):
                plain_ref[g, land : land + RIM * 16] = jnp.zeros((RIM * 16, LANES), F32)

    for g in range(groups):
        for first in (0, span_pairs - edge_pairs):
            fill_windows(plain_ref.at[g], window_ref.at[g], first, edge_pairs)
    shot_blocks([0, (receivers - shot_size) // 2], shot_size // 2)
    send_out(len(portions) - 1)
    held_ref[me] = sent_ref[me]

    for step in range(peers):
        fold_copy(step, source(step)).wait_recv()
    folds = fold_all_ref[...].reshape(shot_size * 8, LANES).astype(F32)
    place = lax.broadcasted_iota(jnp.int32, (16, LANES), 0)
    place = jnp.where(place < share - 2, place + 1, jnp.where(place == share - 2, 0, place))
    take = lax.broadcasted_iota(jnp.int32, (16, LANES), 1) == place * shot_size + me
    mine = lax.dot_general(
        take.astype(F32), folds, (((1,), (1,)), ((), ())), preferred_element_type=F32
    )
    entry = lax.broadcasted_iota(jnp.int32, (shot_size * 8, rows), 0)
    shot = lax.broadcasted_iota(jnp.int32, (shot_size * 8, rows), 1) // CHUNKS
    spread = ((entry // 8) * shot_dev + entry % 8 == shot) & (entry % 8 < shot_dev)
    spread = spread.astype(F32)
    labels = jnp.dot(mine, spread, preferred_element_type=F32)
    live = jnp.sum((labels >= 0.0).astype(F32), axis=1, keepdims=True) / CHUNKS
    gains = jnp.broadcast_to(jnp.sqrt(shots / live), (16, LANES))
    chunk = (lax.broadcasted_iota(jnp.int32, (16, rows), 1) % CHUNKS).astype(F32)
    labels = jnp.where(labels >= 0.0, labels * CHUNKS + chunk, -1.0)
    columns = lax.dot_general(spread, mine, (((0,), (1,)), ((), ())), preferred_element_type=F32)
    chunk = (lax.broadcasted_iota(jnp.int32, (rows, 16), 0) % CHUNKS).astype(F32)
    columns = jnp.where(columns >= 0.0, columns * CHUNKS + chunk, -1.0)
    down = lax.broadcasted_iota(jnp.int32, (rows, rows), 0).astype(F32)
    across = lax.broadcasted_iota(jnp.int32, (rows, rows), 1).astype(F32)
    for k in range(share):
        gain_ref[k] = jnp.broadcast_to(gains[k : k + 1], (CHUNKS, LANES))

    for slot in range(2):
        stack_ref[slot, 0 : RIM * 16 + 8] = jnp.zeros((RIM * 16 + 8, LANES), F32)
        end = (RIM + shots) * 16 + 8
        stack_ref[slot, end:] = jnp.zeros((stack_ref.shape[1] - end, LANES), F32)

    def parts(pair):
        one, two = order[2 * pair], order[2 * pair + 1]
        return [(0, one, 2)] if two == one + 1 else [(0, one, 1), (1, two, 1)]

    def back_copies(pair, step, owner):
        return [
            pltpu.make_async_remote_copy(
                src_ref=back_ref.at[pair, peer(step), :, pl.ds(at, count)],
                dst_ref=out_ref.at[:, pl.ds(row, count), owner],
                send_sem=back_send.at[pair + at, step],
                recv_sem=back_recv.at[pair + at, step],
                device_id={"shot": peer(step)},
                device_id_type=MESH,
            )
            for at, row, count in parts(pair)
        ]

    def back_own(pair):
        return [
            pltpu.make_async_copy(
                back_ref.at[pair, me, :, pl.ds(at, count)],
                out_ref.at[:, pl.ds(row, count), me],
                own_sem.at[pair + at],
            )
            for at, row, count in parts(pair)
        ]

    def prepare(pair):
        slot = pair % 2
        for side in range(2):
            k = 2 * pair + side
            x = held_ref[:, k].reshape(rows, LANES)
            pick = jnp.where(labels[k : k + 1] == down, 1.0, 0.0).astype(BF16)
            unpick_ref[k] = jnp.where(columns[:, k : k + 1] == across, 1.0, 0.0).astype(BF16)
            stack = jnp.dot(pick, x, preferred_element_type=F32)
            for p in range(shots):
                begin = (RIM + p) * 16 + 8 + side * CHUNKS
                stack_ref[slot, begin : begin + CHUNKS] = stack[p * CHUNKS : (p + 1) * CHUNKS]
        for i in range(4):
            fill_windows(stack_ref.at[slot], rcv_window_ref.at[slot], i * 6, 6)

    def finish(pair):
        slot = pair % 2
        (terms,) = fan_terms([(rcv_window_ref.at[slot], 0)], rcv_table_ref, shots // 2)
        begin = RIM * 16 + 8
        value = stack_ref[slot, begin : begin + shots * 16].reshape(shots, 16, LANES) - terms
        for side in range(2):
            k = 2 * pair + side
            own = value[:, side * CHUNKS : (side + 1) * CHUNKS] * gain_ref[k][None]
            back = jnp.dot(
                unpick_ref[k], own.reshape(rows, LANES).astype(BF16), preferred_element_type=F32
            )
            back_ref[pair, :, :, side] = back.astype(BF16).reshape(shot_size, groups, 16, LANES)
        for step in range(peers):
            for copy in back_copies(pair, step, me):
                copy.start()
        for copy in back_own(pair):
            copy.start()

    def arrive(n):
        for step in range(peers):
            out_copy(peer(step), n, source(step)).wait_recv()

    pairs = share // 2
    arrive(0)
    prepare(0)
    for pair in range(pairs):
        if pair + 1 < pairs:
            for n, (begin, _) in enumerate(portions):
                if begin == 2 * (pair + 1):
                    arrive(n)
            prepare(pair + 1)
        finish(pair)

    for side in range(2):

        @pl.when(has[1 - side])
        def _(side=side):
            halo(side).wait_send()

    for step in range(peers):
        fold_copy(step, me).wait_send()
        for n in range(len(portions)):
            out_copy(peer(step), n, me).wait_send()
    for pair in range(pairs):
        for copy in back_own(pair):
            copy.wait()
        for step in range(peers):
            for copy in back_copies(pair, step, me):
                copy.wait_send()
            for copy in back_copies(pair, step, source(step)):
                copy.wait_recv()


def shards(traces, kernels_shot, kernels_rcv, dest, gather, fold, counts):
    shot_dev, rcv_dev, samples = traces.shape
    shot_size = lax.axis_size("shot")
    rline_size = lax.axis_size("rline")
    shots = shot_dev * shot_size
    share = rcv_dev // shot_size
    rows = shots * CHUNKS
    groups = shot_dev // 2
    peers = shot_size - 1
    pairs = share // 2
    span = rcv_dev + 2 * RIM
    fans, trace_taps, sample_taps = kernels_shot.shape
    dma = pltpu.SemaphoreType.DMA
    vmem = pltpu.VMEM
    inputs = (traces, dest, fold, kernels_shot.transpose(1, 0, 2), kernels_rcv.transpose(1, 0, 2))
    returned = pl.pallas_call(
        functools.partial(survey_kernel, shot_size, rline_size),
        out_shape=jax.ShapeDtypeStruct((groups, share, shot_size, 16, LANES), BF16),
        in_specs=[pl.BlockSpec(memory_space=pltpu.HBM)] * 5,
        out_specs=pl.BlockSpec(memory_space=vmem),
        scratch_shapes=[
            vmem(traces.shape, BF16),
            vmem(dest.shape, jnp.int32),
            vmem(fold.shape, jnp.int32),
            vmem((trace_taps, fans, sample_taps), BF16),
            vmem((trace_taps, fans, sample_taps), BF16),
            vmem((LANES, LANES), F32),
            vmem((8, LANES), F32),
            vmem((LANES, shot_dev * LANES), F32),
            vmem((groups, span * 16 + 16, LANES), F32),
            vmem((groups, 4, span // 2, 16, LANES), BF16),
            vmem((2, 1024, 256), BF16),
            vmem((2, 1024, 256), BF16),
            vmem((2, groups, RIM, 16, LANES), BF16),
            vmem((2, groups, RIM, 16, LANES), BF16),
            vmem((8, LANES), jnp.int32),
            vmem((shot_size, 8, LANES), jnp.int32),
            vmem((share, CHUNKS, LANES), F32),
            vmem((share, rows, rows), BF16),
            vmem((shot_size, share, groups, 16, LANES), BF16),
            vmem((shot_size, share, groups, 16, LANES), BF16),
            vmem((2, (shots + 16) * 16 + 16, LANES), F32),
            vmem((2, 4, shots // 2 + 8, 16, LANES), BF16),
            vmem((pairs, shot_size, groups, 2, 16, LANES), BF16),
            dma((4 + shot_dev,)),
            dma((2,)),
            dma((2,)),
            dma((peers,)),
            dma((peers,)),
            dma((shot_size, 4)),
            dma((shot_size, 4)),
            dma((pairs + 1, peers)),
            dma((pairs + 1, peers)),
            dma((pairs + 1,)),
        ],
        compiler_params=pltpu.CompilerParams(
            vmem_limit_bytes=48 << 20, collective_id=0, has_side_effects=True
        ),
        cost_estimate=pl.CostEstimate(flops=7 * 10**9, bytes_accessed=4 * 10**6, transcendentals=0),
    )(*[pltpu.with_memory_space_constraint(a, pltpu.HBM) for a in inputs])
    result = returned.reshape(groups, rcv_dev, 2, CHUNKS, LANES).transpose(0, 2, 1, 3, 4)
    return result.reshape(shot_dev, rcv_dev, samples).astype(F32)


def solution(mesh):
    in_specs = (
        P("shot", "rline", None),
        P(),
        P(),
        P("shot", "rline"),
        P("shot", "rline"),
        P("shot", "rline"),
        P(("shot", "rline")),
    )
    out_specs = P("shot", "rline", None)
    return jax.shard_map(shards, mesh=mesh, in_specs=in_specs, out_specs=out_specs, check_vma=False)
```

```python
import functools

import jax
import jax.numpy as jnp
from jax import lax
from jax.experimental import pallas as pl
from jax.experimental.pallas import tpu as pltpu
from jax.sharding import PartitionSpec as P

LANES = 128
CHUNKS = 8
BF16 = jnp.bfloat16
F32 = jnp.float32
RIM = 7
MESH = pl.DeviceIdType.MESH


def lane_index(shape):
    return lax.broadcasted_iota(jnp.int32, shape, len(shape) - 1)


def build_table(kernel_ref, rows_ref, table_ref):
    reach, fans, taps = kernel_ref.shape
    rows_ref[...] = jnp.zeros(rows_ref.shape, F32)
    for step in range(reach):
        rows_ref[step * 8 : step * 8 + fans, 0:taps] = kernel_ref[step].astype(F32)
    tap = lax.broadcasted_iota(jnp.int32, (LANES, LANES), 0)
    lane = lax.broadcasted_iota(jnp.int32, (LANES, LANES), 1)
    flat = rows_ref[...].astype(BF16)
    low = jnp.dot(flat, (lane == LANES - 1 - tap).astype(BF16), preferred_element_type=F32)
    high = jnp.dot(flat, (lane == LANES // 2 - 1 - tap).astype(BF16), preferred_element_type=F32)
    even = (lane_index((64, LANES)) // 32) % 2 == 0
    for half in range(2):
        before = jnp.zeros((64, LANES), F32)
        columns = slice(half * LANES, (half + 1) * LANES)
        for step in range(16):
            if step < reach:
                at = step * 8 + 2 * half
                row = jnp.broadcast_to(low[at : at + 1] + high[at + 1 : at + 2], (64, LANES))
                here = pltpu.roll(row, 0, 1, stride=1, stride_axis=0)
            else:
                here = jnp.zeros((64, LANES), F32)
            block = jnp.where(even, here, pltpu.roll(before, 32, 1)).astype(BF16)
            table_ref[0, step * 64 : (step + 1) * 64, columns] = block
            other = step + 1 if step % 2 == 0 else step - 1
            table_ref[1, other * 64 : (other + 1) * 64, columns] = block
            before = here


def fill_windows(source_ref, window_ref, first, pairs):
    rows = pairs * 32
    begin = first * 32 + 8
    shape = (pairs, 2, 16, LANES)
    lane = lane_index(shape)
    chunk = lax.broadcasted_iota(jnp.int32, shape, 2) % CHUNKS
    own = source_ref[pl.ds(begin, rows)].reshape(shape)
    left = source_ref[pl.ds(begin - 1, rows)].reshape(shape)
    right = source_ref[pl.ds(begin + 1, rows)].reshape(shape)
    early = jnp.where(lane < 112, own, jnp.where(chunk == 0, 0.0, left))
    late = jnp.where(lane >= 16, own, jnp.where(chunk == CHUNKS - 1, 0.0, right))
    low = lane_index((pairs * 16, LANES)) < 64

    def turned(x, shift):
        return pltpu.roll(x.reshape(pairs * 16, LANES), shift, 1)

    early_a, early_b = turned(early[:, 0], 16), turned(early[:, 1], 80)
    late_a, late_b = turned(late[:, 0], 112), turned(late[:, 1], 48)
    tiles = (
        jnp.where(low, early_a, early_b),
        jnp.where(low, late_a, late_b),
        jnp.where(low, early_b, early_a),
        jnp.where(low, late_b, late_a),
    )
    for quarter, tile in enumerate(tiles):
        window_ref[quarter, pl.ds(first, pairs)] = tile.reshape(pairs, 16, LANES).astype(BF16)


def fan_terms(blocks, table_ref, pairs):
    rows = pairs * 16
    total = len(blocks) * rows
    parts = []
    for half in range(2):
        left = jnp.concatenate(
            [
                jnp.concatenate(
                    [ref[quarter, pl.ds(first + step, pairs)].reshape(rows, LANES) for step in range(8)],
                    axis=1,
                )
                for quarter in (2 * half, 2 * half + 1)
                for ref, first in blocks
            ],
            axis=0,
        )
        coherent = jnp.dot(left, table_ref[half], preferred_element_type=F32)
        parts += [coherent[:total], coherent[total:]]
    squares, cubes = [], []
    for part in parts:
        one, two = part[:, :LANES], part[:, LANES:]
        one_sq, two_sq = one * one, two * two
        squares.append(one_sq + two_sq)
        cubes.append(one_sq * one + two_sq * two)
    lane = lane_index((total, LANES))
    low = lane < 64
    even = (lane // 32) % 2 == 0

    def merged(s):
        s02, s20 = jnp.where(low, s[0], s[2]), jnp.where(low, s[2], s[0])
        s13, s31 = jnp.where(low, s[1], s[3]), jnp.where(low, s[3], s[1])
        a = jnp.where(even, s02, s13) + pltpu.roll(jnp.where(even, s20, s31), 64, 1)
        b = jnp.where(even, s13, s02) + pltpu.roll(jnp.where(even, s31, s20), 64, 1)
        return a, b

    square_a, square_b = merged(squares)
    cube_a, cube_b = merged(cubes)
    term_a = cube_a / (square_a + 1.0)
    term_b = cube_b / (square_b + 1.0)
    first_trace = jnp.where(even, term_a, pltpu.roll(term_b, 32, 1))
    second_trace = jnp.where(even, pltpu.roll(term_b, 96, 1), term_a)
    shape = (len(blocks) * pairs, 16, LANES)
    both = jnp.stack([first_trace.reshape(shape), second_trace.reshape(shape)], axis=1)
    both = both.reshape(len(blocks), 2 * pairs, 16, LANES)
    return [both[i] for i in range(len(blocks))]


def survey_kernel(
    shot_size,
    rline_size,
    traces_hbm,
    dest_hbm,
    fold_hbm,
    shot_taps_hbm,
    rcv_taps_hbm,
    out_ref,
    traces_ref,
    dest_ref,
    fold_ref,
    shot_taps_ref,
    rcv_taps_ref,
    taps_rows_ref,
    alive_ref,
    mask_ref,
    plain_ref,
    window_ref,
    shot_table_ref,
    rcv_table_ref,
    halo_out_ref,
    halo_in_ref,
    fold_own_ref,
    fold_all_ref,
    gain_ref,
    unpick_ref,
    sent_ref,
    held_ref,
    stack_ref,
    rcv_window_ref,
    back_ref,
    returned_ref,
    flat_ref,
    load_sem,
    halo_send,
    halo_recv,
    fold_send,
    fold_recv,
    out_send,
    out_recv,
    back_send,
    back_recv,
    own_sem,
):
    shot_dev, receivers = traces_ref.shape[0], traces_ref.shape[1]
    groups = shot_dev // 2
    share = receivers // shot_size
    peers = shot_size - 1
    shots = shot_size * shot_dev
    rows = shots * CHUNKS
    order = list(range(1, share - 1)) + [0, share - 1]
    cuts = [0, 2, 6, share - 2, share]
    portions = list(zip(cuts, cuts[1:]))
    me = lax.axis_index("shot")
    line = lax.axis_index("rline")
    has = (line > 0, line < rline_size - 1)
    beside = (jnp.maximum(line - 1, 0), jnp.minimum(line + 1, rline_size - 1))

    far = sorted(range(1, shot_size), key=lambda d: abs(d - shot_size // 2))

    def peer(step):
        return lax.rem(me + far[step], shot_size)

    def source(step):
        return lax.rem(me + shot_size - far[step], shot_size)

    loads = [
        pltpu.make_async_copy(a, b, load_sem.at[i])
        for i, (a, b) in enumerate(
            [
                (shot_taps_hbm, shot_taps_ref),
                (rcv_taps_hbm, rcv_taps_ref),
                (dest_hbm, dest_ref),
                (fold_hbm, fold_ref),
            ]
            + [(traces_hbm.at[s], traces_ref.at[s]) for s in range(shot_dev)]
        )
    ]
    for load in loads:
        load.start()
    barrier = pltpu.get_barrier_semaphore()
    for step in range(peers):
        pl.semaphore_signal(barrier, inc=1, device_id={"shot": peer(step)}, device_id_type=MESH)
    for side in range(2):

        @pl.when(has[side])
        def _(side=side):
            pl.semaphore_signal(barrier, inc=1, device_id={"rline": beside[side]}, device_id_type=MESH)

    alive_ref[...] = jnp.zeros(alive_ref.shape, F32)
    fold_own_ref[...] = jnp.full(fold_own_ref.shape, -1, jnp.int32)
    loads[0].wait()
    build_table(shot_taps_ref, taps_rows_ref, shot_table_ref)
    loads[2].wait()
    alive_ref[0:shot_dev, 0:receivers] = (dest_ref[...] >= 0).astype(F32)
    pick_shot = lax.broadcasted_iota(jnp.int32, (8, shot_dev * LANES), 0) == (
        lax.broadcasted_iota(jnp.int32, (8, shot_dev * LANES), 1) // LANES
    )
    mask_ref[...] = lax.dot_general(
        alive_ref[...], pick_shot.astype(F32), (((0,), (0,)), ((), ())), preferred_element_type=F32
    )
    for s in range(shot_dev):
        loads[4 + s].wait()
        for i in range(receivers // 16):
            x = traces_ref[s, pl.ds(i * 16, 16)].astype(F32)
            for half in range(2):
                mask = mask_ref[i * 16 + half * 8 : i * 16 + half * 8 + 8, s * LANES : (s + 1) * LANES]
                begin = (i * 16 + half * 8 + RIM) * 16 + 8 + (s % 2) * CHUNKS
                for c in range(CHUNKS):
                    piece = x[half * 8 : half * 8 + 8, c * LANES : (c + 1) * LANES]
                    plain_ref[s // 2, pl.ds(begin + c, 8, stride=16)] = piece * mask

    for g in range(groups):
        for side, begin in enumerate((receivers - RIM, 0)):
            edge = plain_ref[g, (RIM + begin) * 16 + 8 : (2 * RIM + begin) * 16 + 8]
            halo_out_ref[side, g] = edge.astype(BF16).reshape(RIM, 16, LANES)
    loads[3].wait()
    fold_own_ref[0:shot_dev, 0:receivers] = fold_ref[...]

    span_pairs = (receivers + 2 * RIM) // 2
    edge_pairs = shot_size // 2
    made = [edge_pairs]

    def make_tiles(limit):
        while made[0] < limit:
            count = min(5, limit - made[0])
            for g in range(groups):
                fill_windows(plain_ref.at[g], window_ref.at[g], made[0], count)
            made[0] += count

    def halo(side):
        return pltpu.make_async_remote_copy(
            src_ref=halo_out_ref.at[side],
            dst_ref=halo_in_ref.at[side],
            send_sem=halo_send.at[side],
            recv_sem=halo_recv.at[side],
            device_id={"rline": beside[1 - side]},
            device_id_type=MESH,
        )

    def fold_copy(step, slot):
        return pltpu.make_async_remote_copy(
            src_ref=fold_own_ref,
            dst_ref=fold_all_ref.at[slot],
            send_sem=fold_send.at[step],
            recv_sem=fold_recv.at[step],
            device_id={"shot": peer(step)},
            device_id_type=MESH,
        )

    def out_copy(target, n, slot):
        part = pl.ds(portions[n][0], portions[n][1] - portions[n][0])
        return pltpu.make_async_remote_copy(
            src_ref=sent_ref.at[target, part],
            dst_ref=held_ref.at[slot, part],
            send_sem=out_send.at[target, n],
            recv_sem=out_recv.at[slot, n],
            device_id={"shot": target},
            device_id_type=MESH,
        )

    def shot_blocks(starts, pairs):
        blocks = [(window_ref.at[g], first) for first in starts for g in range(groups)]
        terms = fan_terms(blocks, shot_table_ref, pairs)
        for i, first in enumerate(starts):
            for g in range(groups):
                begin = (2 * first + RIM) * 16 + 8
                centre = plain_ref[g, begin : begin + pairs * 32].reshape(2 * pairs, 16, LANES)
                value = (centre - terms[i * groups + g]).astype(BF16)
                for m in range(2 * pairs):
                    row, target = divmod(2 * first + m, shot_size)
                    sent_ref[target, order.index(row), g] = value[m]

    def send_out(n):
        for step in range(peers):
            out_copy(peer(step), n, me).start()

    def inner_blocks(n):
        begin, end = portions[n]
        make_tiles((order[end - 1] + 1) * shot_size // 2 + RIM)
        shot_blocks([order[begin] * shot_size // 2], (end - begin) * shot_size // 2)

    inner_blocks(0)
    pl.semaphore_wait(barrier, peers + has[0].astype(jnp.int32) + has[1].astype(jnp.int32))
    for side in range(2):

        @pl.when(has[1 - side])
        def _(side=side):
            halo(side).start()

    for n in range(len(portions) - 1):
        if n > 0:
            inner_blocks(n)
        send_out(n)
        if n == 0:
            for step in range(peers):
                fold_copy(step, me).start()
            fold_all_ref[me] = fold_own_ref[...]

    loads[1].wait()
    build_table(rcv_taps_ref, taps_rows_ref, rcv_table_ref)
    for side in range(2):
        land = (RIM + receivers) * 16 + 8 if side else 8

        @pl.when(has[side])
        def _(side=side, land=land):
            halo(side).wait_recv()
            for g in range(groups):
                edge = halo_in_ref[side, g].astype(F32).reshape(RIM * 16, LANES)
                plain_ref[g, land : land + RIM * 16] = edge

        @pl.when(jnp.logical_not(has[side]))
        def _(land=land):
            for g in range(groups):
                plain_ref[g, land : land + RIM * 16] = jnp.zeros((RIM * 16, LANES), F32)

    for g in range(groups):
        for first in (0, span_pairs - edge_pairs):
            fill_windows(plain_ref.at[g], window_ref.at[g], first, edge_pairs)
    shot_blocks([0, (receivers - shot_size) // 2], shot_size // 2)
    send_out(len(portions) - 1)
    held_ref[me] = sent_ref[me]

    for step in range(peers):
        fold_copy(step, source(step)).wait_recv()
    folds = jnp.concatenate([fold_all_ref[t] for t in range(shot_size)], axis=0).astype(F32)
    place = lax.broadcasted_iota(jnp.int32, (16, LANES), 0)
    place = jnp.where(place < share - 2, place + 1, jnp.where(place == share - 2, 0, place))
    take = lax.broadcasted_iota(jnp.int32, (16, LANES), 1) == place * shot_size + me
    mine = lax.dot_general(
        take.astype(F32), folds, (((1,), (1,)), ((), ())), preferred_element_type=F32
    )
    entry = lax.broadcasted_iota(jnp.int32, (shots, rows), 0)
    shot = lax.broadcasted_iota(jnp.int32, (shots, rows), 1) // CHUNKS
    spread = (entry == shot).astype(F32)
    labels = jnp.dot(mine, spread, preferred_element_type=F32)
    live = jnp.sum((labels >= 0.0).astype(F32), axis=1, keepdims=True) / CHUNKS
    gains = jnp.broadcast_to(jnp.sqrt(shots / live), (16, LANES))
    chunk = (lax.broadcasted_iota(jnp.int32, (16, rows), 1) % CHUNKS).astype(F32)
    labels = jnp.where(labels >= 0.0, labels * CHUNKS + chunk, -1.0)
    columns = lax.dot_general(spread, mine, (((0,), (1,)), ((), ())), preferred_element_type=F32)
    chunk = (lax.broadcasted_iota(jnp.int32, (rows, 16), 0) % CHUNKS).astype(F32)
    columns = jnp.where(columns >= 0.0, columns * CHUNKS + chunk, -1.0)
    down = lax.broadcasted_iota(jnp.int32, (rows, rows), 0).astype(F32)
    across = lax.broadcasted_iota(jnp.int32, (rows, rows), 1).astype(F32)
    for k in range(share):
        gain_ref[k] = jnp.broadcast_to(gains[k : k + 1], (CHUNKS, LANES))

    for slot in range(2):
        stack_ref[slot, 0 : RIM * 16 + 8] = jnp.zeros((RIM * 16 + 8, LANES), F32)
        end = (RIM + shots) * 16 + 8
        stack_ref[slot, end:] = jnp.zeros((stack_ref.shape[1] - end, LANES), F32)

    def parts(pair):
        one, two = order[2 * pair], order[2 * pair + 1]
        return [(0, one, 2)] if two == one + 1 else [(0, one, 1), (1, two, 1)]

    def back_copies(pair, step, owner):
        return [
            pltpu.make_async_remote_copy(
                src_ref=back_ref.at[pair, peer(step), :, pl.ds(at, count)],
                dst_ref=returned_ref.at[:, pl.ds(row, count), owner],
                send_sem=back_send.at[pair + at, step],
                recv_sem=back_recv.at[pair + at, step],
                device_id={"shot": peer(step)},
                device_id_type=MESH,
            )
            for at, row, count in parts(pair)
        ]

    def back_own(pair):
        return [
            pltpu.make_async_copy(
                back_ref.at[pair, me, :, pl.ds(at, count)],
                returned_ref.at[:, pl.ds(row, count), me],
                own_sem.at[pair + at],
            )
            for at, row, count in parts(pair)
        ]

    def prepare(pair):
        slot = pair % 2
        for side in range(2):
            k = 2 * pair + side
            x = held_ref[:, k].reshape(rows, LANES)
            pick = jnp.where(labels[k : k + 1] == down, 1.0, 0.0).astype(BF16)
            unpick_ref[k] = jnp.where(columns[:, k : k + 1] == across, 1.0, 0.0).astype(BF16)
            stack = jnp.dot(pick, x, preferred_element_type=F32)
            for p in range(shots):
                begin = (RIM + p) * 16 + 8 + side * CHUNKS
                stack_ref[slot, begin : begin + CHUNKS] = stack[p * CHUNKS : (p + 1) * CHUNKS]
        for i in range(4):
            fill_windows(stack_ref.at[slot], rcv_window_ref.at[slot], i * 6, 6)

    def finish(pair):
        slot = pair % 2
        (terms,) = fan_terms([(rcv_window_ref.at[slot], 0)], rcv_table_ref, shots // 2)
        begin = RIM * 16 + 8
        value = stack_ref[slot, begin : begin + shots * 16].reshape(shots, 16, LANES) - terms
        for side in range(2):
            k = 2 * pair + side
            own = value[:, side * CHUNKS : (side + 1) * CHUNKS] * gain_ref[k][None]
            back = jnp.dot(
                unpick_ref[k], own.reshape(rows, LANES).astype(BF16), preferred_element_type=F32
            )
            back_ref[pair, :, :, side] = back.astype(BF16).reshape(shot_size, groups, 16, LANES)
        for step in range(peers):
            for copy in back_copies(pair, step, me):
                copy.start()
        for copy in back_own(pair):
            copy.start()

    def arrive(n):
        for step in range(peers):
            out_copy(peer(step), n, source(step)).wait_recv()

    pairs = share // 2
    arrive(0)
    prepare(0)
    for pair in range(pairs):
        if pair + 1 < pairs:
            for n, (begin, _) in enumerate(portions):
                if begin == 2 * (pair + 1):
                    arrive(n)
            prepare(pair + 1)
        finish(pair)

    for pair in range(pairs):
        for copy in back_own(pair):
            copy.wait()
        for step in range(peers):
            for copy in back_copies(pair, step, source(step)):
                copy.wait_recv()
        for row in order[2 * pair : 2 * pair + 2]:
            for g in range(groups):
                flat_ref[row, g] = returned_ref[g, row].astype(F32).reshape(shot_size * 16, LANES)
                for s in range(2):
                    for c in range(CHUNKS):
                        out_ref[
                            2 * g + s,
                            row * shot_size : (row + 1) * shot_size,
                            c * LANES : (c + 1) * LANES,
                        ] = flat_ref[row, g, pl.ds(s * CHUNKS + c, shot_size, stride=16)]

    for side in range(2):

        @pl.when(has[1 - side])
        def _(side=side):
            halo(side).wait_send()

    for step in range(peers):
        fold_copy(step, me).wait_send()
        for n in range(len(portions)):
            out_copy(peer(step), n, me).wait_send()
        for pair in range(pairs):
            for copy in back_copies(pair, step, me):
                copy.wait_send()


def shards(traces, kernels_shot, kernels_rcv, dest, gather, fold, counts):
    shot_dev, rcv_dev, samples = traces.shape
    shot_size = lax.axis_size("shot")
    rline_size = lax.axis_size("rline")
    shots = shot_dev * shot_size
    share = rcv_dev // shot_size
    rows = shots * CHUNKS
    groups = shot_dev // 2
    peers = shot_size - 1
    pairs = share // 2
    span = rcv_dev + 2 * RIM
    fans, trace_taps, sample_taps = kernels_shot.shape
    dma = pltpu.SemaphoreType.DMA
    vmem = pltpu.VMEM
    inputs = (traces, dest, fold, kernels_shot.transpose(1, 0, 2), kernels_rcv.transpose(1, 0, 2))
    return pl.pallas_call(
        functools.partial(survey_kernel, shot_size, rline_size),
        out_shape=jax.ShapeDtypeStruct(traces.shape, F32),
        in_specs=[pl.BlockSpec(memory_space=pltpu.HBM)] * 5,
        out_specs=pl.BlockSpec(memory_space=vmem),
        scratch_shapes=[
            vmem(traces.shape, BF16),
            vmem(dest.shape, jnp.int32),
            vmem(fold.shape, jnp.int32),
            vmem((trace_taps, fans, sample_taps), BF16),
            vmem((trace_taps, fans, sample_taps), BF16),
            vmem((LANES, LANES), F32),
            vmem((8, LANES), F32),
            vmem((LANES, shot_dev * LANES), F32),
            vmem((groups, span * 16 + 16, LANES), F32),
            vmem((groups, 4, span // 2, 16, LANES), BF16),
            vmem((2, 1024, 256), BF16),
            vmem((2, 1024, 256), BF16),
            vmem((2, groups, RIM, 16, LANES), BF16),
            vmem((2, groups, RIM, 16, LANES), BF16),
            vmem((shot_dev, LANES), jnp.int32),
            vmem((shot_size, shot_dev, LANES), jnp.int32),
            vmem((share, CHUNKS, LANES), F32),
            vmem((share, rows, rows), BF16),
            vmem((shot_size, share, groups, 16, LANES), BF16),
            vmem((shot_size, share, groups, 16, LANES), BF16),
            vmem((2, (shots + 16) * 16 + 16, LANES), F32),
            vmem((2, 4, shots // 2 + 8, 16, LANES), BF16),
            vmem((pairs, shot_size, groups, 2, 16, LANES), BF16),
            vmem((groups, share, shot_size, 16, LANES), BF16),
            vmem((share, groups, shot_size * 16, LANES), F32),
            dma((4 + shot_dev,)),
            dma((2,)),
            dma((2,)),
            dma((peers,)),
            dma((peers,)),
            dma((shot_size, 4)),
            dma((shot_size, 4)),
            dma((pairs + 1, peers)),
            dma((pairs + 1, peers)),
            dma((pairs + 1,)),
        ],
        compiler_params=pltpu.CompilerParams(
            vmem_limit_bytes=48 << 20, collective_id=0, has_side_effects=True
        ),
        cost_estimate=pl.CostEstimate(flops=7 * 10**9, bytes_accessed=4 * 10**6, transcendentals=0),
    )(*[pltpu.with_memory_space_constraint(a, pltpu.HBM) for a in inputs])


def solution(mesh):
    in_specs = (
        P("shot", "rline", None),
        P(),
        P(),
        P("shot", "rline"),
        P("shot", "rline"),
        P("shot", "rline"),
        P(("shot", "rline")),
    )
    out_specs = P("shot", "rline", None)
    return jax.shard_map(shards, mesh=mesh, in_specs=in_specs, out_specs=out_specs, check_vma=False)
```

```python
import functools

import jax
import jax.numpy as jnp
from jax import lax
from jax.experimental import pallas as pl
from jax.experimental.pallas import tpu as pltpu
from jax.sharding import PartitionSpec as P

LANES = 128
CHUNKS = 8
BF16 = jnp.bfloat16
F32 = jnp.float32
RIM = 7
MESH = pl.DeviceIdType.MESH


def lane_index(shape):
    return lax.broadcasted_iota(jnp.int32, shape, len(shape) - 1)


def build_table(kernel_ref, rows_ref, table_ref):
    reach, fans, taps = kernel_ref.shape
    rows_ref[...] = jnp.zeros(rows_ref.shape, F32)
    for step in range(reach):
        rows_ref[step * 8 : step * 8 + fans, 0:taps] = kernel_ref[step].astype(F32)
    tap = lax.broadcasted_iota(jnp.int32, (LANES, LANES), 0)
    lane = lax.broadcasted_iota(jnp.int32, (LANES, LANES), 1)
    flat = rows_ref[...].astype(BF16)
    low = jnp.dot(flat, (lane == LANES - 1 - tap).astype(BF16), preferred_element_type=F32)
    high = jnp.dot(flat, (lane == LANES // 2 - 1 - tap).astype(BF16), preferred_element_type=F32)
    even = (lane_index((64, LANES)) // 32) % 2 == 0
    for half in range(2):
        before = jnp.zeros((64, LANES), F32)
        columns = slice(half * LANES, (half + 1) * LANES)
        for step in range(16):
            if step < reach:
                at = step * 8 + 2 * half
                row = jnp.broadcast_to(low[at : at + 1] + high[at + 1 : at + 2], (64, LANES))
                here = pltpu.roll(row, 0, 1, stride=1, stride_axis=0)
            else:
                here = jnp.zeros((64, LANES), F32)
            block = jnp.where(even, here, pltpu.roll(before, 32, 1)).astype(BF16)
            table_ref[0, step * 64 : (step + 1) * 64, columns] = block
            other = step + 1 if step % 2 == 0 else step - 1
            table_ref[1, other * 64 : (other + 1) * 64, columns] = block
            before = here


def fill_windows(source_ref, window_ref, first, pairs):
    rows = pairs * 32
    begin = first * 32 + 8
    shape = (pairs, 2, 16, LANES)
    lane = lane_index(shape)
    chunk = lax.broadcasted_iota(jnp.int32, shape, 2) % CHUNKS
    own = source_ref[pl.ds(begin, rows)].reshape(shape)
    left = source_ref[pl.ds(begin - 1, rows)].reshape(shape)
    right = source_ref[pl.ds(begin + 1, rows)].reshape(shape)
    early = jnp.where(lane < 112, own, jnp.where(chunk == 0, 0.0, left))
    late = jnp.where(lane >= 16, own, jnp.where(chunk == CHUNKS - 1, 0.0, right))
    low = lane_index((pairs * 16, LANES)) < 64

    def turned(x, shift):
        return pltpu.roll(x.reshape(pairs * 16, LANES), shift, 1)

    early_a, early_b = turned(early[:, 0], 16), turned(early[:, 1], 80)
    late_a, late_b = turned(late[:, 0], 112), turned(late[:, 1], 48)
    tiles = (
        jnp.where(low, early_a, early_b),
        jnp.where(low, late_a, late_b),
        jnp.where(low, early_b, early_a),
        jnp.where(low, late_b, late_a),
    )
    for quarter, tile in enumerate(tiles):
        window_ref[quarter, pl.ds(first, pairs)] = tile.reshape(pairs, 16, LANES).astype(BF16)


def fan_terms(blocks, table_ref, pairs):
    rows = pairs * 16
    total = len(blocks) * rows
    parts = []
    for half in range(2):
        left = jnp.concatenate(
            [
                jnp.concatenate(
                    [ref[quarter, pl.ds(first + step, pairs)].reshape(rows, LANES) for step in range(8)],
                    axis=1,
                )
                for quarter in (2 * half, 2 * half + 1)
                for ref, first in blocks
            ],
            axis=0,
        )
        coherent = jnp.dot(left, table_ref[half], preferred_element_type=F32)
        parts += [coherent[:total], coherent[total:]]
    squares, cubes = [], []
    for part in parts:
        one, two = part[:, :LANES], part[:, LANES:]
        one_sq, two_sq = one * one, two * two
        squares.append(one_sq + two_sq)
        cubes.append(one_sq * one + two_sq * two)
    lane = lane_index((total, LANES))
    low = lane < 64
    even = (lane // 32) % 2 == 0

    def merged(s):
        s02, s20 = jnp.where(low, s[0], s[2]), jnp.where(low, s[2], s[0])
        s13, s31 = jnp.where(low, s[1], s[3]), jnp.where(low, s[3], s[1])
        a = jnp.where(even, s02, s13) + pltpu.roll(jnp.where(even, s20, s31), 64, 1)
        b = jnp.where(even, s13, s02) + pltpu.roll(jnp.where(even, s31, s20), 64, 1)
        return a, b

    square_a, square_b = merged(squares)
    cube_a, cube_b = merged(cubes)
    term_a = cube_a / (square_a + 1.0)
    term_b = cube_b / (square_b + 1.0)
    first_trace = jnp.where(even, term_a, pltpu.roll(term_b, 32, 1))
    second_trace = jnp.where(even, pltpu.roll(term_b, 96, 1), term_a)
    shape = (len(blocks) * pairs, 16, LANES)
    both = jnp.stack([first_trace.reshape(shape), second_trace.reshape(shape)], axis=1)
    both = both.reshape(len(blocks), 2 * pairs, 16, LANES)
    return [both[i] for i in range(len(blocks))]


def survey_kernel(
    shot_size,
    rline_size,
    traces_hbm,
    dest_hbm,
    fold_hbm,
    shot_taps_hbm,
    rcv_taps_hbm,
    out_ref,
    traces_ref,
    dest_ref,
    fold_ref,
    shot_taps_ref,
    rcv_taps_ref,
    taps_rows_ref,
    alive_ref,
    mask_ref,
    plain_ref,
    window_ref,
    shot_table_ref,
    rcv_table_ref,
    halo_out_ref,
    halo_in_ref,
    fold_own_ref,
    fold_all_ref,
    gain_ref,
    unpick_ref,
    sent_ref,
    held_ref,
    stack_ref,
    rcv_window_ref,
    back_ref,
    returned_ref,
    flat_ref,
    load_sem,
    halo_send,
    halo_recv,
    fold_send,
    fold_recv,
    out_send,
    out_recv,
    back_send,
    back_recv,
    own_sem,
):
    shot_dev, receivers = traces_ref.shape[0], traces_ref.shape[1]
    groups = shot_dev // 2
    share = receivers // shot_size
    peers = shot_size - 1
    shots = shot_size * shot_dev
    rows = shots * CHUNKS
    order = list(range(1, share - 1)) + [0, share - 1]
    cuts = [0, 2, 6, share - 2, share]
    portions = list(zip(cuts, cuts[1:]))
    me = lax.axis_index("shot")
    line = lax.axis_index("rline")
    has = (line > 0, line < rline_size - 1)
    beside = (jnp.maximum(line - 1, 0), jnp.minimum(line + 1, rline_size - 1))

    far = sorted(range(1, shot_size), key=lambda d: abs(d - shot_size // 2))

    def peer(step):
        return lax.rem(me + far[step], shot_size)

    def source(step):
        return lax.rem(me + shot_size - far[step], shot_size)

    loads = [
        pltpu.make_async_copy(a, b, load_sem.at[i])
        for i, (a, b) in enumerate(
            [
                (shot_taps_hbm, shot_taps_ref),
                (rcv_taps_hbm, rcv_taps_ref),
                (dest_hbm, dest_ref),
                (fold_hbm, fold_ref),
            ]
            + [(traces_hbm.at[s], traces_ref.at[s]) for s in range(shot_dev)]
        )
    ]
    for load in loads:
        load.start()
    barrier = pltpu.get_barrier_semaphore()
    for step in range(peers):
        pl.semaphore_signal(barrier, inc=1, device_id={"shot": peer(step)}, device_id_type=MESH)
    for side in range(2):

        @pl.when(has[side])
        def _(side=side):
            pl.semaphore_signal(barrier, inc=1, device_id={"rline": beside[side]}, device_id_type=MESH)

    alive_ref[...] = jnp.zeros(alive_ref.shape, F32)
    fold_own_ref[...] = jnp.full(fold_own_ref.shape, -1, jnp.int32)
    loads[0].wait()
    build_table(shot_taps_ref, taps_rows_ref, shot_table_ref)
    loads[2].wait()
    alive_ref[0:shot_dev, 0:receivers] = (dest_ref[...] >= 0).astype(F32)
    pick_shot = lax.broadcasted_iota(jnp.int32, (8, shot_dev * LANES), 0) == (
        lax.broadcasted_iota(jnp.int32, (8, shot_dev * LANES), 1) // LANES
    )
    mask_ref[...] = lax.dot_general(
        alive_ref[...], pick_shot.astype(F32), (((0,), (0,)), ((), ())), preferred_element_type=F32
    )
    def relayout(tiles):
        for s in range(shot_dev):
            for i in tiles:
                x = traces_ref[s, pl.ds(i * 16, 16)].astype(F32)
                for half in range(2):
                    mask = mask_ref[i * 16 + half * 8 : i * 16 + half * 8 + 8, s * LANES : (s + 1) * LANES]
                    begin = (i * 16 + half * 8 + RIM) * 16 + 8 + (s % 2) * CHUNKS
                    for c in range(CHUNKS):
                        piece = x[half * 8 : half * 8 + 8, c * LANES : (c + 1) * LANES]
                        plain_ref[s // 2, pl.ds(begin + c, 8, stride=16)] = piece * mask

    for s in range(shot_dev):
        loads[4 + s].wait()
    last_tile = receivers // 16 - 1
    relayout([0, 1, last_tile])

    for g in range(groups):
        for side, begin in enumerate((receivers - RIM, 0)):
            edge = plain_ref[g, (RIM + begin) * 16 + 8 : (2 * RIM + begin) * 16 + 8]
            halo_out_ref[side, g] = edge.astype(BF16).reshape(RIM, 16, LANES)
    loads[3].wait()
    fold_own_ref[0:shot_dev, 0:receivers] = fold_ref[...]

    span_pairs = (receivers + 2 * RIM) // 2
    edge_pairs = shot_size // 2
    made = [edge_pairs]

    def make_tiles(limit):
        while made[0] < limit:
            count = min(5, limit - made[0])
            for g in range(groups):
                fill_windows(plain_ref.at[g], window_ref.at[g], made[0], count)
            made[0] += count

    def halo(side):
        return pltpu.make_async_remote_copy(
            src_ref=halo_out_ref.at[side],
            dst_ref=halo_in_ref.at[side],
            send_sem=halo_send.at[side],
            recv_sem=halo_recv.at[side],
            device_id={"rline": beside[1 - side]},
            device_id_type=MESH,
        )

    def fold_copy(step, slot):
        return pltpu.make_async_remote_copy(
            src_ref=fold_own_ref,
            dst_ref=fold_all_ref.at[slot],
            send_sem=fold_send.at[step],
            recv_sem=fold_recv.at[step],
            device_id={"shot": peer(step)},
            device_id_type=MESH,
        )

    def out_copy(target, n, slot):
        part = pl.ds(portions[n][0], portions[n][1] - portions[n][0])
        return pltpu.make_async_remote_copy(
            src_ref=sent_ref.at[target, part],
            dst_ref=held_ref.at[slot, part],
            send_sem=out_send.at[target, n],
            recv_sem=out_recv.at[slot, n],
            device_id={"shot": target},
            device_id_type=MESH,
        )

    def shot_blocks(starts, pairs):
        blocks = [(window_ref.at[g], first) for first in starts for g in range(groups)]
        terms = fan_terms(blocks, shot_table_ref, pairs)
        for i, first in enumerate(starts):
            for g in range(groups):
                begin = (2 * first + RIM) * 16 + 8
                centre = plain_ref[g, begin : begin + pairs * 32].reshape(2 * pairs, 16, LANES)
                value = (centre - terms[i * groups + g]).astype(BF16)
                for m in range(2 * pairs):
                    row, target = divmod(2 * first + m, shot_size)
                    sent_ref[target, order.index(row), g] = value[m]

    def send_out(n):
        for step in range(peers):
            out_copy(peer(step), n, me).start()

    def inner_blocks(n):
        begin, end = portions[n]
        make_tiles((order[end - 1] + 1) * shot_size // 2 + RIM)
        shot_blocks([order[begin] * shot_size // 2], (end - begin) * shot_size // 2)

    inner_blocks(0)
    pl.semaphore_wait(barrier, peers + has[0].astype(jnp.int32) + has[1].astype(jnp.int32))
    for side in range(2):

        @pl.when(has[1 - side])
        def _(side=side):
            halo(side).start()

    for n in range(len(portions) - 1):
        if n == 1:
            relayout(range(2, last_tile))
        if n > 0:
            inner_blocks(n)
        send_out(n)
        if n == 0:
            for step in range(peers):
                fold_copy(step, me).start()
            fold_all_ref[me] = fold_own_ref[...]

    loads[1].wait()
    build_table(rcv_taps_ref, taps_rows_ref, rcv_table_ref)
    for side in range(2):
        land = (RIM + receivers) * 16 + 8 if side else 8

        @pl.when(has[side])
        def _(side=side, land=land):
            halo(side).wait_recv()
            for g in range(groups):
                edge = halo_in_ref[side, g].astype(F32).reshape(RIM * 16, LANES)
                plain_ref[g, land : land + RIM * 16] = edge

        @pl.when(jnp.logical_not(has[side]))
        def _(land=land):
            for g in range(groups):
                plain_ref[g, land : land + RIM * 16] = jnp.zeros((RIM * 16, LANES), F32)

    for g in range(groups):
        for first in (0, span_pairs - edge_pairs):
            fill_windows(plain_ref.at[g], window_ref.at[g], first, edge_pairs)
    shot_blocks([0, (receivers - shot_size) // 2], shot_size // 2)
    send_out(len(portions) - 1)
    held_ref[me] = sent_ref[me]

    for step in range(peers):
        fold_copy(step, source(step)).wait_recv()
    folds = jnp.concatenate([fold_all_ref[t] for t in range(shot_size)], axis=0).astype(F32)
    place = lax.broadcasted_iota(jnp.int32, (16, LANES), 0)
    place = jnp.where(place < share - 2, place + 1, jnp.where(place == share - 2, 0, place))
    take = lax.broadcasted_iota(jnp.int32, (16, LANES), 1) == place * shot_size + me
    mine = lax.dot_general(
        take.astype(F32), folds, (((1,), (1,)), ((), ())), preferred_element_type=F32
    )
    entry = lax.broadcasted_iota(jnp.int32, (shots, rows), 0)
    shot = lax.broadcasted_iota(jnp.int32, (shots, rows), 1) // CHUNKS
    spread = (entry == shot).astype(F32)
    labels = jnp.dot(mine, spread, preferred_element_type=F32)
    live = jnp.sum((labels >= 0.0).astype(F32), axis=1, keepdims=True) / CHUNKS
    gains = jnp.broadcast_to(jnp.sqrt(shots / live), (16, LANES))
    chunk = (lax.broadcasted_iota(jnp.int32, (16, rows), 1) % CHUNKS).astype(F32)
    labels = jnp.where(labels >= 0.0, labels * CHUNKS + chunk, -1.0)
    columns = lax.dot_general(spread, mine, (((0,), (1,)), ((), ())), preferred_element_type=F32)
    chunk = (lax.broadcasted_iota(jnp.int32, (rows, 16), 0) % CHUNKS).astype(F32)
    columns = jnp.where(columns >= 0.0, columns * CHUNKS + chunk, -1.0)
    down = lax.broadcasted_iota(jnp.int32, (rows, rows), 0).astype(F32)
    across = lax.broadcasted_iota(jnp.int32, (rows, rows), 1).astype(F32)
    for k in range(share):
        gain_ref[k] = jnp.broadcast_to(gains[k : k + 1], (CHUNKS, LANES))

    for slot in range(2):
        stack_ref[slot, 0 : RIM * 16 + 8] = jnp.zeros((RIM * 16 + 8, LANES), F32)
        end = (RIM + shots) * 16 + 8
        stack_ref[slot, end:] = jnp.zeros((stack_ref.shape[1] - end, LANES), F32)

    def parts(pair):
        one, two = order[2 * pair], order[2 * pair + 1]
        return [(0, one, 2)] if two == one + 1 else [(0, one, 1), (1, two, 1)]

    def back_copies(pair, step, owner):
        return [
            pltpu.make_async_remote_copy(
                src_ref=back_ref.at[pair, peer(step), :, pl.ds(at, count)],
                dst_ref=returned_ref.at[:, pl.ds(row, count), owner],
                send_sem=back_send.at[pair + at, step],
                recv_sem=back_recv.at[pair + at, step],
                device_id={"shot": peer(step)},
                device_id_type=MESH,
            )
            for at, row, count in parts(pair)
        ]

    def back_own(pair):
        return [
            pltpu.make_async_copy(
                back_ref.at[pair, me, :, pl.ds(at, count)],
                returned_ref.at[:, pl.ds(row, count), me],
                own_sem.at[pair + at],
            )
            for at, row, count in parts(pair)
        ]

    def prepare(pair):
        slot = pair % 2
        for side in range(2):
            k = 2 * pair + side
            x = held_ref[:, k].reshape(rows, LANES)
            pick = jnp.where(labels[k : k + 1] == down, 1.0, 0.0).astype(BF16)
            unpick_ref[k] = jnp.where(columns[:, k : k + 1] == across, 1.0, 0.0).astype(BF16)
            stack = jnp.dot(pick, x, preferred_element_type=F32)
            for p in range(shots):
                begin = (RIM + p) * 16 + 8 + side * CHUNKS
                stack_ref[slot, begin : begin + CHUNKS] = stack[p * CHUNKS : (p + 1) * CHUNKS]
        for i in range(4):
            fill_windows(stack_ref.at[slot], rcv_window_ref.at[slot], i * 6, 6)

    def finish(pair):
        slot = pair % 2
        (terms,) = fan_terms([(rcv_window_ref.at[slot], 0)], rcv_table_ref, shots // 2)
        begin = RIM * 16 + 8
        value = stack_ref[slot, begin : begin + shots * 16].reshape(shots, 16, LANES) - terms
        for side in range(2):
            k = 2 * pair + side
            own = value[:, side * CHUNKS : (side + 1) * CHUNKS] * gain_ref[k][None]
            back = jnp.dot(
                unpick_ref[k], own.reshape(rows, LANES).astype(BF16), preferred_element_type=F32
            )
            back_ref[pair, :, :, side] = back.astype(BF16).reshape(shot_size, groups, 16, LANES)
        for step in range(peers):
            for copy in back_copies(pair, step, me):
                copy.start()
        for copy in back_own(pair):
            copy.start()

    def arrive(n):
        for step in range(peers):
            out_copy(peer(step), n, source(step)).wait_recv()

    pairs = share // 2
    arrive(0)
    prepare(0)
    for pair in range(pairs):
        if pair + 1 < pairs:
            for n, (begin, _) in enumerate(portions):
                if begin == 2 * (pair + 1):
                    arrive(n)
            prepare(pair + 1)
        finish(pair)

    for pair in range(pairs):
        for copy in back_own(pair):
            copy.wait()
        for step in range(peers):
            for copy in back_copies(pair, step, source(step)):
                copy.wait_recv()
        for row in order[2 * pair : 2 * pair + 2]:
            for g in range(groups):
                flat_ref[row, g] = returned_ref[g, row].astype(F32).reshape(shot_size * 16, LANES)
                for s in range(2):
                    for c in range(CHUNKS):
                        out_ref[
                            2 * g + s,
                            row * shot_size : (row + 1) * shot_size,
                            c * LANES : (c + 1) * LANES,
                        ] = flat_ref[row, g, pl.ds(s * CHUNKS + c, shot_size, stride=16)]

    for side in range(2):

        @pl.when(has[1 - side])
        def _(side=side):
            halo(side).wait_send()

    for step in range(peers):
        fold_copy(step, me).wait_send()
        for n in range(len(portions)):
            out_copy(peer(step), n, me).wait_send()
        for pair in range(pairs):
            for copy in back_copies(pair, step, me):
                copy.wait_send()


def shards(traces, kernels_shot, kernels_rcv, dest, gather, fold, counts):
    shot_dev, rcv_dev, samples = traces.shape
    shot_size = lax.axis_size("shot")
    rline_size = lax.axis_size("rline")
    shots = shot_dev * shot_size
    share = rcv_dev // shot_size
    rows = shots * CHUNKS
    groups = shot_dev // 2
    peers = shot_size - 1
    pairs = share // 2
    span = rcv_dev + 2 * RIM
    fans, trace_taps, sample_taps = kernels_shot.shape
    dma = pltpu.SemaphoreType.DMA
    vmem = pltpu.VMEM
    inputs = (traces, dest, fold, kernels_shot.transpose(1, 0, 2), kernels_rcv.transpose(1, 0, 2))
    return pl.pallas_call(
        functools.partial(survey_kernel, shot_size, rline_size),
        out_shape=jax.ShapeDtypeStruct(traces.shape, F32),
        in_specs=[pl.BlockSpec(memory_space=pltpu.HBM)] * 5,
        out_specs=pl.BlockSpec(memory_space=vmem),
        scratch_shapes=[
            vmem(traces.shape, BF16),
            vmem(dest.shape, jnp.int32),
            vmem(fold.shape, jnp.int32),
            vmem((trace_taps, fans, sample_taps), BF16),
            vmem((trace_taps, fans, sample_taps), BF16),
            vmem((LANES, LANES), F32),
            vmem((8, LANES), F32),
            vmem((LANES, shot_dev * LANES), F32),
            vmem((groups, span * 16 + 16, LANES), F32),
            vmem((groups, 4, span // 2, 16, LANES), BF16),
            vmem((2, 1024, 256), BF16),
            vmem((2, 1024, 256), BF16),
            vmem((2, groups, RIM, 16, LANES), BF16),
            vmem((2, groups, RIM, 16, LANES), BF16),
            vmem((shot_dev, LANES), jnp.int32),
            vmem((shot_size, shot_dev, LANES), jnp.int32),
            vmem((share, CHUNKS, LANES), F32),
            vmem((share, rows, rows), BF16),
            vmem((shot_size, share, groups, 16, LANES), BF16),
            vmem((shot_size, share, groups, 16, LANES), BF16),
            vmem((2, (shots + 16) * 16 + 16, LANES), F32),
            vmem((2, 4, shots // 2 + 8, 16, LANES), BF16),
            vmem((pairs, shot_size, groups, 2, 16, LANES), BF16),
            vmem((groups, share, shot_size, 16, LANES), BF16),
            vmem((share, groups, shot_size * 16, LANES), F32),
            dma((4 + shot_dev,)),
            dma((2,)),
            dma((2,)),
            dma((peers,)),
            dma((peers,)),
            dma((shot_size, 4)),
            dma((shot_size, 4)),
            dma((pairs + 1, peers)),
            dma((pairs + 1, peers)),
            dma((pairs + 1,)),
        ],
        compiler_params=pltpu.CompilerParams(
            vmem_limit_bytes=48 << 20, collective_id=0, has_side_effects=True
        ),
        cost_estimate=pl.CostEstimate(flops=7 * 10**9, bytes_accessed=4 * 10**6, transcendentals=0),
    )(*[pltpu.with_memory_space_constraint(a, pltpu.HBM) for a in inputs])


def solution(mesh):
    in_specs = (
        P("shot", "rline", None),
        P(),
        P(),
        P("shot", "rline"),
        P("shot", "rline"),
        P("shot", "rline"),
        P(("shot", "rline")),
    )
    out_specs = P("shot", "rline", None)
    return jax.shard_map(shards, mesh=mesh, in_specs=in_specs, out_specs=out_specs, check_vma=False)
```

```python
import functools

import jax
import jax.numpy as jnp
from jax import lax
from jax.experimental import pallas as pl
from jax.experimental.pallas import tpu as pltpu
from jax.sharding import PartitionSpec as P

LANES = 128
CHUNKS = 8
BF16 = jnp.bfloat16
F32 = jnp.float32
RIM = 7
MESH = pl.DeviceIdType.MESH


def lane_index(shape):
    return lax.broadcasted_iota(jnp.int32, shape, len(shape) - 1)


def build_table(kernel_ref, rows_ref, table_ref):
    reach, fans, taps = kernel_ref.shape
    rows_ref[...] = jnp.zeros(rows_ref.shape, F32)
    for step in range(reach):
        rows_ref[step * 8 : step * 8 + fans, 0:taps] = kernel_ref[step].astype(F32)
    tap = lax.broadcasted_iota(jnp.int32, (LANES, LANES), 0)
    lane = lax.broadcasted_iota(jnp.int32, (LANES, LANES), 1)
    flat = rows_ref[...].astype(BF16)
    low = jnp.dot(flat, (lane == LANES - 1 - tap).astype(BF16), preferred_element_type=F32)
    high = jnp.dot(flat, (lane == LANES // 2 - 1 - tap).astype(BF16), preferred_element_type=F32)
    even = (lane_index((64, LANES)) // 32) % 2 == 0
    for half in range(2):
        before = jnp.zeros((64, LANES), F32)
        columns = slice(half * LANES, (half + 1) * LANES)
        for step in range(16):
            if step < reach:
                at = step * 8 + 2 * half
                row = jnp.broadcast_to(low[at : at + 1] + high[at + 1 : at + 2], (64, LANES))
                here = pltpu.roll(row, 0, 1, stride=1, stride_axis=0)
            else:
                here = jnp.zeros((64, LANES), F32)
            block = jnp.where(even, here, pltpu.roll(before, 32, 1)).astype(BF16)
            table_ref[0, step * 64 : (step + 1) * 64, columns] = block
            other = step + 1 if step % 2 == 0 else step - 1
            table_ref[1, other * 64 : (other + 1) * 64, columns] = block
            before = here


def fill_windows(source_ref, window_ref, first, pairs):
    rows = pairs * 32
    begin = first * 32 + 8
    shape = (pairs, 2, 16, LANES)
    lane = lane_index(shape)
    chunk = lax.broadcasted_iota(jnp.int32, shape, 2) % CHUNKS
    own = source_ref[pl.ds(begin, rows)].reshape(shape)
    left = source_ref[pl.ds(begin - 1, rows)].reshape(shape)
    right = source_ref[pl.ds(begin + 1, rows)].reshape(shape)
    early = jnp.where(lane < 112, own, jnp.where(chunk == 0, 0.0, left))
    late = jnp.where(lane >= 16, own, jnp.where(chunk == CHUNKS - 1, 0.0, right))
    low = lane_index((pairs * 16, LANES)) < 64

    def turned(x, shift):
        return pltpu.roll(x.reshape(pairs * 16, LANES), shift, 1)

    early_a, early_b = turned(early[:, 0], 16), turned(early[:, 1], 80)
    late_a, late_b = turned(late[:, 0], 112), turned(late[:, 1], 48)
    tiles = (
        jnp.where(low, early_a, early_b),
        jnp.where(low, late_a, late_b),
        jnp.where(low, early_b, early_a),
        jnp.where(low, late_b, late_a),
    )
    for quarter, tile in enumerate(tiles):
        window_ref[quarter, pl.ds(first, pairs)] = tile.reshape(pairs, 16, LANES).astype(BF16)


def fan_terms(blocks, table_ref, pairs):
    rows = pairs * 16
    total = len(blocks) * rows
    parts = []
    for half in range(2):
        left = jnp.concatenate(
            [
                jnp.concatenate(
                    [ref[quarter, pl.ds(first + step, pairs)].reshape(rows, LANES) for step in range(8)],
                    axis=1,
                )
                for quarter in (2 * half, 2 * half + 1)
                for ref, first in blocks
            ],
            axis=0,
        )
        coherent = jnp.dot(left, table_ref[half], preferred_element_type=F32)
        parts += [coherent[:total], coherent[total:]]
    squares, cubes = [], []
    for part in parts:
        one, two = part[:, :LANES], part[:, LANES:]
        one_sq, two_sq = one * one, two * two
        squares.append(one_sq + two_sq)
        cubes.append(one_sq * one + two_sq * two)
    lane = lane_index((total, LANES))
    low = lane < 64
    even = (lane // 32) % 2 == 0

    def merged(s):
        s02, s20 = jnp.where(low, s[0], s[2]), jnp.where(low, s[2], s[0])
        s13, s31 = jnp.where(low, s[1], s[3]), jnp.where(low, s[3], s[1])
        a = jnp.where(even, s02, s13) + pltpu.roll(jnp.where(even, s20, s31), 64, 1)
        b = jnp.where(even, s13, s02) + pltpu.roll(jnp.where(even, s31, s20), 64, 1)
        return a, b

    square_a, square_b = merged(squares)
    cube_a, cube_b = merged(cubes)
    term_a = cube_a / (square_a + 1.0)
    term_b = cube_b / (square_b + 1.0)
    first_trace = jnp.where(even, term_a, pltpu.roll(term_b, 32, 1))
    second_trace = jnp.where(even, pltpu.roll(term_b, 96, 1), term_a)
    shape = (len(blocks) * pairs, 16, LANES)
    both = jnp.stack([first_trace.reshape(shape), second_trace.reshape(shape)], axis=1)
    both = both.reshape(len(blocks), 2 * pairs, 16, LANES)
    return [both[i] for i in range(len(blocks))]


def survey_kernel(
    shot_size,
    rline_size,
    traces_hbm,
    dest_hbm,
    fold_hbm,
    shot_taps_hbm,
    rcv_taps_hbm,
    out_ref,
    traces_ref,
    dest_ref,
    fold_ref,
    shot_taps_ref,
    rcv_taps_ref,
    taps_rows_ref,
    alive_ref,
    mask_ref,
    plain_ref,
    window_ref,
    shot_table_ref,
    rcv_table_ref,
    halo_out_ref,
    halo_in_ref,
    fold_own_ref,
    fold_all_ref,
    gain_ref,
    unpick_ref,
    sent_ref,
    held_ref,
    stack_ref,
    rcv_window_ref,
    back_ref,
    returned_ref,
    flat_ref,
    load_sem,
    halo_send,
    halo_recv,
    fold_send,
    fold_recv,
    out_send,
    out_recv,
    back_send,
    back_recv,
    own_sem,
):
    shot_dev, receivers = traces_ref.shape[0], traces_ref.shape[1]
    groups = shot_dev // 2
    share = receivers // shot_size
    peers = shot_size - 1
    shots = shot_size * shot_dev
    rows = shots * CHUNKS
    order = list(range(1, share - 1)) + [0, share - 1]
    cuts = [0, 2, 6, share - 2, share]
    portions = list(zip(cuts, cuts[1:]))
    me = lax.axis_index("shot")
    line = lax.axis_index("rline")
    has = (line > 0, line < rline_size - 1)
    beside = (jnp.maximum(line - 1, 0), jnp.minimum(line + 1, rline_size - 1))

    far = sorted(range(1, shot_size), key=lambda d: abs(d - shot_size // 2))

    def peer(step):
        return lax.rem(me + far[step], shot_size)

    def source(step):
        return lax.rem(me + shot_size - far[step], shot_size)

    loads = [
        pltpu.make_async_copy(a, b, load_sem.at[i])
        for i, (a, b) in enumerate(
            [
                (shot_taps_hbm, shot_taps_ref),
                (rcv_taps_hbm, rcv_taps_ref),
                (dest_hbm, dest_ref),
                (fold_hbm, fold_ref),
            ]
            + [(traces_hbm.at[s], traces_ref.at[s]) for s in range(shot_dev)]
        )
    ]
    for load in loads:
        load.start()
    barrier = pltpu.get_barrier_semaphore()
    for step in range(peers):
        pl.semaphore_signal(barrier, inc=1, device_id={"shot": peer(step)}, device_id_type=MESH)
    for side in range(2):

        @pl.when(has[side])
        def _(side=side):
            pl.semaphore_signal(barrier, inc=1, device_id={"rline": beside[side]}, device_id_type=MESH)

    alive_ref[...] = jnp.zeros(alive_ref.shape, F32)
    fold_own_ref[...] = jnp.full(fold_own_ref.shape, -1, jnp.int32)
    loads[0].wait()
    build_table(shot_taps_ref, taps_rows_ref, shot_table_ref)
    loads[2].wait()
    alive_ref[0:shot_dev, 0:receivers] = (dest_ref[...] >= 0).astype(F32)
    pick_shot = lax.broadcasted_iota(jnp.int32, (8, shot_dev * LANES), 0) == (
        lax.broadcasted_iota(jnp.int32, (8, shot_dev * LANES), 1) // LANES
    )
    mask_ref[...] = lax.dot_general(
        alive_ref[...], pick_shot.astype(F32), (((0,), (0,)), ((), ())), preferred_element_type=F32
    )
    def relayout(tiles):
        for s in range(shot_dev):
            for i in tiles:
                x = traces_ref[s, pl.ds(i * 16, 16)].astype(F32)
                for half in range(2):
                    mask = mask_ref[i * 16 + half * 8 : i * 16 + half * 8 + 8, s * LANES : (s + 1) * LANES]
                    begin = (i * 16 + half * 8 + RIM) * 16 + 8 + (s % 2) * CHUNKS
                    for c in range(CHUNKS):
                        piece = x[half * 8 : half * 8 + 8, c * LANES : (c + 1) * LANES]
                        plain_ref[s // 2, pl.ds(begin + c, 8, stride=16)] = piece * mask

    for s in range(shot_dev):
        loads[4 + s].wait()
    last_tile = receivers // 16 - 1
    relayout([0, 1, last_tile])

    for g in range(groups):
        for side, begin in enumerate((receivers - RIM, 0)):
            edge = plain_ref[g, (RIM + begin) * 16 + 8 : (2 * RIM + begin) * 16 + 8]
            halo_out_ref[side, g] = edge.astype(BF16).reshape(RIM, 16, LANES)
    loads[3].wait()
    fold_own_ref[0:shot_dev, 0:receivers] = fold_ref[...]

    span_pairs = (receivers + 2 * RIM) // 2
    edge_pairs = shot_size // 2
    made = [edge_pairs]

    def make_tiles(limit):
        while made[0] < limit:
            count = min(5, limit - made[0])
            for g in range(groups):
                fill_windows(plain_ref.at[g], window_ref.at[g], made[0], count)
            made[0] += count

    def halo(side):
        return pltpu.make_async_remote_copy(
            src_ref=halo_out_ref.at[side],
            dst_ref=halo_in_ref.at[side],
            send_sem=halo_send.at[side],
            recv_sem=halo_recv.at[side],
            device_id={"rline": beside[1 - side]},
            device_id_type=MESH,
        )

    def fold_copy(step, slot):
        return pltpu.make_async_remote_copy(
            src_ref=fold_own_ref,
            dst_ref=fold_all_ref.at[slot],
            send_sem=fold_send.at[step],
            recv_sem=fold_recv.at[step],
            device_id={"shot": peer(step)},
            device_id_type=MESH,
        )

    def out_copy(target, n, slot):
        part = pl.ds(portions[n][0], portions[n][1] - portions[n][0])
        return pltpu.make_async_remote_copy(
            src_ref=sent_ref.at[target, part],
            dst_ref=held_ref.at[slot, part],
            send_sem=out_send.at[target, n],
            recv_sem=out_recv.at[slot, n],
            device_id={"shot": target},
            device_id_type=MESH,
        )

    def shot_blocks(starts, pairs):
        blocks = [(window_ref.at[g], first) for first in starts for g in range(groups)]
        terms = fan_terms(blocks, shot_table_ref, pairs)
        for i, first in enumerate(starts):
            for g in range(groups):
                begin = (2 * first + RIM) * 16 + 8
                centre = plain_ref[g, begin : begin + pairs * 32].reshape(2 * pairs, 16, LANES)
                value = (centre - terms[i * groups + g]).astype(BF16)
                for m in range(2 * pairs):
                    row, target = divmod(2 * first + m, shot_size)
                    sent_ref[target, order.index(row), g] = value[m]

    def send_out(n):
        for step in range(peers):
            out_copy(peer(step), n, me).start()

    def inner_blocks(n):
        begin, end = portions[n]
        make_tiles((order[end - 1] + 1) * shot_size // 2 + RIM)
        shot_blocks([order[begin] * shot_size // 2], (end - begin) * shot_size // 2)

    inner_blocks(0)
    pl.semaphore_wait(barrier, peers + has[0].astype(jnp.int32) + has[1].astype(jnp.int32))
    for side in range(2):

        @pl.when(has[1 - side])
        def _(side=side):
            halo(side).start()

    for n in range(len(portions) - 1):
        if n == 1:
            relayout(range(2, last_tile))
        if n > 0:
            inner_blocks(n)
        send_out(n)
        if n == 0:
            for step in range(peers):
                fold_copy(step, me).start()
            fold_all_ref[me] = fold_own_ref[...]

    loads[1].wait()
    build_table(rcv_taps_ref, taps_rows_ref, rcv_table_ref)
    for side in range(2):
        land = (RIM + receivers) * 16 + 8 if side else 8

        @pl.when(has[side])
        def _(side=side, land=land):
            halo(side).wait_recv()
            for g in range(groups):
                edge = halo_in_ref[side, g].astype(F32).reshape(RIM * 16, LANES)
                plain_ref[g, land : land + RIM * 16] = edge

        @pl.when(jnp.logical_not(has[side]))
        def _(land=land):
            for g in range(groups):
                plain_ref[g, land : land + RIM * 16] = jnp.zeros((RIM * 16, LANES), F32)

    for g in range(groups):
        for first in (0, span_pairs - edge_pairs):
            fill_windows(plain_ref.at[g], window_ref.at[g], first, edge_pairs)
    shot_blocks([0, (receivers - shot_size) // 2], shot_size // 2)
    send_out(len(portions) - 1)
    held_ref[me] = sent_ref[me]

    for step in range(peers):
        fold_copy(step, source(step)).wait_recv()
    folds = jnp.concatenate([fold_all_ref[t] for t in range(shot_size)], axis=0).astype(F32)
    place = lax.broadcasted_iota(jnp.int32, (16, LANES), 0)
    place = jnp.where(place < share - 2, place + 1, jnp.where(place == share - 2, 0, place))
    take = lax.broadcasted_iota(jnp.int32, (16, LANES), 1) == place * shot_size + me
    mine = lax.dot_general(
        take.astype(F32), folds, (((1,), (1,)), ((), ())), preferred_element_type=F32
    )
    entry = lax.broadcasted_iota(jnp.int32, (shots, rows), 0)
    shot = lax.broadcasted_iota(jnp.int32, (shots, rows), 1) // CHUNKS
    spread = (entry == shot).astype(F32)
    labels = jnp.dot(mine, spread, preferred_element_type=F32)
    live = jnp.sum((labels >= 0.0).astype(F32), axis=1, keepdims=True) / CHUNKS
    gains = jnp.broadcast_to(jnp.sqrt(shots / live), (16, LANES))
    chunk = (lax.broadcasted_iota(jnp.int32, (16, rows), 1) % CHUNKS).astype(F32)
    labels = jnp.where(labels >= 0.0, labels * CHUNKS + chunk, -1.0)
    columns = lax.dot_general(spread, mine, (((0,), (1,)), ((), ())), preferred_element_type=F32)
    chunk = (lax.broadcasted_iota(jnp.int32, (rows, 16), 0) % CHUNKS).astype(F32)
    columns = jnp.where(columns >= 0.0, columns * CHUNKS + chunk, -1.0)
    down = lax.broadcasted_iota(jnp.int32, (rows, rows), 0).astype(F32)
    across = lax.broadcasted_iota(jnp.int32, (rows, rows), 1).astype(F32)
    for k in range(share):
        gain_ref[k] = jnp.broadcast_to(gains[k : k + 1], (CHUNKS, LANES))

    for slot in range(2):
        stack_ref[slot, 0 : RIM * 16 + 8] = jnp.zeros((RIM * 16 + 8, LANES), F32)
        end = (RIM + shots) * 16 + 8
        stack_ref[slot, end:] = jnp.zeros((stack_ref.shape[1] - end, LANES), F32)

    def back_copy(pair, step, owner):
        return pltpu.make_async_remote_copy(
            src_ref=back_ref.at[pair, peer(step)],
            dst_ref=returned_ref.at[pair, owner],
            send_sem=back_send.at[pair, step],
            recv_sem=back_recv.at[pair, step],
            device_id={"shot": peer(step)},
            device_id_type=MESH,
        )

    def back_own(pair):
        return pltpu.make_async_copy(back_ref.at[pair, me], returned_ref.at[pair, me], own_sem.at[pair])

    def prepare(pair):
        slot = pair % 2
        for side in range(2):
            k = 2 * pair + side
            x = held_ref[:, k].reshape(rows, LANES)
            pick = jnp.where(labels[k : k + 1] == down, 1.0, 0.0).astype(BF16)
            unpick_ref[k] = jnp.where(columns[:, k : k + 1] == across, 1.0, 0.0).astype(BF16)
            stack = jnp.dot(pick, x, preferred_element_type=F32)
            for p in range(shots):
                begin = (RIM + p) * 16 + 8 + side * CHUNKS
                stack_ref[slot, begin : begin + CHUNKS] = stack[p * CHUNKS : (p + 1) * CHUNKS]
        for i in range(4):
            fill_windows(stack_ref.at[slot], rcv_window_ref.at[slot], i * 6, 6)

    def finish(pair):
        slot = pair % 2
        (terms,) = fan_terms([(rcv_window_ref.at[slot], 0)], rcv_table_ref, shots // 2)
        begin = RIM * 16 + 8
        value = stack_ref[slot, begin : begin + shots * 16].reshape(shots, 16, LANES) - terms
        for side in range(2):
            k = 2 * pair + side
            own = value[:, side * CHUNKS : (side + 1) * CHUNKS] * gain_ref[k][None]
            back = jnp.dot(
                unpick_ref[k], own.reshape(rows, LANES).astype(BF16), preferred_element_type=F32
            )
            back_ref[pair, :, :, side] = back.astype(BF16).reshape(shot_size, groups, 16, LANES)
        for step in range(peers):
            back_copy(pair, step, me).start()
        back_own(pair).start()

    def arrive(n):
        for step in range(peers):
            out_copy(peer(step), n, source(step)).wait_recv()

    pairs = share // 2
    arrive(0)
    prepare(0)
    for pair in range(pairs):
        if pair + 1 < pairs:
            for n, (begin, _) in enumerate(portions):
                if begin == 2 * (pair + 1):
                    arrive(n)
            prepare(pair + 1)
        finish(pair)

    for pair in range(pairs):
        back_own(pair).wait()
        for step in range(peers):
            back_copy(pair, step, source(step)).wait_recv()
        for side, row in enumerate(order[2 * pair : 2 * pair + 2]):
            for g in range(groups):
                flat_ref[row, g] = returned_ref[pair, :, g, side].astype(F32).reshape(shot_size * 16, LANES)
                for s in range(2):
                    for c in range(CHUNKS):
                        out_ref[
                            2 * g + s,
                            row * shot_size : (row + 1) * shot_size,
                            c * LANES : (c + 1) * LANES,
                        ] = flat_ref[row, g, pl.ds(s * CHUNKS + c, shot_size, stride=16)]

    for side in range(2):

        @pl.when(has[1 - side])
        def _(side=side):
            halo(side).wait_send()

    for step in range(peers):
        fold_copy(step, me).wait_send()
        for n in range(len(portions)):
            out_copy(peer(step), n, me).wait_send()
        for pair in range(pairs):
            back_copy(pair, step, me).wait_send()


def shards(traces, kernels_shot, kernels_rcv, dest, gather, fold, counts):
    shot_dev, rcv_dev, samples = traces.shape
    shot_size = lax.axis_size("shot")
    rline_size = lax.axis_size("rline")
    shots = shot_dev * shot_size
    share = rcv_dev // shot_size
    rows = shots * CHUNKS
    groups = shot_dev // 2
    peers = shot_size - 1
    pairs = share // 2
    span = rcv_dev + 2 * RIM
    fans, trace_taps, sample_taps = kernels_shot.shape
    dma = pltpu.SemaphoreType.DMA
    vmem = pltpu.VMEM
    inputs = (traces, dest, fold, kernels_shot.transpose(1, 0, 2), kernels_rcv.transpose(1, 0, 2))
    return pl.pallas_call(
        functools.partial(survey_kernel, shot_size, rline_size),
        out_shape=jax.ShapeDtypeStruct(traces.shape, F32),
        in_specs=[pl.BlockSpec(memory_space=pltpu.HBM)] * 5,
        out_specs=pl.BlockSpec(memory_space=vmem),
        scratch_shapes=[
            vmem(traces.shape, BF16),
            vmem(dest.shape, jnp.int32),
            vmem(fold.shape, jnp.int32),
            vmem((trace_taps, fans, sample_taps), BF16),
            vmem((trace_taps, fans, sample_taps), BF16),
            vmem((LANES, LANES), F32),
            vmem((8, LANES), F32),
            vmem((LANES, shot_dev * LANES), F32),
            vmem((groups, span * 16 + 16, LANES), F32),
            vmem((groups, 4, span // 2, 16, LANES), BF16),
            vmem((2, 1024, 256), BF16),
            vmem((2, 1024, 256), BF16),
            vmem((2, groups, RIM, 16, LANES), BF16),
            vmem((2, groups, RIM, 16, LANES), BF16),
            vmem((shot_dev, LANES), jnp.int32),
            vmem((shot_size, shot_dev, LANES), jnp.int32),
            vmem((share, CHUNKS, LANES), F32),
            vmem((share, rows, rows), BF16),
            vmem((shot_size, share, groups, 16, LANES), BF16),
            vmem((shot_size, share, groups, 16, LANES), BF16),
            vmem((2, (shots + 16) * 16 + 16, LANES), F32),
            vmem((2, 4, shots // 2 + 8, 16, LANES), BF16),
            vmem((pairs, shot_size, groups, 2, 16, LANES), BF16),
            vmem((pairs, shot_size, groups, 2, 16, LANES), BF16),
            vmem((share, groups, shot_size * 16, LANES), F32),
            dma((4 + shot_dev,)),
            dma((2,)),
            dma((2,)),
            dma((peers,)),
            dma((peers,)),
            dma((shot_size, 4)),
            dma((shot_size, 4)),
            dma((pairs, peers)),
            dma((pairs, peers)),
            dma((pairs,)),
        ],
        compiler_params=pltpu.CompilerParams(
            vmem_limit_bytes=48 << 20, collective_id=0, has_side_effects=True
        ),
        cost_estimate=pl.CostEstimate(flops=7 * 10**9, bytes_accessed=4 * 10**6, transcendentals=0),
    )(*[pltpu.with_memory_space_constraint(a, pltpu.HBM) for a in inputs])


def solution(mesh):
    in_specs = (
        P("shot", "rline", None),
        P(),
        P(),
        P("shot", "rline"),
        P("shot", "rline"),
        P("shot", "rline"),
        P(("shot", "rline")),
    )
    out_specs = P("shot", "rline", None)
    return jax.shard_map(shards, mesh=mesh, in_specs=in_specs, out_specs=out_specs, check_vma=False)
```

```python
import functools

import jax
import jax.numpy as jnp
from jax import lax
from jax.experimental import pallas as pl
from jax.experimental.pallas import tpu as pltpu
from jax.sharding import PartitionSpec as P

LANES = 128
CHUNKS = 8
BF16 = jnp.bfloat16
F32 = jnp.float32
RIM = 7
MESH = pl.DeviceIdType.MESH


def lane_index(shape):
    return lax.broadcasted_iota(jnp.int32, shape, len(shape) - 1)


def build_table(kernel_ref, rows_ref, table_ref):
    reach, fans, taps = kernel_ref.shape
    rows_ref[...] = jnp.zeros(rows_ref.shape, F32)
    for step in range(reach):
        rows_ref[step * 8 : step * 8 + fans, 0:taps] = kernel_ref[step].astype(F32)
    tap = lax.broadcasted_iota(jnp.int32, (LANES, LANES), 0)
    lane = lax.broadcasted_iota(jnp.int32, (LANES, LANES), 1)
    flat = rows_ref[...].astype(BF16)
    low = jnp.dot(flat, (lane == LANES - 1 - tap).astype(BF16), preferred_element_type=F32)
    high = jnp.dot(flat, (lane == LANES // 2 - 1 - tap).astype(BF16), preferred_element_type=F32)
    even = (lane_index((64, LANES)) // 32) % 2 == 0
    for half in range(2):
        before = jnp.zeros((64, LANES), F32)
        columns = slice(half * LANES, (half + 1) * LANES)
        for step in range(16):
            if step < reach:
                at = step * 8 + 2 * half
                row = jnp.broadcast_to(low[at : at + 1] + high[at + 1 : at + 2], (64, LANES))
                here = pltpu.roll(row, 0, 1, stride=1, stride_axis=0)
            else:
                here = jnp.zeros((64, LANES), F32)
            block = jnp.where(even, here, pltpu.roll(before, 32, 1)).astype(BF16)
            table_ref[0, step * 64 : (step + 1) * 64, columns] = block
            other = step + 1 if step % 2 == 0 else step - 1
            table_ref[1, other * 64 : (other + 1) * 64, columns] = block
            before = here


def fill_windows(source_ref, window_ref, first, pairs):
    rows = pairs * 32
    begin = first * 32 + 8
    shape = (pairs, 2, 16, LANES)
    lane = lane_index(shape)
    chunk = lax.broadcasted_iota(jnp.int32, shape, 2) % CHUNKS
    own = source_ref[pl.ds(begin, rows)].reshape(shape)
    left = source_ref[pl.ds(begin - 1, rows)].reshape(shape)
    right = source_ref[pl.ds(begin + 1, rows)].reshape(shape)
    early = jnp.where(lane < 112, own, jnp.where(chunk == 0, 0.0, left))
    late = jnp.where(lane >= 16, own, jnp.where(chunk == CHUNKS - 1, 0.0, right))
    low = lane_index((pairs * 16, LANES)) < 64

    def turned(x, shift):
        return pltpu.roll(x.reshape(pairs * 16, LANES), shift, 1)

    early_a, early_b = turned(early[:, 0], 16), turned(early[:, 1], 80)
    late_a, late_b = turned(late[:, 0], 112), turned(late[:, 1], 48)
    tiles = (
        jnp.where(low, early_a, early_b),
        jnp.where(low, late_a, late_b),
        jnp.where(low, early_b, early_a),
        jnp.where(low, late_b, late_a),
    )
    for quarter, tile in enumerate(tiles):
        window_ref[quarter, pl.ds(first, pairs)] = tile.reshape(pairs, 16, LANES).astype(BF16)


def fan_terms(blocks, table_ref, pairs):
    rows = pairs * 16
    total = len(blocks) * rows
    parts = []
    for half in range(2):
        left = jnp.concatenate(
            [
                jnp.concatenate(
                    [ref[quarter, pl.ds(first + step, pairs)].reshape(rows, LANES) for step in range(8)],
                    axis=1,
                )
                for quarter in (2 * half, 2 * half + 1)
                for ref, first in blocks
            ],
            axis=0,
        )
        coherent = jnp.dot(left, table_ref[half], preferred_element_type=F32)
        parts += [coherent[:total], coherent[total:]]
    squares, cubes = [], []
    for part in parts:
        one, two = part[:, :LANES], part[:, LANES:]
        one_sq, two_sq = one * one, two * two
        squares.append(one_sq + two_sq)
        cubes.append(one_sq * one + two_sq * two)
    lane = lane_index((total, LANES))
    low = lane < 64
    even = (lane // 32) % 2 == 0

    def merged(s):
        s02, s20 = jnp.where(low, s[0], s[2]), jnp.where(low, s[2], s[0])
        s13, s31 = jnp.where(low, s[1], s[3]), jnp.where(low, s[3], s[1])
        a = jnp.where(even, s02, s13) + pltpu.roll(jnp.where(even, s20, s31), 64, 1)
        b = jnp.where(even, s13, s02) + pltpu.roll(jnp.where(even, s31, s20), 64, 1)
        return a, b

    square_a, square_b = merged(squares)
    cube_a, cube_b = merged(cubes)
    term_a = cube_a / (square_a + 1.0)
    term_b = cube_b / (square_b + 1.0)
    first_trace = jnp.where(even, term_a, pltpu.roll(term_b, 32, 1))
    second_trace = jnp.where(even, pltpu.roll(term_b, 96, 1), term_a)
    shape = (len(blocks) * pairs, 16, LANES)
    both = jnp.stack([first_trace.reshape(shape), second_trace.reshape(shape)], axis=1)
    both = both.reshape(len(blocks), 2 * pairs, 16, LANES)
    return [both[i] for i in range(len(blocks))]


def survey_kernel(
    shot_size,
    rline_size,
    traces_hbm,
    dest_hbm,
    fold_hbm,
    shot_taps_hbm,
    rcv_taps_hbm,
    out_ref,
    traces_ref,
    dest_ref,
    fold_ref,
    shot_taps_ref,
    rcv_taps_ref,
    taps_rows_ref,
    alive_ref,
    mask_ref,
    plain_ref,
    window_ref,
    shot_table_ref,
    rcv_table_ref,
    halo_out_ref,
    halo_in_ref,
    fold_own_ref,
    fold_all_ref,
    gain_ref,
    unpick_ref,
    sent_ref,
    held_ref,
    stack_ref,
    rcv_window_ref,
    back_ref,
    returned_ref,
    flat_ref,
    load_sem,
    halo_send,
    halo_recv,
    fold_send,
    fold_recv,
    out_send,
    out_recv,
    back_send,
    back_recv,
    own_sem,
):
    shot_dev, receivers = traces_ref.shape[0], traces_ref.shape[1]
    groups = shot_dev // 2
    share = receivers // shot_size
    peers = shot_size - 1
    shots = shot_size * shot_dev
    rows = shots * CHUNKS
    order = list(range(1, share - 1)) + [0, share - 1]
    cuts = [0, 2, 6, share - 2, share]
    portions = list(zip(cuts, cuts[1:]))
    me = lax.axis_index("shot")
    line = lax.axis_index("rline")
    has = (line > 0, line < rline_size - 1)
    beside = (jnp.maximum(line - 1, 0), jnp.minimum(line + 1, rline_size - 1))

    far = sorted(range(1, shot_size), key=lambda d: abs(d - shot_size // 2))

    def peer(step):
        return lax.rem(me + far[step], shot_size)

    def source(step):
        return lax.rem(me + shot_size - far[step], shot_size)

    loads = [
        pltpu.make_async_copy(a, b, load_sem.at[i])
        for i, (a, b) in enumerate(
            [
                (shot_taps_hbm, shot_taps_ref),
                (rcv_taps_hbm, rcv_taps_ref),
                (dest_hbm, dest_ref),
                (fold_hbm, fold_ref),
            ]
            + [(traces_hbm.at[s], traces_ref.at[s]) for s in range(shot_dev)]
        )
    ]
    for load in loads:
        load.start()
    barrier = pltpu.get_barrier_semaphore()
    for step in range(peers):
        pl.semaphore_signal(barrier, inc=1, device_id={"shot": peer(step)}, device_id_type=MESH)
    for side in range(2):

        @pl.when(has[side])
        def _(side=side):
            pl.semaphore_signal(barrier, inc=1, device_id={"rline": beside[side]}, device_id_type=MESH)

    alive_ref[...] = jnp.zeros(alive_ref.shape, F32)
    fold_own_ref[...] = jnp.full(fold_own_ref.shape, -1, jnp.int32)
    loads[0].wait()
    build_table(shot_taps_ref, taps_rows_ref, shot_table_ref)
    loads[2].wait()
    alive_ref[0:shot_dev, 0:receivers] = (dest_ref[...] >= 0).astype(F32)
    pick_shot = lax.broadcasted_iota(jnp.int32, (8, shot_dev * LANES), 0) == (
        lax.broadcasted_iota(jnp.int32, (8, shot_dev * LANES), 1) // LANES
    )
    mask_ref[...] = lax.dot_general(
        alive_ref[...], pick_shot.astype(F32), (((0,), (0,)), ((), ())), preferred_element_type=F32
    )
    def relayout(tiles):
        for s in range(shot_dev):
            for i in tiles:
                x = traces_ref[s, pl.ds(i * 16, 16)].astype(F32)
                for half in range(2):
                    mask = mask_ref[i * 16 + half * 8 : i * 16 + half * 8 + 8, s * LANES : (s + 1) * LANES]
                    begin = (i * 16 + half * 8 + RIM) * 16 + 8 + (s % 2) * CHUNKS
                    for c in range(CHUNKS):
                        piece = x[half * 8 : half * 8 + 8, c * LANES : (c + 1) * LANES]
                        plain_ref[s // 2, pl.ds(begin + c, 8, stride=16)] = piece * mask

    for s in range(shot_dev):
        loads[4 + s].wait()
    last_tile = receivers // 16 - 1
    relayout([0, 1, last_tile])

    for g in range(groups):
        for side, begin in enumerate((receivers - RIM, 0)):
            edge = plain_ref[g, (RIM + begin) * 16 + 8 : (2 * RIM + begin) * 16 + 8]
            halo_out_ref[side, g] = edge.astype(BF16).reshape(RIM, 16, LANES)
    loads[3].wait()
    fold_own_ref[0:shot_dev, 0:receivers] = fold_ref[...]

    span_pairs = (receivers + 2 * RIM) // 2
    edge_pairs = shot_size // 2
    made = [edge_pairs]

    def make_tiles(limit):
        while made[0] < limit:
            count = min(5, limit - made[0])
            for g in range(groups):
                fill_windows(plain_ref.at[g], window_ref.at[g], made[0], count)
            made[0] += count

    def halo(side):
        return pltpu.make_async_remote_copy(
            src_ref=halo_out_ref.at[side],
            dst_ref=halo_in_ref.at[side],
            send_sem=halo_send.at[side],
            recv_sem=halo_recv.at[side],
            device_id={"rline": beside[1 - side]},
            device_id_type=MESH,
        )

    def fold_copy(step, slot):
        return pltpu.make_async_remote_copy(
            src_ref=fold_own_ref,
            dst_ref=fold_all_ref.at[slot],
            send_sem=fold_send.at[step],
            recv_sem=fold_recv.at[step],
            device_id={"shot": peer(step)},
            device_id_type=MESH,
        )

    def out_copy(target, n, slot):
        part = pl.ds(portions[n][0], portions[n][1] - portions[n][0])
        return pltpu.make_async_remote_copy(
            src_ref=sent_ref.at[target, part],
            dst_ref=held_ref.at[slot, part],
            send_sem=out_send.at[target, n],
            recv_sem=out_recv.at[slot, n],
            device_id={"shot": target},
            device_id_type=MESH,
        )

    def shot_blocks(starts, pairs):
        blocks = [(window_ref.at[g], first) for first in starts for g in range(groups)]
        terms = fan_terms(blocks, shot_table_ref, pairs)
        for i, first in enumerate(starts):
            for g in range(groups):
                begin = (2 * first + RIM) * 16 + 8
                centre = plain_ref[g, begin : begin + pairs * 32].reshape(2 * pairs, 16, LANES)
                value = (centre - terms[i * groups + g]).astype(BF16)
                for m in range(2 * pairs):
                    row, target = divmod(2 * first + m, shot_size)
                    sent_ref[target, order.index(row), g] = value[m]

    def send_out(n):
        for step in range(peers):
            out_copy(peer(step), n, me).start()

    def inner_blocks(n):
        begin, end = portions[n]
        make_tiles((order[end - 1] + 1) * shot_size // 2 + RIM)
        shot_blocks([order[begin] * shot_size // 2], (end - begin) * shot_size // 2)

    inner_blocks(0)
    pl.semaphore_wait(barrier, peers + has[0].astype(jnp.int32) + has[1].astype(jnp.int32))

    for n in range(len(portions) - 1):
        if n == 1:
            relayout(range(2, last_tile))
        if n > 0:
            inner_blocks(n)
        send_out(n)
        if n == 0:
            for side in range(2):

                @pl.when(has[1 - side])
                def _(side=side):
                    halo(side).start()

            for step in range(peers):
                fold_copy(step, me).start()
            fold_all_ref[me] = fold_own_ref[...]

    loads[1].wait()
    build_table(rcv_taps_ref, taps_rows_ref, rcv_table_ref)
    for side in range(2):
        land = (RIM + receivers) * 16 + 8 if side else 8

        @pl.when(has[side])
        def _(side=side, land=land):
            halo(side).wait_recv()
            for g in range(groups):
                edge = halo_in_ref[side, g].astype(F32).reshape(RIM * 16, LANES)
                plain_ref[g, land : land + RIM * 16] = edge

        @pl.when(jnp.logical_not(has[side]))
        def _(land=land):
            for g in range(groups):
                plain_ref[g, land : land + RIM * 16] = jnp.zeros((RIM * 16, LANES), F32)

    for g in range(groups):
        for first in (0, span_pairs - edge_pairs):
            fill_windows(plain_ref.at[g], window_ref.at[g], first, edge_pairs)
    shot_blocks([0, (receivers - shot_size) // 2], shot_size // 2)
    send_out(len(portions) - 1)
    held_ref[me] = sent_ref[me]

    for step in range(peers):
        fold_copy(step, source(step)).wait_recv()
    folds = jnp.concatenate([fold_all_ref[t] for t in range(shot_size)], axis=0).astype(F32)
    place = lax.broadcasted_iota(jnp.int32, (16, LANES), 0)
    place = jnp.where(place < share - 2, place + 1, jnp.where(place == share - 2, 0, place))
    take = lax.broadcasted_iota(jnp.int32, (16, LANES), 1) == place * shot_size + me
    mine = lax.dot_general(
        take.astype(F32), folds, (((1,), (1,)), ((), ())), preferred_element_type=F32
    )
    entry = lax.broadcasted_iota(jnp.int32, (shots, rows), 0)
    shot = lax.broadcasted_iota(jnp.int32, (shots, rows), 1) // CHUNKS
    spread = (entry == shot).astype(F32)
    labels = jnp.dot(mine, spread, preferred_element_type=F32)
    live = jnp.sum((labels >= 0.0).astype(F32), axis=1, keepdims=True) / CHUNKS
    gains = jnp.broadcast_to(jnp.sqrt(shots / live), (16, LANES))
    chunk = (lax.broadcasted_iota(jnp.int32, (16, rows), 1) % CHUNKS).astype(F32)
    labels = jnp.where(labels >= 0.0, labels * CHUNKS + chunk, -1.0)
    columns = lax.dot_general(spread, mine, (((0,), (1,)), ((), ())), preferred_element_type=F32)
    chunk = (lax.broadcasted_iota(jnp.int32, (rows, 16), 0) % CHUNKS).astype(F32)
    columns = jnp.where(columns >= 0.0, columns * CHUNKS + chunk, -1.0)
    down = lax.broadcasted_iota(jnp.int32, (rows, rows), 0).astype(F32)
    across = lax.broadcasted_iota(jnp.int32, (rows, rows), 1).astype(F32)
    for k in range(share):
        gain_ref[k] = jnp.broadcast_to(gains[k : k + 1], (CHUNKS, LANES))

    for slot in range(2):
        stack_ref[slot, 0 : RIM * 16 + 8] = jnp.zeros((RIM * 16 + 8, LANES), F32)
        end = (RIM + shots) * 16 + 8
        stack_ref[slot, end:] = jnp.zeros((stack_ref.shape[1] - end, LANES), F32)

    def back_copy(pair, step, owner):
        return pltpu.make_async_remote_copy(
            src_ref=back_ref.at[pair, peer(step)],
            dst_ref=returned_ref.at[pair, owner],
            send_sem=back_send.at[pair, step],
            recv_sem=back_recv.at[pair, step],
            device_id={"shot": peer(step)},
            device_id_type=MESH,
        )

    def back_own(pair):
        return pltpu.make_async_copy(back_ref.at[pair, me], returned_ref.at[pair, me], own_sem.at[pair])

    def prepare(pair):
        slot = pair % 2
        for side in range(2):
            k = 2 * pair + side
            x = held_ref[:, k].reshape(rows, LANES)
            pick = jnp.where(labels[k : k + 1] == down, 1.0, 0.0).astype(BF16)
            unpick_ref[k] = jnp.where(columns[:, k : k + 1] == across, 1.0, 0.0).astype(BF16)
            stack = jnp.dot(pick, x, preferred_element_type=F32)
            for p in range(shots):
                begin = (RIM + p) * 16 + 8 + side * CHUNKS
                stack_ref[slot, begin : begin + CHUNKS] = stack[p * CHUNKS : (p + 1) * CHUNKS]
        for i in range(4):
            fill_windows(stack_ref.at[slot], rcv_window_ref.at[slot], i * 6, 6)

    def finish(pair):
        slot = pair % 2
        (terms,) = fan_terms([(rcv_window_ref.at[slot], 0)], rcv_table_ref, shots // 2)
        begin = RIM * 16 + 8
        value = stack_ref[slot, begin : begin + shots * 16].reshape(shots, 16, LANES) - terms
        for side in range(2):
            k = 2 * pair + side
            own = value[:, side * CHUNKS : (side + 1) * CHUNKS] * gain_ref[k][None]
            back = jnp.dot(
                unpick_ref[k], own.reshape(rows, LANES).astype(BF16), preferred_element_type=F32
            )
            back_ref[pair, :, :, side] = back.astype(BF16).reshape(shot_size, groups, 16, LANES)
        for step in range(peers):
            back_copy(pair, step, me).start()
        back_own(pair).start()

    def arrive(n):
        for step in range(peers):
            out_copy(peer(step), n, source(step)).wait_recv()

    pairs = share // 2
    arrive(0)
    prepare(0)
    for pair in range(pairs):
        if pair + 1 < pairs:
            for n, (begin, _) in enumerate(portions):
                if begin == 2 * (pair + 1):
                    arrive(n)
            prepare(pair + 1)
        finish(pair)

    for pair in range(pairs):
        back_own(pair).wait()
        for step in range(peers):
            back_copy(pair, step, source(step)).wait_recv()
        for side, row in enumerate(order[2 * pair : 2 * pair + 2]):
            for g in range(groups):
                flat_ref[row, g] = returned_ref[pair, :, g, side].astype(F32).reshape(shot_size * 16, LANES)
                for s in range(2):
                    for c in range(CHUNKS):
                        out_ref[
                            2 * g + s,
                            row * shot_size : (row + 1) * shot_size,
                            c * LANES : (c + 1) * LANES,
                        ] = flat_ref[row, g, pl.ds(s * CHUNKS + c, shot_size, stride=16)]

    for side in range(2):

        @pl.when(has[1 - side])
        def _(side=side):
            halo(side).wait_send()

    for step in range(peers):
        fold_copy(step, me).wait_send()
        for n in range(len(portions)):
            out_copy(peer(step), n, me).wait_send()
        for pair in range(pairs):
            back_copy(pair, step, me).wait_send()


def shards(traces, kernels_shot, kernels_rcv, dest, gather, fold, counts):
    shot_dev, rcv_dev, samples = traces.shape
    shot_size = lax.axis_size("shot")
    rline_size = lax.axis_size("rline")
    shots = shot_dev * shot_size
    share = rcv_dev // shot_size
    rows = shots * CHUNKS
    groups = shot_dev // 2
    peers = shot_size - 1
    pairs = share // 2
    span = rcv_dev + 2 * RIM
    fans, trace_taps, sample_taps = kernels_shot.shape
    dma = pltpu.SemaphoreType.DMA
    vmem = pltpu.VMEM
    inputs = (traces, dest, fold, kernels_shot.transpose(1, 0, 2), kernels_rcv.transpose(1, 0, 2))
    return pl.pallas_call(
        functools.partial(survey_kernel, shot_size, rline_size),
        out_shape=jax.ShapeDtypeStruct(traces.shape, F32),
        in_specs=[pl.BlockSpec(memory_space=pltpu.HBM)] * 5,
        out_specs=pl.BlockSpec(memory_space=vmem),
        scratch_shapes=[
            vmem(traces.shape, BF16),
            vmem(dest.shape, jnp.int32),
            vmem(fold.shape, jnp.int32),
            vmem((trace_taps, fans, sample_taps), BF16),
            vmem((trace_taps, fans, sample_taps), BF16),
            vmem((LANES, LANES), F32),
            vmem((8, LANES), F32),
            vmem((LANES, shot_dev * LANES), F32),
            vmem((groups, span * 16 + 16, LANES), F32),
            vmem((groups, 4, span // 2, 16, LANES), BF16),
            vmem((2, 1024, 256), BF16),
            vmem((2, 1024, 256), BF16),
            vmem((2, groups, RIM, 16, LANES), BF16),
            vmem((2, groups, RIM, 16, LANES), BF16),
            vmem((shot_dev, LANES), jnp.int32),
            vmem((shot_size, shot_dev, LANES), jnp.int32),
            vmem((share, CHUNKS, LANES), F32),
            vmem((share, rows, rows), BF16),
            vmem((shot_size, share, groups, 16, LANES), BF16),
            vmem((shot_size, share, groups, 16, LANES), BF16),
            vmem((2, (shots + 16) * 16 + 16, LANES), F32),
            vmem((2, 4, shots // 2 + 8, 16, LANES), BF16),
            vmem((pairs, shot_size, groups, 2, 16, LANES), BF16),
            vmem((pairs, shot_size, groups, 2, 16, LANES), BF16),
            vmem((share, groups, shot_size * 16, LANES), F32),
            dma((4 + shot_dev,)),
            dma((2,)),
            dma((2,)),
            dma((peers,)),
            dma((peers,)),
            dma((shot_size, 4)),
            dma((shot_size, 4)),
            dma((pairs, peers)),
            dma((pairs, peers)),
            dma((pairs,)),
        ],
        compiler_params=pltpu.CompilerParams(
            vmem_limit_bytes=48 << 20, collective_id=0, has_side_effects=True
        ),
        cost_estimate=pl.CostEstimate(flops=7 * 10**9, bytes_accessed=4 * 10**6, transcendentals=0),
    )(*[pltpu.with_memory_space_constraint(a, pltpu.HBM) for a in inputs])


def solution(mesh):
    in_specs = (
        P("shot", "rline", None),
        P(),
        P(),
        P("shot", "rline"),
        P("shot", "rline"),
        P("shot", "rline"),
        P(("shot", "rline")),
    )
    out_specs = P("shot", "rline", None)
    return jax.shard_map(shards, mesh=mesh, in_specs=in_specs, out_specs=out_specs, check_vma=False)
```
